32 devices in a mesh: batch: 8 (over z, y), stream: 4 (over x, core).
Axes of the slice: x: 2, y: 2, z: 4, core: 2. Of those that a mesh axis runs over, the one named last changes fastest.
Arguments:
- tokens: bfloat16 [8, 2048, 768], P('batch', 'stream'), may hold values from -6 to 6
- cotangent: bfloat16 [8, 2048, 768], P('batch', 'stream'), may hold values from -6 to 6
- block_size: int32 [8], P('batch'), may hold values from 4 to 16, as said below
- gain_attn: float32 [768], P(('batch', 'stream')), may hold values from 0.1 to 1.9
- w_qkv: float32 [768, 2304], P(('batch', 'stream')), may hold values from -0.21875 to 0.21875
- w_out: float32 [768, 768], P(('batch', 'stream')), may hold values from -1.25 to 1.25
- gain_mlp: float32 [768], P(('batch', 'stream')), may hold values from 0.1 to 1.9
- w_up: float32 [768, 3072], P(('batch', 'stream')), may hold values from -0.21875 to 0.21875
- w_down: float32 [3072, 768], P(('batch', 'stream')), may hold values from -0.109375 to 0.109375
Outputs:
- output: bfloat16 [8, 2048, 768], P('batch', 'stream')
- grad_tokens: bfloat16 [8, 2048, 768], P('batch', 'stream')
- grad_gain_attn: float32 [768], P(('batch', 'stream'))
- grad_w_qkv: float32 [768, 2304], P(('batch', 'stream'))
- grad_w_out: float32 [768, 768], P(('batch', 'stream'))
- grad_gain_mlp: float32 [768], P(('batch', 'stream'))
- grad_w_up: float32 [768, 3072], P(('batch', 'stream'))
- grad_w_down: float32 [3072, 768], P(('batch', 'stream'))
The draws below stay inside these ranges and needn't reach their ends.
Inputs may be any that keep to these rules, and one draw needn't show every extreme that they name: `block_size`: each sequence's block size is a power of two; each of 4, 8 and 16 occurs in every draw.
All inputs are finite; a program needn't handle non-finite values.
Results may differ from the reference program's by a relative error of at most 0.015.
Values may be sent and summed in bfloat16 or wider, within the bound.
No kernel may reach another device: no remote copies, remote signals or barrier semaphores. Data moves between devices by JAX's collectives and lax.ppermute only.
A program may use at most 192 MiB of HBM per device.

```python
import math
import jax
import jax.numpy as jnp
from jax import lax

D = 768
HEADS = 12
HEAD_DIM = 64
FF = 3072
LENGTH = 1024
SEQS = 8


def draw_block_size(key, part):
    key_draw, key_order = jax.random.split(jax.random.fold_in(key, 17))
    powers = jax.random.randint(key_draw, (SEQS,), 0, 3).astype(jnp.int32)
    spread_three = jax.random.permutation(key_order, 3).astype(jnp.int32)
    powers = powers.at[:3].set(spread_three)
    return (4 * jnp.power(2, powers)).astype(jnp.int32)


def block_scale(stream_key, shape, pieces, smallest, high):
    def one(axis_at, parts):
        heights = jax.random.uniform(jax.random.fold_in(jax.random.fold_in(stream_key, 6), axis_at), (parts,), jnp.float32, smallest / len(pieces), high / len(pieces))
        return jnp.repeat(jnp.exp(heights), shape[axis_at] // parts).reshape((-1,) + (1,) * (len(shape) - axis_at - 1))

    level = one(*pieces[0])
    for cut in pieces[1:]:
        level = level * one(*cut)
    return level


def normal_values(rng, shape, width, limit, pieces=(), held_as=jnp.bfloat16):
    result = width * jax.random.normal(rng, shape, jnp.float32)
    if pieces:
        result = result * block_scale(rng, shape, pieces, -0.22, 0.18)
    return jnp.clip(result, -limit, limit).astype(held_as)


def setup_inputs(seed: int = 0) -> dict:
    keys = jax.random.split(jax.random.key(seed), 10)
    tokens = normal_values(keys[0], (SEQS, 2 * LENGTH, D), 1.0, 6.0, ((0, 8), (1, 4)))
    cotangent = normal_values(keys[1], (SEQS, 2 * LENGTH, D), 1.0, 6.0, ((0, 8), (1, 4)))
    block_size = draw_block_size(jax.random.fold_in(keys[9], 71), 0)
    gain_attn = jnp.clip(1.0 + 0.18 * jax.random.normal(keys[3], (D,), jnp.float32), 0.1, 1.9)
    w_qkv = normal_values(keys[4], (D, 3 * D), D ** -0.5, 0.21875, ((0, 32),), jnp.float32)
    w_out = normal_values(keys[5], (D, D), (D // 32) ** -0.5, 1.25, ((0, 32),), jnp.float32)
    gain_mlp = jnp.clip(1.0 + 0.18 * jax.random.normal(keys[6], (D,), jnp.float32), 0.1, 1.9)
    w_up = normal_values(keys[7], (D, FF), D ** -0.5, 0.21875, ((0, 32),), jnp.float32)
    w_down = normal_values(keys[8], (FF, D), FF ** -0.5, 0.109375, ((0, 32),), jnp.float32)
    return {"tokens": tokens, "cotangent": cotangent, "block_size": block_size, "gain_attn": gain_attn, "w_qkv": w_qkv, "w_out": w_out, "gain_mlp": gain_mlp, "w_up": w_up, "w_down": w_down}


@jax.custom_vjp
def low(v):
    return lax.optimization_barrier(v.astype(jnp.bfloat16)).astype(jnp.float32)

@jax.custom_vjp
def low_back(v):
    return v

def low_keep(v):
    return (low(v), None)

def low_pass(kept, grad):
    return (grad,)

def back_keep(v):
    return (v, None)

def back_low(kept, grad):
    return (low(grad),)
low.defvjp(low_keep, low_pass)
low_back.defvjp(back_keep, back_low)
EPSILON = 1e-05
MASKED = -1e+30
HIGHEST_MODE = lax.Precision.HIGHEST

def layer_norm(values, gain):
    average = lax.optimization_barrier(jnp.mean(values, -1, keepdims=True))
    centred = values - average
    spread = lax.optimization_barrier(jnp.mean(centred * centred, -1, keepdims=True))
    return centred * lax.rsqrt(spread + EPSILON) * gain

def rotate(values, places):
    half_dim = values.shape[-1] // 2
    frequency = jnp.exp(-math.log(10000.0) * jnp.arange(half_dim, dtype=jnp.float32) / half_dim)
    angles = places.astype(jnp.float32)[:, None] * frequency[None, :]
    cosine = jnp.cos(angles)[:, None, :]
    sine_part = jnp.sin(angles)[:, None, :]
    first_half = values[..., :half_dim]
    second_half = values[..., half_dim:]
    return jnp.concatenate([first_half * cosine - second_half * sine_part, second_half * cosine + first_half * sine_part], -1)

def sequence_layer(inputs, block_len, params):
    gain_one, weight_qkv, weight_out, gain_two, weight_up, weight_down = params
    total_rows = 2 * LENGTH
    row_ids = jnp.arange(total_rows, dtype=jnp.int32)
    places = row_ids % LENGTH
    is_noisy = row_ids >= LENGTH
    block_ids = places // block_len
    earlier = block_ids[None, :] < block_ids[:, None]
    same_block = block_ids[None, :] == block_ids[:, None]
    clean_key = jnp.logical_not(is_noisy)[None, :]
    noisy_query = is_noisy[:, None]
    allowed = jnp.logical_or(jnp.logical_and(clean_key, jnp.where(noisy_query, earlier, jnp.logical_or(earlier, same_block))), jnp.logical_and(jnp.logical_and(noisy_query, is_noisy[None, :]), same_block))
    normed_one = low(layer_norm(inputs, gain_one))
    projected = low_back(jnp.dot(normed_one, weight_qkv, precision=HIGHEST_MODE))
    queries = low(rotate(projected[:, :D].reshape(total_rows, HEADS, HEAD_DIM), places))
    key_rows = low(rotate(projected[:, D:2 * D].reshape(total_rows, HEADS, HEAD_DIM), places))
    value_rows = low(projected[:, 2 * D:].reshape(total_rows, HEADS, HEAD_DIM))
    scores = low_back(jnp.einsum('qhd,khd->hqk', queries, key_rows, precision=HIGHEST_MODE) * HEAD_DIM ** (-0.5))
    scores = jnp.where(allowed[None], scores, MASKED)
    largest = lax.optimization_barrier(jnp.max(scores, -1, keepdims=True))
    exp_terms = jnp.where(allowed[None], jnp.exp(scores - largest), 0.0)
    attention_weights = exp_terms / lax.optimization_barrier(jnp.sum(exp_terms, -1, keepdims=True))
    mixed_rows = jnp.einsum('hqk,khd->qhd', low(attention_weights), value_rows, precision=HIGHEST_MODE)
    merged = low_back(low(mixed_rows.reshape(total_rows, D)))
    after_attention = inputs + low_back(jnp.dot(merged, weight_out, precision=HIGHEST_MODE))
    normed_two = low(layer_norm(after_attention, gain_two))
    hidden_pre = low_back(jnp.dot(normed_two, weight_up, precision=HIGHEST_MODE))
    activated = low(jax.nn.gelu(hidden_pre))
    return after_attention + low_back(jnp.dot(activated, weight_down, precision=HIGHEST_MODE))

def reference(tokens, cotangent, block_size, gain_attn, w_qkv, w_out, gain_mlp, w_up, w_down):
    layer_fn = jax.checkpoint(sequence_layer)

    def forward(inputs, gain_one, weight_qkv, weight_out, gain_two, weight_up, weight_down):
        params = (low(gain_one), low(weight_qkv), low(weight_out), low(gain_two), low(weight_up), low(weight_down))

        def per_sequence(sequence_pair):
            return layer_fn(sequence_pair[0], sequence_pair[1], params)
        return lax.map(per_sequence, (inputs, block_size))
    output, pullback = jax.vjp(forward, tokens.astype(jnp.float32), gain_attn, w_qkv, w_out, gain_mlp, w_up, w_down)
    gradients = pullback(cotangent.astype(jnp.float32))
    return (output.astype(jnp.bfloat16), gradients[0].astype(jnp.bfloat16), gradients[1], gradients[2], gradients[3], gradients[4], gradients[5], gradients[6])
```

```python
import functools
import math

import jax
import jax.numpy as jnp
from jax import lax
from jax.experimental import pallas as pl
from jax.experimental.pallas import tpu as pltpu
from jax.sharding import PartitionSpec as P

HEAD_DIM = 64
EPSILON = 1e-05
MASKED = -1e30
BF = jnp.bfloat16
F32 = jnp.float32
ALL = ("batch", "stream")
CHUNKS = 16
TILE = 256
VMEM = pl.BlockSpec(memory_space=pltpu.VMEM)
SMEM = pl.BlockSpec(memory_space=pltpu.SMEM)
HBM = pl.BlockSpec(memory_space=pl.ANY)
VMEM_BYTES = 58 * 1024 * 1024

HALF_BITS = ((2, 3, 1, 0), (2, 3, 0, 1))


def chip_bits(half, position):
    return sum(((position >> i) & 1) << HALF_BITS[half][i] for i in range(4))


def dot(a, b):
    return jnp.dot(a, b, preferred_element_type=F32)


def dot_nt(a, b):
    return lax.dot_general(a, b, (((1,), (1,)), ((), ())), preferred_element_type=F32)


def dot_tn(a, b):
    return lax.dot_general(a, b, (((0,), (0,)), ((), ())), preferred_element_type=F32)


def transposed(a):
    return a.astype(F32).T.astype(a.dtype)


def params():
    return pltpu.CompilerParams(vmem_limit_bytes=VMEM_BYTES)


def cost(flops, bytes_accessed, transcendentals=0):
    return pl.CostEstimate(
        flops=int(flops), bytes_accessed=int(bytes_accessed), transcendentals=int(transcendentals)
    )


def sds(shape, dtype):
    return jax.ShapeDtypeStruct(shape, dtype)


def chunk_copies(bufs, place, sems, me, store):
    copies = []
    for half in range(2):
        for position in range(CHUNKS):
            chip = me ^ chip_bits(half, position)
            buf = bufs[2 * half + position // 8].at[position % 8]
            view = place(half, chip)
            pair = (view, buf) if store else (buf, view)
            copies.append(pltpu.make_async_copy(*pair, sems.at[len(copies)]))
    return copies


def place_columns(ref, split):
    rows = ref.shape[0] // CHUNKS

    def place(half, chip):
        at = pl.ds(pl.multiple_of(chip * rows, 16), rows)
        return ref.at[at, pl.ds(0, split) if half == 0 else pl.ds(split, ref.shape[1] - split)]

    return place


def place_rows(ref):
    rows = ref.shape[0] // (2 * CHUNKS)

    def place(half, chip):
        return ref.at[pl.ds(pl.multiple_of((2 * chip + half) * rows, 16), rows), :]

    return place


def run_copies(copies):
    for copy in copies:
        copy.start()
    for copy in copies:
        copy.wait()


def normalize(values):
    centred = values - jnp.mean(values, -1, keepdims=True)
    inverse = lax.rsqrt(jnp.mean(centred * centred, -1, keepdims=True) + EPSILON)
    return centred * inverse, inverse


def swap_halves(values):
    lanes = lax.broadcasted_iota(jnp.int32, values.shape, 1)
    return jnp.where(
        lanes % HEAD_DIM < HEAD_DIM // 2,
        pltpu.roll(values, 128 - HEAD_DIM // 2, 1),
        pltpu.roll(values, HEAD_DIM // 2, 1),
    )


def turn(values, cosine, sine):
    return jnp.concatenate(
        [
            values[:, at : at + 128] * cosine + swap_halves(values[:, at : at + 128]) * sine
            for at in range(0, values.shape[1], 128)
        ],
        1,
    )


def qkv_kernel(info, x_ref, cos_ref, sin_ref, w0, w1, w2, w3, at_ref, qkv_ref, gains_ref, wout_ref, w_ref, sems):
    width = x_ref.shape[1]
    half_width = width // 2
    split = w0.shape[2]
    step = pl.program_id(0)

    @pl.when(step == 0)
    def _():
        run_copies(chunk_copies((w0, w1, w2, w3), place_columns(w_ref, split), sems, info[3], False))
        wout_ref[...] = w_ref[:, 3 * half_width : 4 * half_width]
        gains_ref[...] = w_ref[:, 4 * half_width :].astype(F32).T[:8]

    normed, _ = normalize(x_ref[...].astype(F32))
    low = (normed * gains_ref[0:1]).astype(BF)
    at_ref[...] = transposed(low)
    cosine, sine = cos_ref[...], sin_ref[...]

    @pl.when(step < 4)
    def _():
        queries = dot(low, w_ref[:, :half_width])
        qkv_ref[:, :half_width] = turn(queries, cosine, sine).astype(BF)

    keys = dot(low, w_ref[:, half_width : 2 * half_width])
    qkv_ref[:, half_width : 2 * half_width] = turn(keys, cosine, sine).astype(BF)
    qkv_ref[:, 2 * half_width :] = dot(low, w_ref[:, 2 * half_width : 3 * half_width]).astype(BF)


def tile_masks(info):
    noisy, block_len = info[1], info[2]
    keys = lax.broadcasted_iota(jnp.int32, (TILE, TILE), 0)
    queries = lax.broadcasted_iota(jnp.int32, (TILE, TILE), 1)
    starts = queries & (-block_len)
    clean_ok = keys < starts + jnp.where(noisy == 1, 0, block_len)
    local_ok = jnp.logical_and((keys & (-block_len)) == starts, noisy == 1)
    return clean_ok, local_ok


def head_lanes(shape, head, dim):
    lanes = lax.broadcasted_iota(jnp.int32, shape, dim)
    return (lanes < HEAD_DIM) if head == 0 else (lanes >= HEAD_DIM)


def pick(mask, values, other=0.0):
    return jnp.where(mask, values.astype(F32), other).astype(BF)


def pair_scores(query_head, clean_keys, own_keys, tile, masks):
    size = (tile + 1) * TILE
    scores = dot_nt(clean_keys[:size], query_head)
    own = dot_nt(own_keys[tile * TILE : size], query_head)
    parts = [scores[: size - TILE]] if tile else []
    parts.append(jnp.where(masks[0], scores[size - TILE :], MASKED))
    parts.append(jnp.where(masks[1], own, MASKED))
    return parts


def attend_kernel(info, q_ref, k_ref, v_ref, kc_ref, vc_ref, ot_ref, lse_ref):
    masks = tile_masks(info)
    length = q_ref.shape[0]
    own_vt = v_ref[...].astype(F32).T
    clean_vt = vc_ref[...].astype(F32).T
    own_heads = [pick(head_lanes(own_vt.shape, h, 0), own_vt, 1.0) for h in range(2)]
    clean_heads = [pick(head_lanes(own_vt.shape, h, 0), clean_vt, 1.0) for h in range(2)]
    for tile in range(length // TILE):
        at = tile * TILE
        queries = q_ref[at : at + TILE, :] * BF(HEAD_DIM**-0.5)
        outs, totals = [], []
        for h in range(2):
            query_head = pick(head_lanes(queries.shape, h, 1), queries)
            parts = pair_scores(query_head, kc_ref, k_ref, tile, masks)
            largest = functools.reduce(
                jnp.maximum, [jnp.max(part, 0, keepdims=True) for part in parts]
            )
            weights = [jnp.exp(part - largest).astype(BF) for part in parts]
            mixed = dot(own_heads[h][:, at : at + TILE], weights[-1])
            mixed += dot(clean_heads[h][:, at : at + TILE], weights[-2])
            if tile:
                mixed += dot(clean_heads[h][:, :at], weights[0])
            total = mixed[HEAD_DIM : HEAD_DIM + 1] if h == 0 else mixed[0:1]
            outs.append(mixed[h * HEAD_DIM : (h + 1) * HEAD_DIM] / total)
            lse_ref[h : h + 1, at : at + TILE] = largest + jnp.log(total)
        ot_ref[:, at : at + TILE] = jnp.concatenate(outs, 0).astype(BF)


def out_kernel(info, x_ref, ot_own, ot_oth, wo_own, wo_oth, gains_ref, r1_ref, a2_ref, ot_all):
    core = info[0]
    rows, width = x_ref.shape
    half = width // 2
    mine = pl.ds(pl.multiple_of(core * half, 128), half)
    theirs = pl.ds(pl.multiple_of((1 - core) * half, 128), half)
    at_rows = pl.ds(pl.multiple_of(core * rows, 128), rows)
    ot_all[mine, :] = ot_own[:, at_rows]
    ot_all[theirs, :] = ot_oth[:, at_rows]
    merged = transposed(ot_all[...])
    r1_ref[:, mine] = dot(merged, wo_own[...])
    r1_ref[:, theirs] = dot(merged, wo_oth[...])
    r1 = x_ref[...].astype(F32) + r1_ref[...]
    r1_ref[...] = r1
    normed, _ = normalize(r1)
    a2_ref[...] = (normed * gains_ref[1:2]).astype(BF)


def gelu_parts(u):
    c = math.sqrt(2.0 / math.pi)
    square = u * u
    inner = jnp.tanh(c * u * (1.0 + 0.044715 * square))
    half = 0.5 * (1.0 + inner)
    slope = half + 0.5 * u * (1.0 - inner * inner) * c * (1.0 + 3 * 0.044715 * square)
    return u * half, slope


def up_kernel(
    info, a2_own, a2_oth, dy_own, dy_oth, w0, w1, w2, w3,
    g_ref, slope_ref, at_ref, d0, d1, d2, d3, w_ref, dy_all, dw_ref, sems,
):
    rows, width = a2_own.shape
    copies = chunk_copies((w0, w1, w2, w3), place_columns(w_ref, w0.shape[2]), sems, info[3], False)
    for copy in copies:
        copy.start()
    dy_all[:rows, :] = dy_own[...]
    dy_all[rows:, :] = dy_oth[...]
    for copy in copies:
        copy.wait()
    for at in range(0, 2 * rows, TILE):
        a2 = (a2_own if at < rows else a2_oth)[at % rows : at % rows + TILE, :]
        at_ref[:, at : at + TILE] = transposed(a2)
        for col in range(0, w_ref.shape[1], 512):
            active, slope = gelu_parts(dot(a2, w_ref[:, col : col + 512]))
            g_ref[at : at + TILE, col : col + 512] = active.astype(BF)
            slope_ref[at : at + TILE, col : col + 512] = slope.astype(BF)
    for col in range(0, w_ref.shape[1], TILE):
        dw_ref[col : col + TILE, :] = dot_tn(g_ref[:, col : col + TILE], dy_all[...]).astype(BF)
    run_copies(chunk_copies((d0, d1, d2, d3), place_rows(dw_ref), sems, info[3], True))


def down_kernel(
    info, a2t_ref, g_ref, slope_ref, dy_own, dy_oth, u0, u1, u2, u3, w0, w1, w2, w3,
    e_ref, y_ref, send_ref, d0, d1, d2, d3, up_ref, w_ref, du_ref, dw_ref, sems, more_sems,
):
    rows, width = dy_own.shape
    copies = chunk_copies((w0, w1, w2, w3), place_rows(w_ref), sems, info[3], False)
    copies += chunk_copies((u0, u1, u2, u3), place_columns(up_ref, u0.shape[2]), more_sems, info[3], False)
    run_copies(copies)
    hidden = w_ref.shape[0]
    for at in range(0, 2 * rows, TILE):
        mine = at < rows
        low = at % rows
        dy = (dy_own if mine else dy_oth)[low : low + TILE, :]
        for col in range(0, hidden, 512):
            grad = dot_nt(dy, w_ref[col : col + 512, :])
            du_ref[at : at + TILE, col : col + 512] = (
                grad * slope_ref[at : at + TILE, col : col + 512].astype(F32)
            ).astype(BF)
    for col in range(0, hidden, TILE):
        dw_ref[:, col : col + TILE] = dot(a2t_ref[...], du_ref[:, col : col + TILE]).astype(BF)
    out_copies = chunk_copies((d0, d1, d2, d3), place_columns(dw_ref, d0.shape[2]), sems, info[3], True)
    for copy in out_copies:
        copy.start()
    for at in range(0, 2 * rows, TILE):
        mine = at < rows
        low = at % rows
        e = dot_nt(du_ref[at : at + TILE, :], up_ref[...])
        y = dot(g_ref[at : at + TILE, :], w_ref[...])
        if mine:
            e_ref[low : low + TILE, :] = e
            y_ref[low : low + TILE, :] = y
        else:
            send_ref[0, low : low + TILE, :] = e.astype(BF)
            send_ref[1, low : low + TILE, :] = y.astype(BF)
    for copy in out_copies:
        copy.wait()


def norm_back(upstream, normed, inverse, gain):
    scaled = upstream * gain
    return inverse * (
        scaled
        - jnp.mean(scaled, -1, keepdims=True)
        - normed * jnp.mean(scaled * normed, -1, keepdims=True)
    )


def mlp_back_kernel(r1_ref, e_ref, y_ref, recv_ref, dy_ref, gains_ref, out_ref, dr1_ref, dr_ref, gg_ref):
    total = jnp.zeros((1, r1_ref.shape[1]), F32)
    for at in range(0, r1_ref.shape[0], TILE):
        rows = slice(at, at + TILE)
        r1 = r1_ref[rows, :]
        out_ref[rows, :] = (r1 + y_ref[rows, :] + recv_ref[1, rows, :].astype(F32)).astype(BF)
        normed, inverse = normalize(r1)
        upstream = e_ref[rows, :] + recv_ref[0, rows, :].astype(F32)
        total += jnp.sum(upstream * normed, 0, keepdims=True)
        dr1 = dy_ref[rows, :].astype(F32) + norm_back(upstream, normed, inverse, gains_ref[1:2])
        dr1_ref[rows, :] = dr1
        dr_ref[rows, :] = dr1.astype(BF)
    gg_ref[...] = jnp.broadcast_to(total, gg_ref.shape)


def out_back_kernel(info, dr_own, dr_oth, wo_own, wo_oth, ot_own, ot_oth, do_ref, dwo_ref, dr_all, ot_all):
    core = info[0]
    rows, width = dr_own.shape
    half = width // 2
    mine = pl.ds(pl.multiple_of(core * half, 128), half)
    theirs = pl.ds(pl.multiple_of((1 - core) * half, 128), half)
    dr_all[pl.ds(pl.multiple_of(core * rows, 128), rows), :] = dr_own[...]
    dr_all[pl.ds(pl.multiple_of((1 - core) * rows, 128), rows), :] = dr_oth[...]
    ot_all[mine, :] = ot_own[...]
    ot_all[theirs, :] = ot_oth[...]
    grad = dot_nt(dr_all[:, mine], wo_own[mine, :])
    grad += dot_nt(dr_all[:, theirs], wo_oth[mine, :])
    do_ref[...] = grad.astype(BF)
    dwo_ref[...] = dot(ot_all[...], dr_all[:, mine]).astype(BF)


def attend_back_kernel(
    info, q_ref, k_ref, v_ref, kc_ref, vc_ref, do_ref, ot_ref, lse_ref, cos_ref, sin_ref,
    dq_ref, dk_ref, dv_ref, dkc_ref, dvc_ref, dk_sum, dv_sum,
):
    masks = tile_masks(info)
    length = q_ref.shape[0]
    dk_sum[...] = jnp.zeros_like(dk_sum)
    dv_sum[...] = jnp.zeros_like(dv_sum)
    scale = HEAD_DIM**-0.5
    own_kt = k_ref[...].astype(F32).T * scale
    clean_kt = kc_ref[...].astype(F32).T * scale
    own_heads = [pick(head_lanes(own_kt.shape, h, 0), own_kt) for h in range(2)]
    clean_heads = [pick(head_lanes(own_kt.shape, h, 0), clean_kt) for h in range(2)]
    for tile in range(length // TILE):
        at = tile * TILE
        size = at + TILE
        cosine, sine = cos_ref[at:size, :], -sin_ref[at:size, :]
        queries = q_ref[at:size, :] * BF(scale)
        grads = do_ref[at:size, :]
        products = grads.astype(F32).T * ot_ref[:, at:size].astype(F32)
        dq = jnp.zeros((128, TILE), F32)
        dk = jnp.zeros((TILE, 128), F32)
        dv = jnp.zeros((TILE, 128), F32)
        for h in range(2):
            lanes = head_lanes(queries.shape, h, 1)
            query_head = pick(lanes, queries)
            grad_head = pick(lanes, grads)
            shared = jnp.sum(products[h * HEAD_DIM : (h + 1) * HEAD_DIM], 0, keepdims=True)
            parts = pair_scores(query_head, kc_ref, k_ref, tile, masks)
            clean_dp = dot_nt(vc_ref[:size, :], grad_head)
            slopes = [clean_dp[:at]] if tile else []
            slopes += [clean_dp[at:], dot_nt(v_ref[at:size, :], grad_head)]
            lse = lse_ref[h : h + 1, at:size]
            spans = ([(0, at)] if tile else []) + [(at, size), None]
            for part, slope, span in zip(parts, slopes, spans):
                weights = jnp.exp(part - lse)
                change = (weights * (slope - shared)).astype(BF)
                weights = weights.astype(BF)
                if span is None:
                    dv += dot(weights, grad_head)
                    dk += dot(change, query_head)
                    dq += dot(own_heads[h][:, at:size], change)
                else:
                    rows = slice(*span)
                    dv_sum[rows, :] += dot(weights, grad_head)
                    dk_sum[rows, :] += dot(change, query_head)
                    dq += dot(clean_heads[h][:, rows], change)
        dq_ref[at:size, :] = turn(dq.T, cosine, sine).astype(BF)
        dk_ref[at:size, :] = turn(dk, cosine, sine).astype(BF)
        dv_ref[at:size, :] = dv.astype(BF)
    dkc_ref[...] = turn(dk_sum[...], cos_ref[...], -sin_ref[...]).astype(BF)
    dvc_ref[...] = dv_sum[...].astype(BF)


def qkv_back_kernel(
    info, dq_ref, dk_ref, dv_ref, dkc_ref, dvc_ref, x_ref, at_ref, gains_ref, gg_ref, dwo_ref,
    w0, w1, w2, w3, own_ref, own_send, clean_ref, d0, d1, d2, d3, w_ref, dw_ref, part_ref, clean_part, sems,
):
    core, noisy = info[0], info[1]
    length, half = dq_ref.shape
    width = 2 * half
    rows = length // 2
    split = w0.shape[2]
    run_copies(chunk_copies((w0, w1, w2, w3), place_columns(w_ref, split), sems, info[3], False))
    is_noisy = (noisy == 1).astype(F32)
    gain_total = jnp.zeros((1, width), F32)
    for at in range(0, length, TILE):
        span = slice(at, at + TILE)
        clean = dot_nt(dkc_ref[span, :], w_ref[:, half : 2 * half])
        clean += dot_nt(dvc_ref[span, :], w_ref[:, 2 * half : 3 * half])
        own = dot_nt(dq_ref[span, :], w_ref[:, :half])
        own += dot_nt(dk_ref[span, :], w_ref[:, half : 2 * half])
        own += dot_nt(dv_ref[span, :], w_ref[:, 2 * half : 3 * half])
        own += clean * (1.0 - is_noisy)
        clean *= is_noisy
        normed, _ = normalize(x_ref[span, :].astype(F32))
        clean_normed, _ = normalize(x_ref[length + at : length + at + TILE, :].astype(F32))
        gain_total += jnp.sum(own * normed + clean * clean_normed, 0, keepdims=True)
        part_ref[span, :] = own
        clean_part[span, :] = clean.astype(BF)
    mine = pl.ds(pl.multiple_of(core * rows, 128), rows)
    theirs = pl.ds(pl.multiple_of((1 - core) * rows, 128), rows)
    own_ref[...] = part_ref[mine, :]
    own_send[0] = part_ref[theirs, :].astype(BF)
    own_send[1] = clean_part[theirs, :]
    clean_ref[...] = clean_part[mine, :]
    dw_ref[:, :half] = dot(at_ref[:, :length], dq_ref[...]).astype(BF)
    dw_ref[:, half : 2 * half] = (
        dot(at_ref[:, :length], dk_ref[...]) + dot(at_ref[:, length:], dkc_ref[...])
    ).astype(BF)
    dw_ref[:, 2 * half : 3 * half] = (
        dot(at_ref[:, :length], dv_ref[...]) + dot(at_ref[:, length:], dvc_ref[...])
    ).astype(BF)
    dw_ref[:, 3 * half : 4 * half] = dwo_ref[...]
    lane_row = lax.broadcasted_iota(jnp.int32, (128, width), 0)
    packed = jnp.where(lane_row == 0, gain_total, jnp.where(lane_row == 1, gg_ref[0:1], 0.0))
    dw_ref[:, 4 * half :] = packed.T.astype(BF)
    run_copies(chunk_copies((d0, d1, d2, d3), place_columns(dw_ref, split), sems, info[3], True))


def input_back_kernel(x_ref, own_ref, recv_ref, clean_ref, dr1_ref, gains_ref, out_ref):
    for at in range(0, x_ref.shape[0], TILE):
        rows = slice(at, at + TILE)
        normed, inverse = normalize(x_ref[rows, :].astype(F32))
        upstream = own_ref[rows, :] + recv_ref[rows, :].astype(F32) + clean_ref[rows, :].astype(F32)
        out_ref[rows, :] = (
            dr1_ref[rows, :] + norm_back(upstream, normed, inverse, gains_ref[0:1])
        ).astype(BF)


def core_swap(value):
    size = lax.axis_size("stream")
    return lax.ppermute(value, "stream", [(i, i ^ 1) for i in range(size)])


def axis_swap(value, bit):
    if bit == 0:
        return lax.ppermute(value, "stream", [(i, i ^ 2) for i in range(lax.axis_size("stream"))])
    mask = 1 << (bit - 1)
    return lax.ppermute(value, "batch", [(i, i ^ mask) for i in range(lax.axis_size("batch"))])


def chip_groups():
    batches, streams = lax.axis_size("batch"), lax.axis_size("stream")
    return [
        [b * streams + 2 * x + c for b in range(batches) for x in range(streams // 2)]
        for c in range(2)
    ]


def gather(chunk, split, stacked=False):
    if 2 * lax.axis_size("batch") == CHUNKS:
        held = chunk[None]
        for bit in HALF_BITS[0][:2]:
            held = jnp.concatenate([held, axis_swap(held, bit)], 0)
        result = []
        for half in range(2):
            part = held[:, :, :split] if half == 0 else held[:, :, split:]
            third = axis_swap(part, HALF_BITS[half][2])
            part = jnp.concatenate([part, third], 0)
            result += [part, axis_swap(part, HALF_BITS[half][3])]
        return result
    full = lax.all_gather(chunk, ALL, axis=0, tiled=True, axis_index_groups=chip_groups())
    rows = full.shape[0] // CHUNKS
    result = []
    for half in range(2):
        if stacked:
            part = full.reshape(CHUNKS, 2, rows // 2, -1)[:, half]
        else:
            part = full[:, :split] if half == 0 else full[:, split:]
            part = part.reshape(CHUNKS, rows, -1)
        part = jnp.stack([part[chip_bits(half, p)] for p in range(CHUNKS)])
        result += [part[:8], part[8:]]
    return result


def scatter_sum(parts, stacked=False):
    result = []
    if 2 * lax.axis_size("batch") == CHUNKS:
        for half in range(2):
            keep, send = parts[2 * half], parts[2 * half + 1]
            for level in (3, 2, 1, 0):
                received = axis_swap(send, HALF_BITS[half][level])
                total = keep.astype(F32) + received.astype(F32)
                if level:
                    count = 1 << (level - 1)
                    keep, send = total[:count].astype(BF), total[count:].astype(BF)
            result.append(total[0])
        return result
    order = [[chip_bits(half, p) for p in range(CHUNKS)] for half in range(2)]
    pieces = []
    for half in range(2):
        both = jnp.concatenate(parts[2 * half : 2 * half + 2], 0)
        pieces.append(jnp.stack([both[order[half].index(k)] for k in range(CHUNKS)]).astype(F32))
    axis = 1 if stacked else 2
    full = jnp.concatenate(pieces, axis)
    full = full.reshape(-1, full.shape[2])
    mine = lax.psum_scatter(full, ALL, scatter_dimension=0, tiled=True, axis_index_groups=chip_groups())
    if stacked:
        return [mine]
    split = pieces[0].shape[2]
    return [mine[:, :split], mine[:, split:]]


def local(tokens, cotangent, block_size, gain_attn, w_qkv, w_out, gain_mlp, w_up, w_down):
    rows, width = tokens.shape[1:]
    half = width // 2
    length = 2 * rows
    batches = lax.axis_size("batch")
    chips = 2 * batches
    hidden = w_up.shape[1] // 2
    fast = chips == CHUNKS
    stream, batch = lax.axis_index("stream"), lax.axis_index("batch")
    core, noisy = stream % 2, stream // 2
    me = batch * 2 + noisy if fast else jnp.zeros_like(batch)
    info = jnp.stack([core, noisy, block_size[0], me]).astype(jnp.int32)
    first = core == 0
    n_rows = w_qkv.shape[0]
    piece = width // CHUNKS

    def in_order(own, other, axis):
        return jnp.where(
            first, jnp.concatenate([own, other], axis), jnp.concatenate([other, own], axis)
        )

    def mine_theirs(zero, one):
        return jnp.where(first, zero, one), jnp.where(first, one, zero)

    low = w_qkv.astype(BF).reshape(n_rows, 3, 2, half)
    out_low = w_out.astype(BF)
    gains = jnp.stack([gain_attn, gain_mlp], 1).astype(BF)
    gains = jnp.pad(gains, ((0, 0), (0, 126)))
    one = [
        jnp.concatenate(
            [low[:, :, c].reshape(n_rows, -1), out_low[:, c * half : (c + 1) * half], gains], 1
        )
        for c in range(2)
    ]
    mine, theirs = mine_theirs(*one)
    chunk_one = in_order(mine, core_swap(theirs), 0)
    up_low = w_up.astype(BF).reshape(n_rows, chips, 2, -1)
    mine, theirs = mine_theirs(*[up_low[:, :, c].reshape(n_rows, -1) for c in range(2)])
    chunk_two = in_order(mine, core_swap(theirs), 0)
    down_low = w_down.astype(BF)
    if fast:
        down_low = jnp.concatenate([down_low[:piece], down_low[piece:]], 1)

    x_own = tokens[0]
    dy_own = cotangent[0]
    streams = lax.axis_size("stream")
    to_noisy = [(i, i + streams // 2) for i in range(streams // 2)]
    to_clean = [(b, a) for a, b in to_noisy]
    arrived = lax.ppermute(x_own, "stream", to_noisy)
    clean_own = jnp.where(noisy == 1, arrived, x_own)
    split_one = 7 * 128
    bufs_one = gather(chunk_one, split_one)
    x_oth = core_swap(x_own)
    clean_oth = core_swap(clean_own)
    x_all = jnp.concatenate([in_order(x_own, x_oth, 0), in_order(clean_own, clean_oth, 0)], 0)
    dy_oth = core_swap(dy_own)
    bufs_two = gather(chunk_two, hidden // 2)
    bufs_three = gather(down_low, width, stacked=True)

    places = jnp.arange(length, dtype=jnp.int32)
    lanes = jnp.arange(128, dtype=jnp.int32)
    half_dim = HEAD_DIM // 2
    frequency = jnp.exp(-math.log(10000.0) * (lanes % half_dim).astype(F32) / half_dim)
    angles = places.astype(F32)[:, None] * frequency[None, :]
    cosine = jnp.cos(angles)
    sine = jnp.where((lanes % HEAD_DIM < half_dim)[None], -jnp.sin(angles), jnp.sin(angles))

    cols_one = 4 * half + 128
    tiles = length // TILE
    a1t, qkv, gain_rows, wo_own = pl.pallas_call(
        qkv_kernel,
        grid=(2 * tiles,),
        in_specs=[
            SMEM,
            pl.BlockSpec((TILE, width), lambda i: (i, 0)),
            pl.BlockSpec((TILE, 128), lambda i: (i % tiles, 0)),
            pl.BlockSpec((TILE, 128), lambda i: (i % tiles, 0)),
        ]
        + [HBM] * 4,
        out_specs=[
            pl.BlockSpec((width, TILE), lambda i: (0, i)),
            pl.BlockSpec((TILE, 3 * half), lambda i: (i, 0)),
            pl.BlockSpec((8, width), lambda i: (0, 0)),
            pl.BlockSpec((width, half), lambda i: (0, 0)),
        ],
        out_shape=[
            sds((width, 2 * length), BF),
            sds((2 * length, 3 * half), BF),
            sds((8, width), F32),
            sds((width, half), BF),
        ],
        scratch_shapes=[pltpu.VMEM((width, cols_one), BF), pltpu.SemaphoreType.DMA((32,))],
        compiler_params=params(),
        cost_estimate=cost(2 * length * width * 2.5 * width, 12 << 20),
    )(info, x_all, cosine, sine, *bufs_one)
    wo_oth = core_swap(wo_own)

    pairs = half // 128

    def pair_spec(part, clean):
        return pl.BlockSpec((length, 128), lambda p: (clean, part * pairs + p))

    qkv_specs = [pair_spec(0, 0), pair_spec(1, 0), pair_spec(2, 0), pair_spec(1, 1), pair_spec(2, 1)]
    attend_flops = 2 * 2 * length * length * half
    ot_own, lse = pl.pallas_call(
        attend_kernel,
        grid=(pairs,),
        in_specs=[SMEM] + qkv_specs,
        out_specs=[
            pl.BlockSpec((128, length), lambda p: (p, 0)),
            pl.BlockSpec((8, length), lambda p: (p, 0)),
        ],
        out_shape=[sds((half, length), BF), sds((8 * pairs, length), F32)],
        compiler_params=params(),
        cost_estimate=cost(4 * attend_flops, 6 << 20, length * length * 6),
    )(info, qkv, qkv, qkv, qkv, qkv)
    ot_oth = core_swap(ot_own)

    r1, a2_own = pl.pallas_call(
        out_kernel,
        in_specs=[SMEM] + [VMEM] * 6,
        out_specs=[VMEM] * 2,
        out_shape=[sds((rows, width), F32), sds((rows, width), BF)],
        scratch_shapes=[pltpu.VMEM((width, rows), BF)],
        compiler_params=params(),
        cost_estimate=cost(2 * rows * width * width, 6 << 20),
    )(info, x_own, ot_own, ot_oth, wo_own, wo_oth, gain_rows)
    a2_oth = core_swap(a2_own)

    down_bufs = [sds((8, piece, width), BF)] * 4
    up_bufs = [sds((8, piece, hidden // 2), BF)] * 4
    g, slope, a2t, *down_parts = pl.pallas_call(
        up_kernel,
        in_specs=[SMEM] + [VMEM] * 4 + [HBM] * 4,
        out_specs=[VMEM] * 3 + [HBM] * 4,
        out_shape=[sds((length, hidden), BF), sds((length, hidden), BF), sds((width, length), BF)]
        + down_bufs,
        scratch_shapes=[
            pltpu.VMEM((width, hidden), BF),
            pltpu.VMEM((length, width), BF),
            pltpu.VMEM((hidden, width), BF),
            pltpu.SemaphoreType.DMA((32,)),
        ],
        compiler_params=params(),
        cost_estimate=cost(4 * length * width * hidden, 16 << 20, length * hidden),
    )(info, a2_own, a2_oth, dy_own, dy_oth, *bufs_two)

    e_own, y_own, ey_send, *up_parts = pl.pallas_call(
        down_kernel,
        in_specs=[SMEM] + [VMEM] * 5 + [HBM] * 8,
        out_specs=[VMEM] * 3 + [HBM] * 4,
        out_shape=[sds((rows, width), F32), sds((rows, width), F32), sds((2, rows, width), BF)]
        + up_bufs,
        scratch_shapes=[
            pltpu.VMEM((width, hidden), BF),
            pltpu.VMEM((hidden, width), BF),
            pltpu.VMEM((length, hidden), BF),
            pltpu.VMEM((width, hidden), BF),
            pltpu.SemaphoreType.DMA((32,)),
            pltpu.SemaphoreType.DMA((32,)),
        ],
        compiler_params=params(),
        cost_estimate=cost(8 * length * width * hidden, 20 << 20),
    )(info, a2t, g, slope, dy_own, dy_oth, *bufs_two, *bufs_three)
    grad_down = scatter_sum(down_parts, stacked=True)
    ey_recv = core_swap(ey_send)
    grad_up = scatter_sum(up_parts)

    output, dr1, dr_own, gain_two_part = pl.pallas_call(
        mlp_back_kernel,
        in_specs=[VMEM] * 6,
        out_specs=[VMEM] * 4,
        out_shape=[
            sds((rows, width), BF),
            sds((rows, width), F32),
            sds((rows, width), BF),
            sds((8, width), F32),
        ],
        compiler_params=params(),
        cost_estimate=cost(rows * width * 40, 12 << 20),
    )(r1, e_own, y_own, ey_recv, dy_own, gain_rows)
    dr_oth = core_swap(dr_own)

    do, dwo = pl.pallas_call(
        out_back_kernel,
        in_specs=[SMEM] + [VMEM] * 6,
        out_specs=[VMEM] * 2,
        out_shape=[sds((length, half), BF), sds((width, half), BF)],
        scratch_shapes=[pltpu.VMEM((length, width), BF), pltpu.VMEM((width, length), BF)],
        compiler_params=params(),
        cost_estimate=cost(4 * length * width * half, 6 << 20),
    )(info, dr_own, dr_oth, wo_own, wo_oth, ot_own, ot_oth)

    column = pl.BlockSpec((length, 128), lambda p: (0, p))
    whole = pl.BlockSpec((length, 128), lambda p: (0, 0))
    grads = pl.pallas_call(
        attend_back_kernel,
        grid=(pairs,),
        in_specs=[SMEM]
        + qkv_specs
        + [
            column,
            pl.BlockSpec((128, length), lambda p: (p, 0)),
            pl.BlockSpec((8, length), lambda p: (p, 0)),
            whole,
            whole,
        ],
        out_specs=[column] * 5,
        out_shape=[sds((length, half), BF)] * 5,
        scratch_shapes=[pltpu.VMEM((length, 128), F32)] * 2,
        compiler_params=params(),
        cost_estimate=cost(10 * attend_flops, 10 << 20, length * length * 6),
    )(info, qkv, qkv, qkv, qkv, qkv, do, ot_own, lse, cosine, sine)

    own_part, own_send, clean_part, *one_parts = pl.pallas_call(
        qkv_back_kernel,
        in_specs=[SMEM] + [VMEM] * 10 + [HBM] * 4,
        out_specs=[VMEM] * 3 + [HBM] * 4,
        out_shape=[
            sds((rows, width), F32),
            sds((2, rows, width), BF),
            sds((rows, width), BF),
        ]
        + [sds((8, piece, split_one), BF)] * 2
        + [sds((8, piece, cols_one - split_one), BF)] * 2,
        scratch_shapes=[
            pltpu.VMEM((width, cols_one), BF),
            pltpu.VMEM((width, cols_one), BF),
            pltpu.VMEM((length, width), F32),
            pltpu.VMEM((length, width), BF),
            pltpu.SemaphoreType.DMA((32,)),
        ],
        compiler_params=params(),
        cost_estimate=cost(20 * length * width * half, 20 << 20),
    )(info, *grads, x_all, a1t, gain_rows, gain_two_part, dwo, *bufs_one)
    swapped = core_swap(own_send)
    clean_total = (clean_part.astype(F32) + swapped[1].astype(F32)).astype(BF)
    clean_back = lax.ppermute(clean_total, "stream", to_clean)
    grad_one = scatter_sum(one_parts)

    input_grad = pl.pallas_call(
        input_back_kernel,
        in_specs=[VMEM] * 6,
        out_specs=VMEM,
        out_shape=sds((rows, width), BF),
        compiler_params=params(),
        cost_estimate=cost(rows * width * 40, 8 << 20),
    )(x_own, own_part, swapped[0], clean_back, dr1, gain_rows)

    def finish(halves):
        total = jnp.concatenate(halves, 1)
        keep, send = mine_theirs(total[:n_rows], total[n_rows:])
        received = core_swap(send)
        return keep, received, mine_theirs(keep, received)

    keep, received, ordered = finish(grad_one)
    gain_sum = keep[:, 4 * half : 4 * half + 2] + received[:, 4 * half : 4 * half + 2]
    grad_qkv = jnp.stack([v[:, : 3 * half].reshape(n_rows, 3, half) for v in ordered], 2)
    grad_out = jnp.concatenate([v[:, 3 * half : 4 * half] for v in ordered], 1)
    _, _, ordered = finish(grad_up)
    grad_w_up = jnp.stack([v.reshape(n_rows, chips, -1) for v in ordered], 2)
    return (
        output[None],
        input_grad[None],
        gain_sum[:, 0],
        grad_qkv.reshape(n_rows, 3 * width),
        grad_out,
        gain_sum[:, 1],
        grad_w_up.reshape(n_rows, 2 * hidden),
        jnp.concatenate(grad_down, 0),
    )


def solution(mesh):
    rows = P("batch", "stream", None)
    flat, split = P(ALL), P(ALL, None)
    return jax.shard_map(
        local,
        mesh=mesh,
        in_specs=(rows, rows, P("batch"), flat, split, split, flat, split, split),
        out_specs=(rows, rows, flat, split, split, flat, split, split),
        check_vma=False,
    )
```

```python
import functools
import math

import jax
import jax.numpy as jnp
from jax import lax
from jax.experimental import pallas as pl
from jax.experimental.pallas import tpu as pltpu
from jax.sharding import PartitionSpec as P

HEAD_DIM = 64
EPSILON = 1e-05
MASKED = -1e30
BF = jnp.bfloat16
F32 = jnp.float32
ALL = ("batch", "stream")
CHUNKS = 16
BLOCK = 128
TILE = 256
VMEM = pl.BlockSpec(memory_space=pltpu.VMEM)
SMEM = pl.BlockSpec(memory_space=pltpu.SMEM)
HBM = pl.BlockSpec(memory_space=pl.ANY)


def chip_bits(position, core):
    last = ((position >> 2) & 1) * (2 - core) ^ ((position >> 3) & 1) * (1 + core)
    return (position & 3) << 2 ^ last


def dot(a, b):
    return jnp.dot(a, b, preferred_element_type=F32)


def dot_nt(a, b):
    return lax.dot_general(a, b, (((1,), (1,)), ((), ())), preferred_element_type=F32)


def dot_tn(a, b):
    return lax.dot_general(a, b, (((0,), (0,)), ((), ())), preferred_element_type=F32)


def transposed(a):
    return a.astype(F32).T.astype(a.dtype)


def params(mib):
    return pltpu.CompilerParams(vmem_limit_bytes=mib << 20)


def cost(flops, bytes_accessed, transcendentals=0):
    return pl.CostEstimate(
        flops=int(flops), bytes_accessed=int(bytes_accessed), transcendentals=int(transcendentals)
    )


def sds(shape, dtype):
    return jax.ShapeDtypeStruct(shape, dtype)


def chunk_copies(bufs, ref, sems, info, store):
    rows = ref.shape[0] // CHUNKS
    copies = []
    for position in range(CHUNKS):
        chip = info[3] ^ chip_bits(position, info[0])
        buf = bufs[position // 8].at[position % 8]
        view = ref.at[pl.ds(pl.multiple_of(chip * rows, 16), rows), :]
        pair = (view, buf) if store else (buf, view)
        copies.append(pltpu.make_async_copy(*pair, sems.at[position]))
    return copies


def start(copies):
    for copy in copies:
        copy.start()
    return copies


def wait(copies):
    for copy in copies:
        copy.wait()


def fetch(pairs, sems):
    return start([pltpu.make_async_copy(a, b, sems.at[i]) for i, (a, b) in enumerate(pairs)])


def normalize(values):
    centred = values - jnp.mean(values, -1, keepdims=True)
    inverse = lax.rsqrt(jnp.mean(centred * centred, -1, keepdims=True) + EPSILON)
    return centred * inverse, inverse


def norm_back(scaled, normed, inverse):
    return inverse * (
        scaled
        - jnp.mean(scaled, -1, keepdims=True)
        - normed * jnp.mean(scaled * normed, -1, keepdims=True)
    )


def swap_halves(values):
    lanes = lax.broadcasted_iota(jnp.int32, values.shape, 1)
    return jnp.where(
        lanes % HEAD_DIM < HEAD_DIM // 2,
        pltpu.roll(values, 128 - HEAD_DIM // 2, 1),
        pltpu.roll(values, HEAD_DIM // 2, 1),
    )


def turn(values, cosine, sine):
    return jnp.concatenate(
        [
            values[:, at : at + 128] * cosine + swap_halves(values[:, at : at + 128]) * sine
            for at in range(0, values.shape[1], 128)
        ],
        1,
    )


def norm_kernel(info, x_own, x_oth, clean_own, clean_oth, a1_ref):
    core = info[0]
    rows = x_own.shape[0]
    for i, ref in enumerate((x_own, x_oth, clean_own, clean_oth)):
        slot = 2 * (i // 2) + (core if i % 2 == 0 else 1 - core)
        for at in range(0, rows, TILE):
            normed, _ = normalize(ref[at : at + TILE, :].astype(F32))
            a1_ref[slot, at : at + TILE, :] = normed.astype(BF)


def qkv_kernel(info, a1_ref, cos_ref, sin_ref, w0, w1, qkv_ref, wout_ref, w_ref, sems):
    half = a1_ref.shape[1] // 2
    step = pl.program_id(0)

    @pl.when(step == 0)
    def _():
        wait(start(chunk_copies((w0, w1), w_ref, sems, info, False)))
        wout_ref[...] = w_ref[:, 3 * half :]

    low = a1_ref[...]
    cosine, sine = cos_ref[...], sin_ref[...]
    keys = dot(low, w_ref[:, half : 2 * half])
    qkv_ref[:, 2 * half :] = dot(low, w_ref[:, 2 * half : 3 * half]).astype(BF)
    qkv_ref[:, half : 2 * half] = turn(keys, cosine, sine).astype(BF)

    @pl.when(step < 2)
    def _():
        queries = dot(low, w_ref[:, :half])
        qkv_ref[:, :half] = turn(queries, cosine, sine).astype(BF)


def block_masks(info):
    noisy, block_len = info[1], info[2]
    keys = lax.broadcasted_iota(jnp.int32, (BLOCK, 2 * BLOCK), 0)
    queries = lax.broadcasted_iota(jnp.int32, (BLOCK, 2 * BLOCK), 1) % BLOCK
    starts = queries & (-block_len)
    clean_ok = keys < starts + jnp.where(noisy == 1, 0, block_len)
    local_ok = jnp.logical_and((keys & (-block_len)) == starts, noisy == 1)
    return clean_ok, local_ok


def by_head(values):
    wide = values.astype(F32)
    first = lax.broadcasted_iota(jnp.int32, wide.shape, 1) < HEAD_DIM
    return jnp.concatenate([jnp.where(first, wide, 0.0), jnp.where(first, 0.0, wide)], 0).astype(BF)


def head_quadrants(mixed):
    return jnp.concatenate([mixed[:HEAD_DIM, :BLOCK], mixed[HEAD_DIM : 2 * HEAD_DIM, BLOCK:]], 0)


def block_scores(queries, clean_keys, own_keys, at, masks):
    size = at + BLOCK
    scores = dot_nt(clean_keys[:size, :], queries)
    own = dot_nt(own_keys[at:size, :], queries)
    parts = [scores[:at]] if at else []
    parts.append(jnp.where(masks[0], scores[at:], MASKED))
    parts.append(jnp.where(masks[1], own, MASKED))
    return parts


def attend_kernel(info, q_ref, k_ref, v_ref, kc_ref, vc_ref, ot_ref, lse_ref):
    masks = block_masks(info)
    length = q_ref.shape[0]
    ones = jnp.ones((16, length), BF)
    own_vt = jnp.concatenate([transposed(v_ref[...]), ones], 0)
    clean_vt = jnp.concatenate([transposed(vc_ref[...]), ones], 0)

    def scores(at):
        queries = by_head(q_ref[at : at + BLOCK, :] * BF(HEAD_DIM**-0.5))
        return block_scores(queries, kc_ref, k_ref, at, masks)

    ready = scores(0)
    for at in range(0, length, BLOCK):
        parts = ready
        if at + BLOCK < length:
            ready = scores(at + BLOCK)
        size = at + BLOCK
        largest = functools.reduce(jnp.maximum, [jnp.max(part, 0, keepdims=True) for part in parts])
        weights = [jnp.exp(part - largest).astype(BF) for part in parts]
        mixed = dot(own_vt[:, at:size], weights[-1]) + dot(clean_vt[:, at:size], weights[-2])
        if at:
            mixed += dot(clean_vt[:, :at], weights[0])
        total = mixed[128:129]
        ot_ref[:, at:size] = head_quadrants(mixed / total).astype(BF)
        block = at // BLOCK
        lse_ref[block : block + 1, :] = largest + jnp.log(total)


def out_kernel(info, x_ref, ot_own, ot_oth, wo_own, wo_oth, r1_ref, a2_ref, ot_all):
    core = info[0]
    rows, width = x_ref.shape
    half = width // 2
    mine = pl.ds(pl.multiple_of(core * half, 128), half)
    theirs = pl.ds(pl.multiple_of((1 - core) * half, 128), half)
    at_rows = pl.ds(pl.multiple_of(core * rows, 128), rows)
    ot_all[mine, :] = ot_own[:, at_rows]
    ot_all[theirs, :] = ot_oth[:, at_rows]
    merged = transposed(ot_all[...])
    r1_ref[:, mine] = dot(merged, wo_own[...])
    r1_ref[:, theirs] = dot(merged, wo_oth[...])
    for at in range(0, rows, TILE):
        r1 = x_ref[at : at + TILE, :].astype(F32) + r1_ref[at : at + TILE, :]
        r1_ref[at : at + TILE, :] = r1
        a2_ref[at : at + TILE, :] = normalize(r1)[0].astype(BF)


def gelu_parts(u):
    c = math.sqrt(2.0 / math.pi)
    square = u * u
    half = 0.5 + 0.5 * jnp.tanh(u * (c + (0.044715 * c) * square))
    active = u * half
    slope = half + active * (1.0 - half) * (2.0 * c + (6.0 * 0.044715 * c) * square)
    return active, slope


def up_kernel(
    info, a2_own, a2_oth, dy_own, dy_oth, w0, w1, g_out, slope_out, d0, d1,
    a2_ref, dy_ref, w_ref, g_ref, slope_ref, dw_ref, sems, w_sems, g_sems,
):
    rows = a2_own.shape[0]
    hidden = w_ref.shape[1]
    a2_in = fetch([(a2_own, a2_ref.at[pl.ds(0, rows)]), (a2_oth, a2_ref.at[pl.ds(rows, rows)])], sems)
    w_in = start(chunk_copies((w0, w1), w_ref, w_sems, info, False))
    dy_in = fetch(
        [(dy_own, dy_ref.at[pl.ds(0, rows)]), (dy_oth, dy_ref.at[pl.ds(rows, rows)])], sems.at[pl.ds(2, 2)]
    )
    wait(a2_in + w_in)
    ready = dot(a2_ref[...], w_ref[:, :TILE])
    out = []
    for col in range(0, hidden, TILE):
        u = ready
        if col + TILE < hidden:
            ready = dot(a2_ref[...], w_ref[:, col + TILE : col + 2 * TILE])
        span = slice(col, col + TILE)
        active, slope = gelu_parts(u)
        g_ref[:, span] = active.astype(BF)
        slope_ref[:, span] = slope.astype(BF)
        at = pl.ds(col, TILE)
        pairs = [(g_ref.at[:, at], g_out.at[:, at]), (slope_ref.at[:, at], slope_out.at[:, at])]
        out += fetch(pairs, g_sems.at[pl.ds(2 * (col // TILE), 2)])
        if col == 0:
            wait(dy_in)
        dw_ref[span, :] = dot_tn(g_ref[:, span], dy_ref[...]).astype(BF)
    wait(out + start(chunk_copies((d0, d1), dw_ref, w_sems, info, True)))


def down_kernel(
    info, a2_own, a2_oth, slope_in, dy_own, dy_oth, u0, u1, w0, w1, e_ref, send_ref, d0, d1,
    a2_ref, dy_ref, slope_ref, up_ref, w_ref, du_ref, dw_ref, sems, w_sems, u_sems,
):
    rows = a2_own.shape[0]
    hidden = w_ref.shape[0]
    low, high = pl.ds(0, rows), pl.ds(rows, rows)
    dy_in = fetch([(dy_own, dy_ref.at[low]), (dy_oth, dy_ref.at[high])], sems)
    w_in = start(chunk_copies((w0, w1), w_ref, w_sems, info, False))
    slope_copy = fetch([(slope_in, slope_ref)], sems.at[pl.ds(2, 1)])
    a2_in = fetch([(a2_own, a2_ref.at[low]), (a2_oth, a2_ref.at[high])], sems.at[pl.ds(3, 2)])
    u_in = start(chunk_copies((u0, u1), up_ref, u_sems, info, False))
    wait(dy_in + w_in)
    ready = dot_nt(dy_ref[...], w_ref[:TILE, :])
    for col in range(0, hidden, TILE):
        grad = ready
        if col + TILE < hidden:
            ready = dot_nt(dy_ref[...], w_ref[col + TILE : col + 2 * TILE, :])
        if col == 0:
            wait(slope_copy + a2_in)
        span = slice(col, col + TILE)
        du_ref[:, span] = (grad * slope_ref[:, span].astype(F32)).astype(BF)
        dw_ref[:, span] = dot_tn(a2_ref[...], du_ref[:, span]).astype(BF)
    out = start(chunk_copies((d0, d1), dw_ref, w_sems, info, True))
    wait(u_in)
    send_ref[...] = dot_nt(du_ref[rows:, :], up_ref[...]).astype(BF)
    e_ref[...] = dot_nt(du_ref[:rows, :], up_ref[...])
    wait(out)


def mix_kernel(info, g_in, w0, w1, y_ref, send_ref, g_ref, w_ref, sems, w_sems):
    rows = y_ref.shape[0]
    w_in = start(chunk_copies((w0, w1), w_ref, w_sems, info, False))
    wait(fetch([(g_in, g_ref)], sems) + w_in)
    send_ref[...] = dot(g_ref[rows:, :], w_ref[...]).astype(BF)
    y_ref[...] = dot(g_ref[:rows, :], w_ref[...])


def mlp_back_kernel(r1_ref, e_ref, recv_ref, dy_ref, dr1_ref, dr_ref):
    normed, inverse = normalize(r1_ref[...])
    scaled = e_ref[...] + recv_ref[...].astype(F32)
    dr1 = dy_ref[...].astype(F32) + norm_back(scaled, normed, inverse)
    dr1_ref[...] = dr1
    dr_ref[...] = dr1.astype(BF)


def out_back_kernel(info, dr_own, dr_oth, wo_own, wo_oth, ot_own, ot_oth, do_ref, dwo_ref, dr_all, ot_all):
    core = info[0]
    rows, width = dr_own.shape
    half = width // 2
    mine = pl.ds(pl.multiple_of(core * half, 128), half)
    theirs = pl.ds(pl.multiple_of((1 - core) * half, 128), half)
    dr_all[pl.ds(pl.multiple_of(core * rows, 128), rows), :] = dr_own[...]
    dr_all[pl.ds(pl.multiple_of((1 - core) * rows, 128), rows), :] = dr_oth[...]
    ot_all[mine, :] = ot_own[...]
    ot_all[theirs, :] = ot_oth[...]
    grad = dot_nt(dr_all[:, mine], wo_own[mine, :])
    grad += dot_nt(dr_all[:, theirs], wo_oth[mine, :])
    do_ref[...] = grad.astype(BF)
    dwo_ref[...] = dot(ot_all[...], dr_all[:, mine]).astype(BF)


def attend_back_kernel(
    info, q_ref, k_ref, v_ref, kc_ref, vc_ref, do_ref, ot_ref, lse_ref, cos_ref, sin_ref,
    dq_ref, dk_ref, dv_ref, dkc_ref, dvc_ref, dk_sum, dv_sum,
):
    masks = block_masks(info)
    length = q_ref.shape[0]
    dk_sum[...] = jnp.zeros_like(dk_sum)
    dv_sum[...] = jnp.zeros_like(dv_sum)
    scale = BF(HEAD_DIM**-0.5)
    own_kt = transposed(k_ref[...] * scale)
    clean_kt = transposed(kc_ref[...] * scale)

    def first_part(at):
        size = at + BLOCK
        queries = by_head(q_ref[at:size, :] * scale)
        grads = by_head(do_ref[at:size, :])
        parts = block_scores(queries, kc_ref, k_ref, at, masks)
        clean_dp = dot_nt(vc_ref[:size, :], grads)
        slopes = [clean_dp[:at]] if at else []
        slopes += [clean_dp[at:], dot_nt(v_ref[at:size, :], grads)]
        return queries, grads, parts, slopes

    ready = first_part(0)
    for at in range(0, length, BLOCK):
        queries, grads, parts, slopes = ready
        size = at + BLOCK
        if size < length:
            ready = first_part(size)
        block = at // BLOCK
        lse = lse_ref[block : block + 1, :]
        products = do_ref[at:size, :].astype(F32).T * ot_ref[:, at:size].astype(F32)
        shared = jnp.concatenate(
            [
                jnp.sum(products[:HEAD_DIM], 0, keepdims=True),
                jnp.sum(products[HEAD_DIM:], 0, keepdims=True),
            ],
            1,
        )
        weights = [jnp.exp(part - lse) for part in parts]
        changes = [(w * (s - shared)).astype(BF) for w, s in zip(weights, slopes)]
        weights = [w.astype(BF) for w in weights]
        dq = dot(own_kt[:, at:size], changes[-1]) + dot(clean_kt[:, at:size], changes[-2])
        dk = dot(changes[-1], queries)
        dv_ref[at:size, :] = dot(weights[-1], grads).astype(BF)
        dk_sum[at:size, :] += dot(changes[-2], queries)
        dv_sum[at:size, :] += dot(weights[-2], grads)
        if at:
            dq += dot(clean_kt[:, :at], changes[0])
            dk_sum[:at, :] += dot(changes[0], queries)
            dv_sum[:at, :] += dot(weights[0], grads)
        cosine, sine = cos_ref[at:size, :], -sin_ref[at:size, :]
        dq_ref[at:size, :] = turn(head_quadrants(dq).T, cosine, sine).astype(BF)
        dk_ref[at:size, :] = turn(dk, cosine, sine).astype(BF)
    dkc_ref[...] = turn(dk_sum[...], cos_ref[...], -sin_ref[...]).astype(BF)
    dvc_ref[...] = dv_sum[...].astype(BF)


def qkv_weight_kernel(
    info, dq_ref, dk_ref, dv_ref, dkc_ref, dvc_ref, a1_ref, dwo_ref, d0, d1, dw_ref, sems
):
    length, half = dq_ref.shape
    own, clean = a1_ref.at[pl.ds(0, length)], a1_ref.at[pl.ds(length, length)]
    dw_ref[:, :half] = dot_tn(own[...], dq_ref[...]).astype(BF)
    for i, (a, b) in enumerate(((dk_ref, dkc_ref), (dv_ref, dvc_ref))):
        total = dot_tn(own[...], a[...]) + dot_tn(clean[...], b[...])
        dw_ref[:, (i + 1) * half : (i + 2) * half] = total.astype(BF)
    dw_ref[:, 3 * half :] = dwo_ref[...]
    wait(start(chunk_copies((d0, d1), dw_ref, sems, info, True)))


def qkv_back_kernel(
    info, dq_ref, dk_ref, dv_ref, dkc_ref, dvc_ref, w0, w1, own_ref, send_ref, clean_ref, w_ref, sems
):
    core, noisy = info[0], info[1]
    half = dq_ref.shape[1]
    rows = own_ref.shape[0]
    wait(start(chunk_copies((w0, w1), w_ref, sems, info, False)))
    clean_device = (noisy == 0).astype(F32)
    w_q, w_k, w_v = [w_ref.at[:, pl.ds(i * half, half)] for i in range(3)]
    for turn_of in range(2):
        at = (1 - core if turn_of == 0 else core) * rows
        span = pl.ds(pl.multiple_of(at, 128), rows)
        clean = dot_nt(dkc_ref[span, :], w_k[...]) + dot_nt(dvc_ref[span, :], w_v[...])
        own = dot_nt(dq_ref[span, :], w_q[...]) + dot_nt(dk_ref[span, :], w_k[...])
        own += dot_nt(dv_ref[span, :], w_v[...])
        own += clean * clean_device
        if turn_of == 0:
            send_ref[0] = own.astype(BF)
            send_ref[1] = clean.astype(BF)
        else:
            own_ref[...] = own
            clean_ref[...] = clean.astype(BF)


def input_back_kernel(x_ref, own_ref, recv_ref, clean_ref, dr1_ref, out_ref):
    for at in range(0, x_ref.shape[0], TILE):
        rows = slice(at, at + TILE)
        normed, inverse = normalize(x_ref[rows, :].astype(F32))
        scaled = own_ref[rows, :] + recv_ref[0, rows, :].astype(F32) + clean_ref[rows, :].astype(F32)
        out_ref[rows, :] = (dr1_ref[rows, :] + norm_back(scaled, normed, inverse)).astype(BF)


def core_swap(value):
    size = lax.axis_size("stream")
    return lax.ppermute(value, "stream", [(i, i ^ 1) for i in range(size)])


def z_swap(value, bits):
    size = lax.axis_size("batch")
    return lax.ppermute(value, "batch", [(i, i ^ (bits << 1)) for i in range(size)])


def cross_swap(value, y_core):
    batches, streams = lax.axis_size("batch"), lax.axis_size("stream")
    pairs = []
    for b in range(batches):
        for s in range(streams):
            peer = (b ^ 1, s) if s % 2 == y_core else (b, s ^ 2)
            pairs.append((b * streams + s, peer[0] * streams + peer[1]))
    return lax.ppermute(value, ALL, pairs)


def chip_groups():
    batches, streams = lax.axis_size("batch"), lax.axis_size("stream")
    return [
        [b * streams + 2 * x + c for b in range(batches) for x in range(streams // 2)]
        for c in range(2)
    ]


def gather(chunk, first):
    if 2 * lax.axis_size("batch") == CHUNKS:
        held = chunk[None]
        held = jnp.concatenate([held] + [z_swap(held, bits) for bits in (1, 2, 3)], 0)
        held = jnp.concatenate([held, cross_swap(held, 0)], 0)
        return [held, cross_swap(held, 1)]
    full = lax.all_gather(chunk, ALL, axis=0, tiled=True, axis_index_groups=chip_groups())
    full = full.reshape(CHUNKS, -1, full.shape[1])
    orders = [jnp.stack([full[chip_bits(p, c)] for p in range(CHUNKS)]) for c in range(2)]
    full = jnp.where(first, *orders)
    return [full[:8], full[8:]]


def scatter_sum(keep, send, first):
    if 2 * lax.axis_size("batch") == CHUNKS:
        total = keep.astype(F32) + cross_swap(send, 1).astype(F32)
        keep, send = total[:4].astype(BF), total[4:].astype(BF)
        total = keep.astype(F32) + cross_swap(send, 0).astype(F32)
        sends = total.astype(BF)
        arrived = [z_swap(sends[bits], bits) for bits in (1, 2, 3)]
        return total[0] + sum(part.astype(F32) for part in arrived)
    both = jnp.concatenate([keep, send], 0)
    order = [[chip_bits(p, c) for p in range(CHUNKS)] for c in range(2)]
    sorted_ = [jnp.stack([both[order[c].index(k)] for k in range(CHUNKS)]) for c in range(2)]
    full = jnp.where(first, *sorted_).astype(F32)
    full = full.reshape(-1, full.shape[2])
    return lax.psum_scatter(
        full, ALL, scatter_dimension=0, tiled=True, axis_index_groups=chip_groups()
    )


def local(tokens, cotangent, block_size, gain_attn, w_qkv, w_out, gain_mlp, w_up, w_down):
    rows, width = tokens.shape[1:]
    half = width // 2
    length = 2 * rows
    batches = lax.axis_size("batch")
    chips = 2 * batches
    hidden = w_up.shape[1] // 2
    stream, batch = lax.axis_index("stream"), lax.axis_index("batch")
    core, noisy = stream % 2, stream // 2
    me = batch * 2 + noisy if chips == CHUNKS else jnp.zeros_like(batch)
    info = jnp.stack([core, noisy, block_size[0], me]).astype(jnp.int32)
    first = core == 0
    n_rows = w_qkv.shape[0]

    def in_order(own, other, axis):
        return jnp.where(
            first, jnp.concatenate([own, other], axis), jnp.concatenate([other, own], axis)
        )

    def mine_theirs(zero, one):
        return jnp.where(first, zero, one), jnp.where(first, one, zero)

    gain_one = gain_attn.astype(BF).astype(F32)[:, None]
    gain_two = gain_mlp.astype(BF).astype(F32)[:, None]
    qkv_rows = w_qkv.astype(BF).astype(F32)
    up_rows = w_up.astype(BF).astype(F32)
    scaled = (qkv_rows * gain_one).astype(BF).reshape(n_rows, 3, 2, half)
    out_low = w_out.astype(BF)
    one = [
        jnp.concatenate([scaled[:, :, c].reshape(n_rows, -1), out_low[:, c * half : (c + 1) * half]], 1)
        for c in range(2)
    ]
    mine, theirs = mine_theirs(*one)
    chunk_one = in_order(mine, core_swap(theirs), 0)
    scaled = (up_rows * gain_two).astype(BF).reshape(n_rows, chips, 2, -1)
    mine, theirs = mine_theirs(*[scaled[:, :, c].reshape(n_rows, -1) for c in range(2)])
    chunk_two = in_order(mine, core_swap(theirs), 0)

    x_own = tokens[0]
    dy_own = cotangent[0]
    streams = lax.axis_size("stream")
    to_noisy = [(i, i + streams // 2) for i in range(streams // 2)]
    to_clean = [(b, a) for a, b in to_noisy]
    arrived = lax.ppermute(x_own, "stream", to_noisy)
    clean_own = jnp.where(noisy == 1, arrived, x_own)
    bufs_one = gather(chunk_one, first)
    x_oth = core_swap(x_own)
    clean_oth = core_swap(clean_own)
    dy_oth = core_swap(dy_own)
    bufs_two = gather(chunk_two, first)
    bufs_three = gather(w_down.astype(BF), first)

    a1 = pl.pallas_call(
        norm_kernel,
        in_specs=[SMEM] + [VMEM] * 4,
        out_specs=VMEM,
        out_shape=sds((4, rows, width), BF),
        compiler_params=params(20),
        cost_estimate=cost(4 * rows * width * 30, 6 << 20),
    )(info, x_own, x_oth, clean_own, clean_oth).reshape(2 * length, width)

    places = jnp.arange(length, dtype=jnp.int32)
    lanes = jnp.arange(128, dtype=jnp.int32)
    half_dim = HEAD_DIM // 2
    frequency = jnp.exp(-math.log(10000.0) * (lanes % half_dim).astype(F32) / half_dim)
    angles = places.astype(F32)[:, None] * frequency[None, :]
    cosine = jnp.cos(angles)
    sine = jnp.where((lanes % HEAD_DIM < half_dim)[None], -jnp.sin(angles), jnp.sin(angles))

    sem = pltpu.SemaphoreType.DMA
    qkv, wo_own = pl.pallas_call(
        qkv_kernel,
        grid=(4,),
        in_specs=[
            SMEM,
            pl.BlockSpec((rows, width), lambda i: (i, 0)),
            pl.BlockSpec((rows, 128), lambda i: (i % 2, 0)),
            pl.BlockSpec((rows, 128), lambda i: (i % 2, 0)),
        ]
        + [HBM] * 2,
        out_specs=[
            pl.BlockSpec((rows, 3 * half), lambda i: (i, 0)),
            pl.BlockSpec((width, half), lambda i: (0, 0)),
        ],
        out_shape=[sds((2 * length, 3 * half), BF), sds((width, half), BF)],
        scratch_shapes=[pltpu.VMEM((width, 4 * half), BF), sem((CHUNKS,))],
        compiler_params=params(32),
        cost_estimate=cost(2 * length * width * 2.5 * width, 12 << 20),
    )(info, a1, cosine, sine, *bufs_one)
    wo_oth = core_swap(wo_own)

    pairs = half // 128

    def pair_spec(part, clean):
        return pl.BlockSpec((length, 128), lambda p: (clean, part * pairs + p))

    qkv_specs = [pair_spec(0, 0), pair_spec(1, 0), pair_spec(2, 0), pair_spec(1, 1), pair_spec(2, 1)]
    attend_flops = 2 * 2 * length * length * half
    lse_spec = pl.BlockSpec((length // BLOCK, 2 * BLOCK), lambda p: (p, 0))
    ot_own, lse = pl.pallas_call(
        attend_kernel,
        grid=(pairs,),
        in_specs=[SMEM] + qkv_specs,
        out_specs=[pl.BlockSpec((128, length), lambda p: (p, 0)), lse_spec],
        out_shape=[sds((half, length), BF), sds((pairs * length // BLOCK, 2 * BLOCK), F32)],
        compiler_params=params(40),
        cost_estimate=cost(4 * attend_flops, 6 << 20, length * length * 6),
    )(info, qkv, qkv, qkv, qkv, qkv)
    ot_oth = core_swap(ot_own)

    r1, a2_own = pl.pallas_call(
        out_kernel,
        in_specs=[SMEM] + [VMEM] * 5,
        out_specs=[VMEM] * 2,
        out_shape=[sds((rows, width), F32), sds((rows, width), BF)],
        scratch_shapes=[pltpu.VMEM((width, rows), BF)],
        compiler_params=params(24),
        cost_estimate=cost(2 * rows * width * width, 6 << 20),
    )(info, x_own, ot_own, ot_oth, wo_own, wo_oth)
    a2_oth = core_swap(a2_own)

    down_bufs = [sds((8, 2 * width // CHUNKS, width), BF)] * 2
    up_bufs = [sds((8, width // CHUNKS, hidden), BF)] * 2
    g, slope, *down_parts = pl.pallas_call(
        up_kernel,
        in_specs=[SMEM] + [HBM] * 6,
        out_specs=[HBM] * 4,
        out_shape=[sds((length, hidden), BF), sds((length, hidden), BF)] + down_bufs,
        scratch_shapes=[
            pltpu.VMEM((length, width), BF),
            pltpu.VMEM((length, width), BF),
            pltpu.VMEM((width, hidden), BF),
            pltpu.VMEM((length, hidden), BF),
            pltpu.VMEM((length, hidden), BF),
            pltpu.VMEM((hidden, width), BF),
            sem((4,)),
            sem((CHUNKS,)),
            sem((2 * hidden // TILE,)),
        ],
        compiler_params=params(44),
        cost_estimate=cost(4 * length * width * hidden, 16 << 20, length * hidden),
    )(info, a2_own, a2_oth, dy_own, dy_oth, *bufs_two)

    e_own, e_send, *up_parts = pl.pallas_call(
        down_kernel,
        in_specs=[SMEM] + [HBM] * 9,
        out_specs=[VMEM] * 2 + [HBM] * 2,
        out_shape=[sds((rows, width), F32), sds((rows, width), BF)] + up_bufs,
        scratch_shapes=[
            pltpu.VMEM((length, width), BF),
            pltpu.VMEM((length, width), BF),
            pltpu.VMEM((length, hidden), BF),
            pltpu.VMEM((width, hidden), BF),
            pltpu.VMEM((hidden, width), BF),
            pltpu.VMEM((length, hidden), BF),
            pltpu.VMEM((width, hidden), BF),
            sem((5,)),
            sem((CHUNKS,)),
            sem((CHUNKS,)),
        ],
        compiler_params=params(44),
        cost_estimate=cost(6 * length * width * hidden, 20 << 20),
    )(info, a2_own, a2_oth, slope, dy_own, dy_oth, *bufs_two, *bufs_three)
    e_recv = core_swap(e_send)
    grad_down = scatter_sum(*down_parts, first)
    grad_up = scatter_sum(*up_parts, first)

    row_block = pl.BlockSpec((BLOCK, width), lambda i: (i, 0))
    dr1, dr_own = pl.pallas_call(
        mlp_back_kernel,
        grid=(rows // BLOCK,),
        in_specs=[row_block] * 4,
        out_specs=[row_block] * 2,
        out_shape=[sds((rows, width), F32), sds((rows, width), BF)],
        compiler_params=params(16),
        cost_estimate=cost(rows * width * 40, 8 << 20),
    )(r1, e_own, e_recv, dy_own)
    dr_oth = core_swap(dr_own)

    do, dwo = pl.pallas_call(
        out_back_kernel,
        in_specs=[SMEM] + [VMEM] * 6,
        out_specs=[VMEM] * 2,
        out_shape=[sds((length, half), BF), sds((width, half), BF)],
        scratch_shapes=[pltpu.VMEM((length, width), BF), pltpu.VMEM((width, length), BF)],
        compiler_params=params(24),
        cost_estimate=cost(4 * length * width * half, 6 << 20),
    )(info, dr_own, dr_oth, wo_own, wo_oth, ot_own, ot_oth)

    column = pl.BlockSpec((length, 128), lambda p: (0, p))
    whole = pl.BlockSpec((length, 128), lambda p: (0, 0))
    grads = pl.pallas_call(
        attend_back_kernel,
        grid=(pairs,),
        in_specs=[SMEM]
        + qkv_specs
        + [column, pl.BlockSpec((128, length), lambda p: (p, 0)), lse_spec, whole, whole],
        out_specs=[column] * 5,
        out_shape=[sds((length, half), BF)] * 5,
        scratch_shapes=[pltpu.VMEM((length, 128), F32)] * 2,
        compiler_params=params(48),
        cost_estimate=cost(10 * attend_flops, 10 << 20, length * length * 6),
    )(info, qkv, qkv, qkv, qkv, qkv, do, ot_own, lse, cosine, sine)

    one_parts = pl.pallas_call(
        qkv_weight_kernel,
        in_specs=[SMEM] + [VMEM] * 7,
        out_specs=[HBM] * 2,
        out_shape=up_bufs,
        scratch_shapes=[pltpu.VMEM((width, 4 * half), BF), sem((CHUNKS,))],
        compiler_params=params(32),
        cost_estimate=cost(10 * length * width * half, 12 << 20),
    )(info, *grads, a1, dwo)
    grad_one = scatter_sum(*one_parts, first)

    own_part, own_send, clean_part = pl.pallas_call(
        qkv_back_kernel,
        in_specs=[SMEM] + [VMEM] * 5 + [HBM] * 2,
        out_specs=[VMEM] * 3,
        out_shape=[sds((rows, width), F32), sds((2, rows, width), BF), sds((rows, width), BF)],
        scratch_shapes=[pltpu.VMEM((width, 4 * half), BF), sem((CHUNKS,))],
        compiler_params=params(32),
        cost_estimate=cost(10 * length * width * half, 12 << 20),
    )(info, *grads, *bufs_one)
    swapped = core_swap(own_send)
    clean_total = (clean_part.astype(F32) + swapped[1].astype(F32)).astype(BF)
    clean_back = lax.ppermute(clean_total, "stream", to_clean)

    y_own, y_send = pl.pallas_call(
        mix_kernel,
        in_specs=[SMEM] + [HBM] * 3,
        out_specs=[VMEM] * 2,
        out_shape=[sds((rows, width), F32), sds((rows, width), BF)],
        scratch_shapes=[
            pltpu.VMEM((length, hidden), BF),
            pltpu.VMEM((hidden, width), BF),
            sem((1,)),
            sem((CHUNKS,)),
        ],
        compiler_params=params(24),
        cost_estimate=cost(2 * length * width * hidden, 10 << 20),
    )(info, g, *bufs_three)
    output = (r1 + y_own + core_swap(y_send).astype(F32)).astype(BF)

    input_grad = pl.pallas_call(
        input_back_kernel,
        in_specs=[VMEM] * 5,
        out_specs=VMEM,
        out_shape=sds((rows, width), BF),
        compiler_params=params(16),
        cost_estimate=cost(rows * width * 40, 8 << 20),
    )(x_own, own_part, swapped, clean_back, dr1)

    def finish(total):
        keep, send = mine_theirs(total[:n_rows], total[n_rows:])
        return mine_theirs(keep, core_swap(send))

    ordered = finish(grad_one)
    sums_qkv = jnp.stack([v[:, : 3 * half].reshape(n_rows, 3, half) for v in ordered], 2)
    sums_qkv = sums_qkv.reshape(n_rows, 3 * width)
    grad_out = jnp.concatenate([v[:, 3 * half :] for v in ordered], 1)
    sums_up = jnp.stack([v.reshape(n_rows, chips, -1) for v in finish(grad_up)], 2)
    sums_up = sums_up.reshape(n_rows, 2 * hidden)
    return (
        output[None],
        input_grad[None],
        jnp.sum(sums_qkv * qkv_rows, 1),
        sums_qkv * gain_one,
        grad_out,
        jnp.sum(sums_up * up_rows, 1),
        sums_up * gain_two,
        grad_down,
    )


def solution(mesh):
    rows = P("batch", "stream", None)
    flat, split = P(ALL), P(ALL, None)
    return jax.shard_map(
        local,
        mesh=mesh,
        in_specs=(rows, rows, P("batch"), flat, split, split, flat, split, split),
        out_specs=(rows, rows, flat, split, split, flat, split, split),
        check_vma=False,
    )
```

```python
import functools
import math

import jax
import jax.numpy as jnp
from jax import lax
from jax.experimental import pallas as pl
from jax.experimental.pallas import tpu as pltpu
from jax.sharding import PartitionSpec as P

HEAD_DIM = 64
EPSILON = 1e-05
MASKED = -1e30
BF = jnp.bfloat16
F32 = jnp.float32
ALL = ("batch", "stream")
CHUNKS = 16
WIDE = 768
BLOCK = 128
TILE = 256
VMEM = pl.BlockSpec(memory_space=pltpu.VMEM)
SMEM = pl.BlockSpec(memory_space=pltpu.SMEM)
HBM = pl.BlockSpec(memory_space=pl.ANY)


def chip_bits(position, core):
    last = ((position >> 2) & 1) * (2 - core) ^ ((position >> 3) & 1) * (1 + core)
    return (position & 3) << 2 ^ last


def dot(a, b):
    return jnp.dot(a, b, preferred_element_type=F32)


def dot_nt(a, b):
    return lax.dot_general(a, b, (((1,), (1,)), ((), ())), preferred_element_type=F32)


def dot_tn(a, b):
    return lax.dot_general(a, b, (((0,), (0,)), ((), ())), preferred_element_type=F32)


def transposed(a):
    return a.astype(F32).T.astype(a.dtype)


def params(mib):
    return pltpu.CompilerParams(vmem_limit_bytes=mib << 20)


def cost(us):
    return pl.CostEstimate(flops=int(us * 1e9), bytes_accessed=1, transcendentals=0)


def sds(shape, dtype):
    return jax.ShapeDtypeStruct(shape, dtype)


TOKEN = sds((8, 128), F32)


def tied_call(
    kernel, inputs, ties=(), token=False, in_specs=None, out_specs=None, out_shape=None, **options
):
    n_in, n_ties = len(inputs), len(ties)
    n_out = len(out_shape)

    def body(*refs):
        rest = refs[n_in + n_ties :]
        if token:
            rest[n_out][...] = jnp.zeros(TOKEN.shape, F32)
            rest = rest[:n_out] + rest[n_out + 1 :]
        kernel(*refs[:n_in], *rest)

    if "grid" in options:
        small = pl.BlockSpec(TOKEN.shape, lambda *_: (0, 0))
    else:
        small = VMEM
    inputs = [
        pltpu.with_memory_space_constraint(value, pltpu.HBM) if spec is HBM else value
        for value, spec in zip(inputs, in_specs)
    ]
    out_shape = [
        pltpu.HBM(shape.shape, shape.dtype) if spec is HBM else shape
        for shape, spec in zip(out_shape, out_specs)
    ]
    call = pl.pallas_call(
        body,
        in_specs=list(in_specs) + [small] * n_ties,
        out_specs=list(out_specs) + [small] * token,
        out_shape=list(out_shape) + [TOKEN] * token,
        **options,
    )
    return call(*inputs, *ties)


def chunk_copies(bufs, ref, sems, info, store):
    rows = ref.shape[0] // CHUNKS
    copies = []
    for position in range(CHUNKS):
        chip = info[3] ^ chip_bits(position, info[0])
        buf = bufs[position // 8].at[position % 8]
        view = ref.at[pl.ds(pl.multiple_of(chip * rows, 16), rows), :]
        pair = (view, buf) if store else (buf, view)
        copies.append(pltpu.make_async_copy(*pair, sems.at[position]))
    return copies


def start(copies):
    for copy in copies:
        copy.start()
    return copies


def wait(copies):
    for copy in copies:
        copy.wait()


def fetch(pairs, sems):
    return start([pltpu.make_async_copy(a, b, sems.at[i]) for i, (a, b) in enumerate(pairs)])


def normalize(values):
    centred = values - jnp.mean(values, -1, keepdims=True)
    inverse = lax.rsqrt(jnp.mean(centred * centred, -1, keepdims=True) + EPSILON)
    return centred * inverse, inverse


def norm_back(scaled, normed, inverse):
    return inverse * (
        scaled
        - jnp.mean(scaled, -1, keepdims=True)
        - normed * jnp.mean(scaled * normed, -1, keepdims=True)
    )


def swap_halves(values):
    lanes = lax.broadcasted_iota(jnp.int32, values.shape, 1)
    return jnp.where(
        lanes % HEAD_DIM < HEAD_DIM // 2,
        pltpu.roll(values, 128 - HEAD_DIM // 2, 1),
        pltpu.roll(values, HEAD_DIM // 2, 1),
    )


def turn(values, cosine, sine):
    return jnp.concatenate(
        [
            values[:, at : at + 128] * cosine + swap_halves(values[:, at : at + 128]) * sine
            for at in range(0, values.shape[1], 128)
        ],
        1,
    )


def norm_kernel(info, x_own, x_oth, clean_own, clean_oth, a1_ref):
    core = info[0]
    rows = x_own.shape[0]
    for i, ref in enumerate((x_own, x_oth, clean_own, clean_oth)):
        slot = 2 * (i // 2) + (core if i % 2 == 0 else 1 - core)
        for at in range(0, rows, TILE):
            normed, _ = normalize(ref[at : at + TILE, :].astype(F32))
            a1_ref[slot, at : at + TILE, :] = normed.astype(BF)


def qkv_kernel(info, a1_ref, cos_ref, sin_ref, w0, w1, qkv_ref, wout_ref, w_ref, sems):
    half = a1_ref.shape[1] // 2
    step = pl.program_id(0)

    @pl.when(step == 0)
    def _():
        wait(start(chunk_copies((w0, w1), w_ref, sems, info, False)))
        wout_ref[...] = w_ref[:, 3 * half :]

    low = a1_ref[...]
    cosine, sine = cos_ref[...], sin_ref[...]
    keys = dot(low, w_ref[:, half : 2 * half])
    qkv_ref[:, 2 * half :] = dot(low, w_ref[:, 2 * half : 3 * half]).astype(BF)
    qkv_ref[:, half : 2 * half] = turn(keys, cosine, sine).astype(BF)

    @pl.when(step < 2)
    def _():
        queries = dot(low, w_ref[:, :half])
        qkv_ref[:, :half] = turn(queries, cosine, sine).astype(BF)


def block_masks(info):
    noisy, block_len = info[1], info[2]
    keys = lax.broadcasted_iota(jnp.int32, (BLOCK, 2 * BLOCK), 0)
    queries = lax.broadcasted_iota(jnp.int32, (BLOCK, 2 * BLOCK), 1) % BLOCK
    starts = queries & (-block_len)
    clean_ok = keys < starts + jnp.where(noisy == 1, 0, block_len)
    local_ok = jnp.logical_and((keys & (-block_len)) == starts, noisy == 1)
    return clean_ok, local_ok


def by_head(values):
    wide = values.astype(F32)
    first = lax.broadcasted_iota(jnp.int32, wide.shape, 1) < HEAD_DIM
    return jnp.concatenate([jnp.where(first, wide, 0.0), jnp.where(first, 0.0, wide)], 0).astype(BF)


def head_quadrants(mixed):
    return jnp.concatenate([mixed[:HEAD_DIM, :BLOCK], mixed[HEAD_DIM : 2 * HEAD_DIM, BLOCK:]], 0)


def block_scores(queries, clean_keys, own_keys, at, masks):
    size = at + BLOCK
    scores = dot_nt(clean_keys[:size, :], queries)
    own = dot_nt(own_keys[at:size, :], queries)
    parts = [scores[:at]] if at else []
    parts.append(jnp.where(masks[0], scores[at:], MASKED))
    parts.append(jnp.where(masks[1], own, MASKED))
    return parts


def attend_kernel(info, q_ref, k_ref, v_ref, kc_ref, vc_ref, ot_ref, lse_ref):
    masks = block_masks(info)
    length = q_ref.shape[0]
    ones = jnp.ones((16, length), BF)
    own_vt = jnp.concatenate([transposed(v_ref[...]), ones], 0)
    clean_vt = jnp.concatenate([transposed(vc_ref[...]), ones], 0)

    def scores(at):
        queries = by_head(q_ref[at : at + BLOCK, :] * BF(HEAD_DIM**-0.5))
        return block_scores(queries, kc_ref, k_ref, at, masks)

    ready = scores(0)
    for at in range(0, length, BLOCK):
        parts = ready
        if at + BLOCK < length:
            ready = scores(at + BLOCK)
        size = at + BLOCK
        largest = functools.reduce(jnp.maximum, [jnp.max(part, 0, keepdims=True) for part in parts])
        weights = [jnp.exp(part - largest).astype(BF) for part in parts]
        mixed = dot(own_vt[:, at:size], weights[-1]) + dot(clean_vt[:, at:size], weights[-2])
        if at:
            mixed += dot(clean_vt[:, :at], weights[0])
        total = mixed[128:129]
        ot_ref[:, at:size] = head_quadrants(mixed / total).astype(BF)
        block = at // BLOCK
        lse_ref[block : block + 1, :] = largest + jnp.log(total)


def out_kernel(info, x_ref, ot_own, ot_oth, wo_own, wo_oth, r1_ref, a2_ref, ot_all):
    core = info[0]
    rows, width = x_ref.shape
    half = width // 2
    mine = pl.ds(pl.multiple_of(core * half, 128), half)
    theirs = pl.ds(pl.multiple_of((1 - core) * half, 128), half)
    at_rows = pl.ds(pl.multiple_of(core * rows, 128), rows)
    ot_all[mine, :] = ot_own[:, at_rows]
    ot_all[theirs, :] = ot_oth[:, at_rows]
    merged = transposed(ot_all[...])
    r1_ref[:, mine] = dot(merged, wo_own[...])
    r1_ref[:, theirs] = dot(merged, wo_oth[...])
    for at in range(0, rows, TILE):
        r1 = x_ref[at : at + TILE, :].astype(F32) + r1_ref[at : at + TILE, :]
        r1_ref[at : at + TILE, :] = r1
        a2_ref[at : at + TILE, :] = normalize(r1)[0].astype(BF)


def gelu_parts(u):
    c = math.sqrt(2.0 / math.pi)
    square = u * u
    half = 0.5 + 0.5 * jnp.tanh(u * (c + (0.044715 * c) * square))
    active = u * half
    slope = half + active * (1.0 - half) * (2.0 * c + (6.0 * 0.044715 * c) * square)
    return active, slope


def up_kernel(
    info, a2_own, a2_oth, dy_own, dy_oth, w0, w1, g_out, slope_out, d0, d1,
    a2_ref, dy_ref, w_ref, g_ref, slope_ref, dw_ref, sems, w_sems, g_sems,
):
    rows = a2_own.shape[0]
    hidden = w_ref.shape[1]
    a2_in = fetch([(a2_own, a2_ref.at[pl.ds(0, rows)]), (a2_oth, a2_ref.at[pl.ds(rows, rows)])], sems)
    w_in = start(chunk_copies((w0, w1), w_ref, w_sems, info, False))
    dy_in = fetch(
        [(dy_own, dy_ref.at[pl.ds(0, rows)]), (dy_oth, dy_ref.at[pl.ds(rows, rows)])], sems.at[pl.ds(2, 2)]
    )
    wait(a2_in + w_in)
    ready = dot(a2_ref[...], w_ref[:, :TILE])
    out = []
    for col in range(0, hidden, TILE):
        u = ready
        if col + TILE < hidden:
            ready = dot(a2_ref[...], w_ref[:, col + TILE : col + 2 * TILE])
        span = slice(col, col + TILE)
        active, slope = gelu_parts(u)
        g_ref[:, span] = active.astype(BF)
        slope_ref[:, span] = slope.astype(BF)
        at = pl.ds(col, TILE)
        pairs = [(g_ref.at[:, at], g_out.at[:, at]), (slope_ref.at[:, at], slope_out.at[:, at])]
        out += fetch(pairs, g_sems.at[pl.ds(2 * (col // TILE), 2)])
        if col == 0:
            wait(dy_in)
        dw_ref[span, :] = dot_tn(g_ref[:, span], dy_ref[...]).astype(BF)
    wait(out + start(chunk_copies((d0, d1), dw_ref, w_sems, info, True)))


def down_kernel(
    info, a2_own, a2_oth, slope_in, dy_own, dy_oth, u0, u1, w0, w1, e_ref, send_ref, d0, d1,
    a2_ref, dy_ref, slope_ref, up_ref, w_ref, du_ref, dw_ref, sems, w_sems, u_sems,
):
    rows = a2_own.shape[0]
    hidden = w_ref.shape[0]
    low, high = pl.ds(0, rows), pl.ds(rows, rows)
    dy_in = fetch([(dy_own, dy_ref.at[low]), (dy_oth, dy_ref.at[high])], sems)
    w_in = start(chunk_copies((w0, w1), w_ref, w_sems, info, False))
    slope_copy = fetch([(slope_in, slope_ref)], sems.at[pl.ds(2, 1)])
    a2_in = fetch([(a2_own, a2_ref.at[low]), (a2_oth, a2_ref.at[high])], sems.at[pl.ds(3, 2)])
    u_in = start(chunk_copies((u0, u1), up_ref, u_sems, info, False))
    wait(dy_in + w_in)
    ready = dot_nt(dy_ref[...], w_ref[:TILE, :])
    for col in range(0, hidden, TILE):
        grad = ready
        if col + TILE < hidden:
            ready = dot_nt(dy_ref[...], w_ref[col + TILE : col + 2 * TILE, :])
        if col == 0:
            wait(slope_copy + a2_in)
        span = slice(col, col + TILE)
        du_ref[:, span] = (grad * slope_ref[:, span].astype(F32)).astype(BF)
        dw_ref[:, span] = dot_tn(a2_ref[...], du_ref[:, span]).astype(BF)
    out = start(chunk_copies((d0, d1), dw_ref, w_sems, info, True))
    wait(u_in)
    send_ref[...] = dot_nt(du_ref[rows:, :], up_ref[...]).astype(BF)
    e_ref[...] = dot_nt(du_ref[:rows, :], up_ref[...])
    wait(out)


def mix_kernel(info, g_in, w0, w1, y_ref, send_ref, g_ref, w_ref, sems, w_sems):
    rows = y_ref.shape[0]
    w_in = start(chunk_copies((w0, w1), w_ref, w_sems, info, False))
    wait(fetch([(g_in, g_ref)], sems) + w_in)
    send_ref[...] = dot(g_ref[rows:, :], w_ref[...]).astype(BF)
    y_ref[...] = dot(g_ref[:rows, :], w_ref[...])


def join_kernel(*refs):
    at = 0
    for ref in refs[:-1]:
        refs[-1][at : at + ref.shape[0]] = ref[...]
        at += ref.shape[0]


def halve_kernel(keep_ref, recv_ref, keep_out, send_out):
    count = keep_out.shape[0]
    for part in range(2):
        span = slice(part * count, (part + 1) * count)
        total = keep_ref[span].astype(F32) + recv_ref[span].astype(F32)
        (keep_out, send_out)[part][...] = total.astype(BF)


def spread_kernel(*refs):
    count = (len(refs) - 3) // 3
    totals, sends = refs[2 * count : 3 * count], refs[3 * count :]
    at = 0
    for i in range(count):
        keep_ref, recv_ref = refs[2 * i], refs[2 * i + 1]
        rows, columns = totals[i].shape
        for part in range(4):
            total = keep_ref[part].astype(F32) + recv_ref[part].astype(F32)
            if part == 0:
                totals[i][...] = total
                continue
            for j in range(columns // WIDE):
                low = at + j * rows
                sends[part - 1][low : low + rows, :] = total[:, j * WIDE : (j + 1) * WIDE].astype(BF)
        at += rows * columns // WIDE


def result_kernel(count, info, *refs):
    totals, arrived, outs = refs[:count], refs[count : count + 3], list(refs[count + 3 :])
    core = info[0]
    at = 0
    for i in range(count):
        rows, columns = totals[i].shape
        parts = []
        for j in range(columns // WIDE):
            low = at + j * rows
            part = totals[i][:, j * WIDE : (j + 1) * WIDE]
            for ref in arrived:
                part = part + ref[low : low + rows, :].astype(F32)
            parts.append(part)
        at += rows * columns // WIDE
        keep = outs.pop(0)
        if keep.shape[0] == rows:
            for j, part in enumerate(parts):
                keep[:, j * WIDE : (j + 1) * WIDE] = part
            continue
        send = outs.pop(0)
        half = rows // 2
        for j, part in enumerate(parts):
            span = slice(j * WIDE, (j + 1) * WIDE)
            keep[:, span] = jnp.where(core == 0, part[:half], part[half:])
            send[:, span] = jnp.where(core == 0, part[half:], part[:half])


def clean_kernel(own_ref, recv_ref, out_ref):
    out_ref[...] = (own_ref[...].astype(F32) + recv_ref[...].astype(F32)).astype(BF)


def mlp_back_kernel(r1_ref, e_ref, recv_ref, dy_ref, dr1_ref, dr_ref):
    normed, inverse = normalize(r1_ref[...])
    scaled = e_ref[...] + recv_ref[...].astype(F32)
    dr1 = dy_ref[...].astype(F32) + norm_back(scaled, normed, inverse)
    dr1_ref[...] = dr1
    dr_ref[...] = dr1.astype(BF)


def out_back_kernel(info, dr_own, dr_oth, wo_own, wo_oth, ot_own, ot_oth, do_ref, dwo_ref, dr_all, ot_all):
    core = info[0]
    rows, width = dr_own.shape
    half = width // 2
    mine = pl.ds(pl.multiple_of(core * half, 128), half)
    theirs = pl.ds(pl.multiple_of((1 - core) * half, 128), half)
    dr_all[pl.ds(pl.multiple_of(core * rows, 128), rows), :] = dr_own[...]
    dr_all[pl.ds(pl.multiple_of((1 - core) * rows, 128), rows), :] = dr_oth[...]
    ot_all[mine, :] = ot_own[...]
    ot_all[theirs, :] = ot_oth[...]
    grad = dot_nt(dr_all[:, mine], wo_own[mine, :])
    grad += dot_nt(dr_all[:, theirs], wo_oth[mine, :])
    do_ref[...] = grad.astype(BF)
    dwo_ref[...] = dot(ot_all[...], dr_all[:, mine]).astype(BF)


def attend_back_kernel(
    info, q_ref, k_ref, v_ref, kc_ref, vc_ref, do_ref, ot_ref, lse_ref, cos_ref, sin_ref,
    dq_ref, dk_ref, dv_ref, dkc_ref, dvc_ref, dk_sum, dv_sum,
):
    masks = block_masks(info)
    length = q_ref.shape[0]
    dk_sum[...] = jnp.zeros_like(dk_sum)
    dv_sum[...] = jnp.zeros_like(dv_sum)
    scale = BF(HEAD_DIM**-0.5)
    own_kt = transposed(k_ref[...] * scale)
    clean_kt = transposed(kc_ref[...] * scale)

    def first_part(at):
        size = at + BLOCK
        queries = by_head(q_ref[at:size, :] * scale)
        grads = by_head(do_ref[at:size, :])
        parts = block_scores(queries, kc_ref, k_ref, at, masks)
        clean_dp = dot_nt(vc_ref[:size, :], grads)
        slopes = [clean_dp[:at]] if at else []
        slopes += [clean_dp[at:], dot_nt(v_ref[at:size, :], grads)]
        return queries, grads, parts, slopes

    ready = first_part(0)
    for at in range(0, length, BLOCK):
        queries, grads, parts, slopes = ready
        size = at + BLOCK
        if size < length:
            ready = first_part(size)
        block = at // BLOCK
        lse = lse_ref[block : block + 1, :]
        products = do_ref[at:size, :].astype(F32).T * ot_ref[:, at:size].astype(F32)
        shared = jnp.concatenate(
            [
                jnp.sum(products[:HEAD_DIM], 0, keepdims=True),
                jnp.sum(products[HEAD_DIM:], 0, keepdims=True),
            ],
            1,
        )
        weights = [jnp.exp(part - lse) for part in parts]
        changes = [(w * (s - shared)).astype(BF) for w, s in zip(weights, slopes)]
        weights = [w.astype(BF) for w in weights]
        dq = dot(own_kt[:, at:size], changes[-1]) + dot(clean_kt[:, at:size], changes[-2])
        dk = dot(changes[-1], queries)
        dv_ref[at:size, :] = dot(weights[-1], grads).astype(BF)
        dk_sum[at:size, :] += dot(changes[-2], queries)
        dv_sum[at:size, :] += dot(weights[-2], grads)
        if at:
            dq += dot(clean_kt[:, :at], changes[0])
            dk_sum[:at, :] += dot(changes[0], queries)
            dv_sum[:at, :] += dot(weights[0], grads)
        cosine, sine = cos_ref[at:size, :], -sin_ref[at:size, :]
        dq_ref[at:size, :] = turn(head_quadrants(dq).T, cosine, sine).astype(BF)
        dk_ref[at:size, :] = turn(dk, cosine, sine).astype(BF)
    dkc_ref[...] = turn(dk_sum[...], cos_ref[...], -sin_ref[...]).astype(BF)
    dvc_ref[...] = dv_sum[...].astype(BF)


def qkv_weight_kernel(
    info, dq_ref, dk_ref, dv_ref, dkc_ref, dvc_ref, a1_ref, dwo_ref, d0, d1, dw_ref, sems
):
    length, half = dq_ref.shape
    own, clean = a1_ref.at[pl.ds(0, length)], a1_ref.at[pl.ds(length, length)]
    dw_ref[:, :half] = dot_tn(own[...], dq_ref[...]).astype(BF)
    for i, (a, b) in enumerate(((dk_ref, dkc_ref), (dv_ref, dvc_ref))):
        total = dot_tn(own[...], a[...]) + dot_tn(clean[...], b[...])
        dw_ref[:, (i + 1) * half : (i + 2) * half] = total.astype(BF)
    dw_ref[:, 3 * half :] = dwo_ref[...]
    wait(start(chunk_copies((d0, d1), dw_ref, sems, info, True)))


def clean_back_kernel(info, dkc_ref, dvc_ref, w0, w1, keep_ref, send_ref, w_ref, sems):
    core = info[0]
    half = dkc_ref.shape[1]
    rows = keep_ref.shape[0]
    wait(start(chunk_copies((w0, w1), w_ref, sems, info, False)))
    w_k, w_v = [w_ref.at[:, pl.ds(i * half, half)] for i in (1, 2)]
    for at, ref in (((1 - core) * rows, send_ref), (core * rows, keep_ref)):
        span = pl.ds(pl.multiple_of(at, 128), rows)
        clean = dot_nt(dkc_ref[span, :], w_k[...]) + dot_nt(dvc_ref[span, :], w_v[...])
        ref[...] = clean.astype(BF)


def qkv_back_kernel(
    info, dq_ref, dk_ref, dv_ref, w0, w1, own_ref, send_ref, w_ref, sems
):
    core = info[0]
    half = dq_ref.shape[1]
    rows = own_ref.shape[0]
    wait(start(chunk_copies((w0, w1), w_ref, sems, info, False)))
    w_q, w_k, w_v = [w_ref.at[:, pl.ds(i * half, half)] for i in range(3)]
    for at, ref in (((1 - core) * rows, send_ref), (core * rows, own_ref)):
        span = pl.ds(pl.multiple_of(at, 128), rows)
        own = dot_nt(dq_ref[span, :], w_q[...]) + dot_nt(dk_ref[span, :], w_k[...])
        own += dot_nt(dv_ref[span, :], w_v[...])
        ref[...] = own.astype(ref.dtype)


def input_back_kernel(info, x_ref, own_ref, recv_ref, clean_ref, arrived_ref, dr1_ref, out_ref):
    for at in range(0, x_ref.shape[0], TILE):
        rows = slice(at, at + TILE)
        normed, inverse = normalize(x_ref[rows, :].astype(F32))
        scaled = own_ref[rows, :] + recv_ref[rows, :].astype(F32)
        clean = clean_ref[rows, :].astype(F32) + arrived_ref[rows, :].astype(F32)
        scaled += jnp.where(info[1] == 0, clean, 0.0)
        out_ref[rows, :] = (dr1_ref[rows, :] + norm_back(scaled, normed, inverse)).astype(BF)


def core_swap(value):
    size = lax.axis_size("stream")
    return lax.ppermute(value, "stream", [(i, i ^ 1) for i in range(size)])


def z_swap(value, bits):
    size = lax.axis_size("batch")
    return lax.ppermute(value, "batch", [(i, i ^ (bits << 1)) for i in range(size)])


def cross_swap(value, y_core):
    batches, streams = lax.axis_size("batch"), lax.axis_size("stream")
    pairs = []
    for b in range(batches):
        for s in range(streams):
            peer = (b ^ 1, s) if s % 2 == y_core else (b, s ^ 2)
            pairs.append((b * streams + s, peer[0] * streams + peer[1]))
    return lax.ppermute(value, ALL, pairs)


def chip_groups():
    batches, streams = lax.axis_size("batch"), lax.axis_size("stream")
    return [
        [b * streams + 2 * x + c for b in range(batches) for x in range(streams // 2)]
        for c in range(2)
    ]


def join(parts, ties=()):
    shape = (sum(part.shape[0] for part in parts),) + parts[0].shape[1:]
    return tied_call(
        join_kernel,
        parts,
        ties,
        True,
        in_specs=[VMEM] * len(parts),
        out_specs=[VMEM],
        out_shape=[sds(shape, BF)],
        compiler_params=params(8),
        cost_estimate=cost(0.5),
    )


def is_fast():
    return 2 * lax.axis_size("batch") == CHUNKS


class Gather:
    def __init__(self, chunk, first, *ties):
        self.chunk, self.first, self.tokens = chunk, first, []
        if is_fast():
            held = chunk[None]
            if ties:
                held, token = join([held], ties)
                self.tokens = [token]
            self.parts = [held] + [z_swap(held, bits) for bits in (1, 2, 3)]

    def middle(self, *ties):
        if is_fast():
            self.held, token = join(self.parts, ties)
            self.received = cross_swap(self.held, 0)
            self.tokens = [token]
        return self.tokens

    def last(self, *ties):
        if is_fast():
            held, token = join([self.held, self.received], ties)
            self.tokens = [token]
            return [held, cross_swap(held, 1)]
        return slow_gather(self.chunk, self.first)


def slow_gather(chunk, first):
    full = lax.all_gather(chunk, ALL, axis=0, tiled=True, axis_index_groups=chip_groups())
    full = full.reshape(CHUNKS, -1, full.shape[1])
    orders = [jnp.stack([full[chip_bits(p, c)] for p in range(CHUNKS)]) for c in range(2)]
    full = jnp.where(first, *orders)
    return [full[:8], full[8:]]


def halve(keep, received, ties):
    count, rows, columns = keep.shape
    return tied_call(
        halve_kernel,
        [keep, received],
        ties,
        True,
        in_specs=[VMEM] * 2,
        out_specs=[VMEM] * 2,
        out_shape=[sds((count // 2, rows, columns), BF)] * 2,
        compiler_params=params(12),
        cost_estimate=cost(0.5),
    )


class ScatterSum:
    def __init__(self, keep, send, whole=False):
        self.keep, self.send, self.whole = keep, send, whole
        if is_fast():
            self.received = cross_swap(send, 1)

    def second(self, *ties):
        if not is_fast():
            return []
        self.keep, send, token = halve(self.keep, self.received, ties)
        self.received = cross_swap(send, 0)
        return [token]


def third(sums, ties):
    if not is_fast():
        return [], [], []
    shapes = [part.keep.shape[1:] for part in sums]
    rows = sum(rows * columns for rows, columns in shapes) // WIDE
    *out, token = tied_call(
        spread_kernel,
        [part for one in sums for part in (one.keep, one.received)],
        ties,
        True,
        in_specs=[VMEM] * (2 * len(sums)),
        out_specs=[VMEM] * (len(sums) + 3),
        out_shape=[sds(shape, F32) for shape in shapes] + [sds((rows, WIDE), BF)] * 3,
        compiler_params=params(16),
        cost_estimate=cost(0.5),
    )
    arrived = [z_swap(part, i + 1) for i, part in enumerate(out[len(sums) :])]
    return out[: len(sums)], arrived, [token]


def result(sums, totals, arrived, info, first, ties):
    if not is_fast():
        out = []
        for one in sums:
            total = slow_sum(one.keep, one.send, first)
            if one.whole:
                out.append(total)
            else:
                count = total.shape[0] // 2
                out.append(jnp.where(first, total[:count], total[count:]))
                out.append(jnp.where(first, total[count:], total[:count]))
        return out, []
    shapes = []
    for one, total in zip(sums, totals):
        rows, columns = total.shape
        shapes += [(rows, columns)] if one.whole else [(rows // 2, columns)] * 2
    *out, token = tied_call(
        functools.partial(result_kernel, len(sums)),
        [info, *totals, *arrived],
        ties,
        True,
        in_specs=[SMEM] + [VMEM] * (len(sums) + 3),
        out_specs=[VMEM] * len(shapes),
        out_shape=[sds(shape, F32) for shape in shapes],
        compiler_params=params(8),
        cost_estimate=cost(30),
    )
    return out, [token]


def slow_sum(keep, send, first):
    both = jnp.concatenate([keep, send], 0)
    orders = [[chip_bits(p, c) for p in range(CHUNKS)] for c in range(2)]
    sorted_ = [jnp.stack([both[orders[c].index(k)] for k in range(CHUNKS)]) for c in range(2)]
    full = jnp.where(first, *sorted_).astype(F32)
    full = full.reshape(-1, full.shape[2])
    return lax.psum_scatter(
        full, ALL, scatter_dimension=0, tiled=True, axis_index_groups=chip_groups()
    )


def local(tokens, cotangent, block_size, gain_attn, w_qkv, w_out, gain_mlp, w_up, w_down):
    rows, width = tokens.shape[1:]
    half = width // 2
    length = 2 * rows
    batches = lax.axis_size("batch")
    chips = 2 * batches
    hidden = w_up.shape[1] // 2
    stream, batch = lax.axis_index("stream"), lax.axis_index("batch")
    core, noisy = stream % 2, stream // 2
    me = batch * 2 + noisy if chips == CHUNKS else jnp.zeros_like(batch)
    info = jnp.stack([core, noisy, block_size[0], me]).astype(jnp.int32)
    first = core == 0
    n_rows = w_qkv.shape[0]

    def in_order(own, other, axis):
        return jnp.where(
            first, jnp.concatenate([own, other], axis), jnp.concatenate([other, own], axis)
        )

    def mine_theirs(zero, one):
        return jnp.where(first, zero, one), jnp.where(first, one, zero)

    gain_one = gain_attn.astype(BF).astype(F32)[:, None]
    gain_two = gain_mlp.astype(BF).astype(F32)[:, None]
    qkv_rows = w_qkv.astype(BF).astype(F32)
    up_rows = w_up.astype(BF).astype(F32)
    scaled = (qkv_rows * gain_one).astype(BF).reshape(n_rows, 3, 2, half)
    out_low = w_out.astype(BF)
    one = [
        jnp.concatenate([scaled[:, :, c].reshape(n_rows, -1), out_low[:, c * half : (c + 1) * half]], 1)
        for c in range(2)
    ]
    mine, theirs = mine_theirs(*one)
    chunk_one = in_order(mine, core_swap(theirs), 0)
    scaled = (up_rows * gain_two).astype(BF).reshape(n_rows, chips, 2, -1)
    mine, theirs = mine_theirs(*[scaled[:, :, c].reshape(n_rows, -1) for c in range(2)])
    chunk_two = in_order(mine, core_swap(theirs), 0)

    x_own = tokens[0]
    dy_own = cotangent[0]
    streams = lax.axis_size("stream")
    to_noisy = [(i, i + streams // 2) for i in range(streams // 2)]
    to_clean = [(b, a) for a, b in to_noisy]
    arrived = lax.ppermute(x_own, "stream", to_noisy)
    clean_own = jnp.where(noisy == 1, arrived, x_own)
    x_oth = core_swap(x_own)
    clean_oth = core_swap(clean_own)
    dy_oth = core_swap(dy_own)
    places = jnp.arange(length, dtype=jnp.int32)
    lanes = jnp.arange(128, dtype=jnp.int32)
    half_dim = HEAD_DIM // 2
    frequency = jnp.exp(-math.log(10000.0) * (lanes % half_dim).astype(F32) / half_dim)
    angles = places.astype(F32)[:, None] * frequency[None, :]
    cosine = jnp.cos(angles)
    sine = jnp.where((lanes % HEAD_DIM < half_dim)[None], -jnp.sin(angles), jnp.sin(angles))

    a1, norm_done = tied_call(
        norm_kernel,
        [info, x_own, x_oth, clean_own, clean_oth],
        (cosine[:8], sine[:8]),
        True,
        in_specs=[SMEM] + [VMEM] * 4,
        out_specs=[VMEM],
        out_shape=[sds((4, rows, width), BF)],
        compiler_params=params(20),
        cost_estimate=cost(3),
    )
    a1 = a1.reshape(2 * length, width)

    one = Gather(chunk_one, first)
    one.middle()
    bufs_one = one.last()
    two = Gather(chunk_two, first, *one.tokens)
    two_early = two.middle(norm_done)
    three = Gather(w_down.astype(BF), first, *two_early)
    three_start = three.tokens

    sem = pltpu.SemaphoreType.DMA
    qkv, wo_own, *qkv_done = tied_call(
        qkv_kernel,
        [info, a1, cosine, sine, *bufs_one],
        three_start,
        True,
        grid=(4,),
        in_specs=[
            SMEM,
            pl.BlockSpec((rows, width), lambda i: (i, 0)),
            pl.BlockSpec((rows, 128), lambda i: (i % 2, 0)),
            pl.BlockSpec((rows, 128), lambda i: (i % 2, 0)),
        ]
        + [HBM] * 2,
        out_specs=[
            pl.BlockSpec((rows, 3 * half), lambda i: (i, 0)),
            pl.BlockSpec((width, half), lambda i: (0, 0)),
        ],
        out_shape=[sds((2 * length, 3 * half), BF), sds((width, half), BF)],
        scratch_shapes=[pltpu.VMEM((width, 4 * half), BF), sem((CHUNKS,))],
        compiler_params=params(24),
        cost_estimate=cost(30),
    )
    wo_oth = core_swap(wo_own)
    bufs_two = two.last(*qkv_done)
    three_early = three.middle(*two.tokens)

    pairs = half // 128

    def pair_spec(part, clean):
        return pl.BlockSpec((length, 128), lambda p: (clean, part * pairs + p))

    qkv_specs = [pair_spec(0, 0), pair_spec(1, 0), pair_spec(2, 0), pair_spec(1, 1), pair_spec(2, 1)]
    attend_flops = 2 * 2 * length * length * half
    lse_spec = pl.BlockSpec((length // BLOCK, 2 * BLOCK), lambda p: (p, 0))
    ot_own, lse, *attend_done = tied_call(
        attend_kernel,
        [info, qkv, qkv, qkv, qkv, qkv],
        three_early,
        True,
        grid=(pairs,),
        in_specs=[SMEM] + qkv_specs,
        out_specs=[pl.BlockSpec((128, length), lambda p: (p, 0)), lse_spec],
        out_shape=[sds((half, length), BF), sds((pairs * length // BLOCK, 2 * BLOCK), F32)],
        compiler_params=params(28),
        cost_estimate=cost(30),
    )
    ot_oth = core_swap(ot_own)
    bufs_three = three.last(*attend_done)

    r1, a2_own = tied_call(
        out_kernel,
        [info, x_own, ot_own, ot_oth, wo_own, wo_oth],
        three.tokens,
        in_specs=[SMEM] + [VMEM] * 5,
        out_specs=[VMEM] * 2,
        out_shape=[sds((rows, width), F32), sds((rows, width), BF)],
        scratch_shapes=[pltpu.VMEM((width, rows), BF)],
        compiler_params=params(16),
        cost_estimate=cost(2),
    )
    a2_oth = core_swap(a2_own)

    down_bufs = [sds((8, 2 * width // CHUNKS, width), BF)] * 2
    up_bufs = [sds((8, width // CHUNKS, hidden), BF)] * 2
    g, slope, *down_parts = tied_call(
        up_kernel,
        [info, a2_own, a2_oth, dy_own, dy_oth, *bufs_two],
        in_specs=[SMEM] + [HBM] * 6,
        out_specs=[HBM] * 4,
        out_shape=[sds((length, hidden), BF), sds((length, hidden), BF)] + down_bufs,
        scratch_shapes=[
            pltpu.VMEM((length, width), BF),
            pltpu.VMEM((length, width), BF),
            pltpu.VMEM((width, hidden), BF),
            pltpu.VMEM((length, hidden), BF),
            pltpu.VMEM((length, hidden), BF),
            pltpu.VMEM((hidden, width), BF),
            sem((4,)),
            sem((CHUNKS,)),
            sem((2 * hidden // TILE,)),
        ],
        compiler_params=params(44),
        cost_estimate=cost(30),
    )
    sum_down = ScatterSum(*down_parts, whole=True)

    e_own, e_send, up_keep, up_send, *down_done = tied_call(
        down_kernel,
        [info, a2_own, a2_oth, slope, dy_own, dy_oth, *bufs_two, *bufs_three],
        (),
        True,
        in_specs=[SMEM] + [HBM] * 9,
        out_specs=[VMEM] * 2 + [HBM] * 2,
        out_shape=[sds((rows, width), F32), sds((rows, width), BF)] + up_bufs,
        scratch_shapes=[
            pltpu.VMEM((length, width), BF),
            pltpu.VMEM((length, width), BF),
            pltpu.VMEM((length, hidden), BF),
            pltpu.VMEM((width, hidden), BF),
            pltpu.VMEM((hidden, width), BF),
            pltpu.VMEM((length, hidden), BF),
            pltpu.VMEM((width, hidden), BF),
            sem((5,)),
            sem((CHUNKS,)),
            sem((CHUNKS,)),
        ],
        compiler_params=params(30),
        cost_estimate=cost(30),
    )
    e_recv = core_swap(e_send)
    sum_up = ScatterSum(up_keep, up_send)
    down_second = sum_down.second(*down_done)

    row_block = pl.BlockSpec((BLOCK, width), lambda i: (i, 0))
    dr1, dr_own = tied_call(
        mlp_back_kernel,
        [r1, e_own, e_recv, dy_own],
        down_second,
        grid=(rows // BLOCK,),
        in_specs=[row_block] * 4,
        out_specs=[row_block] * 2,
        out_shape=[sds((rows, width), F32), sds((rows, width), BF)],
        compiler_params=params(8),
        cost_estimate=cost(1),
    )
    dr_oth = core_swap(dr_own)

    do, dwo = tied_call(
        out_back_kernel,
        [info, dr_own, dr_oth, wo_own, wo_oth, ot_own, ot_oth],
        in_specs=[SMEM] + [VMEM] * 6,
        out_specs=[VMEM] * 2,
        out_shape=[sds((length, half), BF), sds((width, half), BF)],
        scratch_shapes=[pltpu.VMEM((length, width), BF), pltpu.VMEM((width, length), BF)],
        compiler_params=params(20),
        cost_estimate=cost(2),
    )

    column = pl.BlockSpec((length, 128), lambda p: (0, p))
    whole = pl.BlockSpec((length, 128), lambda p: (0, 0))
    *grads, attend_back_done = tied_call(
        attend_back_kernel,
        [info, qkv, qkv, qkv, qkv, qkv, do, ot_own, lse, cosine, sine],
        (),
        True,
        grid=(pairs,),
        in_specs=[SMEM]
        + qkv_specs
        + [column, pl.BlockSpec((128, length), lambda p: (p, 0)), lse_spec, whole, whole],
        out_specs=[column] * 5,
        out_shape=[sds((length, half), BF)] * 5,
        scratch_shapes=[pltpu.VMEM((length, 128), F32)] * 2,
        compiler_params=params(36),
        cost_estimate=cost(30),
    )
    up_second = sum_up.second(attend_back_done)

    *one_parts, weight_done = tied_call(
        qkv_weight_kernel,
        [info, *grads, a1, dwo],
        up_second,
        True,
        in_specs=[SMEM] + [VMEM] * 7,
        out_specs=[HBM] * 2,
        out_shape=up_bufs,
        scratch_shapes=[pltpu.VMEM((width, 4 * half), BF), sem((CHUNKS,))],
        compiler_params=params(24),
        cost_estimate=cost(30),
    )
    sum_one = ScatterSum(*one_parts)
    mlp_totals, mlp_arrived, mlp_third = third([sum_down, sum_up], (weight_done,))

    clean_part, clean_send = tied_call(
        clean_back_kernel,
        [info, *grads[3:], *bufs_one],
        mlp_third,
        in_specs=[SMEM] + [VMEM] * 2 + [HBM] * 2,
        out_specs=[VMEM] * 2,
        out_shape=[sds((rows, width), BF)] * 2,
        scratch_shapes=[pltpu.VMEM((width, 4 * half), BF), sem((CHUNKS,))],
        compiler_params=params(24),
        cost_estimate=cost(2),
    )
    clean_total, clean_done = tied_call(
        clean_kernel,
        [clean_part, core_swap(clean_send)],
        (),
        True,
        in_specs=[VMEM] * 2,
        out_specs=[VMEM],
        out_shape=[sds((rows, width), BF)],
        compiler_params=params(8),
        cost_estimate=cost(0.5),
    )
    y_own, y_send, mix_done = tied_call(
        mix_kernel,
        [info, g, *bufs_three],
        (clean_done,),
        True,
        in_specs=[SMEM] + [HBM] * 3,
        out_specs=[VMEM] * 2,
        out_shape=[sds((rows, width), F32), sds((rows, width), BF)],
        scratch_shapes=[
            pltpu.VMEM((length, hidden), BF),
            pltpu.VMEM((hidden, width), BF),
            sem((1,)),
            sem((CHUNKS,)),
        ],
        compiler_params=params(16),
        cost_estimate=cost(30),
    )
    one_second = sum_one.second(mix_done)

    own_part, own_send, back_done = tied_call(
        qkv_back_kernel,
        [info, *grads[:3], *bufs_one],
        one_second,
        True,
        in_specs=[SMEM] + [VMEM] * 3 + [HBM] * 2,
        out_specs=[VMEM] * 2,
        out_shape=[sds((rows, width), F32), sds((rows, width), BF)],
        scratch_shapes=[pltpu.VMEM((width, 4 * half), BF), sem((CHUNKS,))],
        compiler_params=params(24),
        cost_estimate=cost(30),
    )
    own_arrived = core_swap(own_send)
    one_totals, one_arrived, one_third = third([sum_one], (back_done,))
    clean_arrived = lax.ppermute(clean_total, "stream", to_clean)
    (grad_down, *up_rows_sums), mlp_done = result(
        [sum_down, sum_up], mlp_totals, mlp_arrived, info, first, one_third
    )
    output = (r1 + y_own + core_swap(y_send).astype(F32)).astype(BF)

    input_grad, input_done = tied_call(
        input_back_kernel,
        [info, x_own, own_part, own_arrived, clean_total, clean_arrived, dr1],
        mlp_done,
        True,
        in_specs=[SMEM] + [VMEM] * 6,
        out_specs=[VMEM],
        out_shape=[sds((rows, width), BF)],
        compiler_params=params(12),
        cost_estimate=cost(2),
    )
    one_rows_sums, _ = result([sum_one], one_totals, one_arrived, info, first, (input_done,))

    def finish(keep, send):
        return mine_theirs(keep, core_swap(send))

    ordered = finish(*one_rows_sums)
    sums_qkv = jnp.stack([v[:, : 3 * half].reshape(n_rows, 3, half) for v in ordered], 2)
    sums_qkv = sums_qkv.reshape(n_rows, 3 * width)
    grad_out = jnp.concatenate([v[:, 3 * half :] for v in ordered], 1)
    sums_up = jnp.stack([v.reshape(n_rows, chips, -1) for v in finish(*up_rows_sums)], 2)
    sums_up = sums_up.reshape(n_rows, 2 * hidden)
    return (
        output[None],
        input_grad[None],
        jnp.sum(sums_qkv * qkv_rows, 1),
        sums_qkv * gain_one,
        grad_out,
        jnp.sum(sums_up * up_rows, 1),
        sums_up * gain_two,
        grad_down,
    )


def solution(mesh):
    rows = P("batch", "stream", None)
    flat, split = P(ALL), P(ALL, None)
    return jax.shard_map(
        local,
        mesh=mesh,
        in_specs=(rows, rows, P("batch"), flat, split, split, flat, split, split),
        out_specs=(rows, rows, flat, split, split, flat, split, split),
        check_vma=False,
    )
```

```python
import functools
import math
import types

import jax
import jax.numpy as jnp
from jax import lax
from jax.experimental import pallas as pl
from jax.experimental.pallas import tpu as pltpu
from jax.sharding import PartitionSpec as P

HEAD_DIM = 64
EPSILON = 1e-05
MASKED = -1e30
BF = jnp.bfloat16
F32 = jnp.float32
ALL = ("batch", "stream")
COSTS = dict(
    touch=0.1,
    halve=0.5,
    spread=0.5,
    prepare=0.5,
    norm=1.5,
    qkv=30.0,
    attend=30.0,
    out_weight=0.5,
    out=0.5,
    up=30.0,
    down=30.0,
    mlp_back=0.1,
    out_back=0.3,
    attend_back=30.0,
    qkv_weight=30.0,
    clean_back=30.0,
    mix=30.0,
    clean=0.5,
    qkv_back=30.0,
    input_back=30.0,
    finish=0.5,
    finish_up=30.0,
    join=0.4,
    result=0.05,
)
CHUNKS = 16
WIDE = 384
BLOCK = 128
TILE = 256
VMEM = pl.BlockSpec(memory_space=pltpu.VMEM)
SMEM = pl.BlockSpec(memory_space=pltpu.SMEM)
HBM = pl.BlockSpec(memory_space=pl.ANY)


def chip_bits(position, core):
    last = ((position >> 2) & 1) * (2 - core) ^ ((position >> 3) & 1) * (1 + core)
    return (position & 3) << 2 ^ last


def dot(a, b):
    return jnp.dot(a, b, preferred_element_type=F32)


def dot_nt(a, b):
    return lax.dot_general(a, b, (((1,), (1,)), ((), ())), preferred_element_type=F32)


def dot_tn(a, b):
    return lax.dot_general(a, b, (((0,), (0,)), ((), ())), preferred_element_type=F32)


def transposed(a):
    return a.astype(F32).T.astype(a.dtype)


def params(mib):
    return pltpu.CompilerParams(vmem_limit_bytes=mib << 20)


def cost(us):
    return pl.CostEstimate(flops=int(us * 1e9), bytes_accessed=1, transcendentals=0)


def sds(shape, dtype):
    return jax.ShapeDtypeStruct(shape, dtype)


TOKEN = sds((8, 128), F32)


def tied_call(
    kernel, inputs, ties=(), token=False, in_specs=None, out_specs=None, out_shape=None, **options
):
    n_in, n_ties = len(inputs), len(ties)
    name = getattr(kernel, "func", kernel).__name__
    options["cost_estimate"] = cost(COSTS[name[: -len("_kernel")]])
    n_out = len(out_shape)

    def body(*refs):
        rest = refs[n_in + n_ties :]
        if token:
            rest[n_out][...] = jnp.zeros(TOKEN.shape, F32)
            rest = rest[:n_out] + rest[n_out + 1 :]
        kernel(*refs[:n_in], *rest)

    if "grid" in options:
        small = pl.BlockSpec(TOKEN.shape, lambda *_: (0, 0))
    else:
        small = VMEM
    inputs = [
        pltpu.with_memory_space_constraint(value, pltpu.HBM) if spec is HBM else value
        for value, spec in zip(inputs, in_specs)
    ]
    out_shape = [
        pltpu.HBM(shape.shape, shape.dtype) if spec is HBM else shape
        for shape, spec in zip(out_shape, out_specs)
    ]
    call = pl.pallas_call(
        body,
        in_specs=list(in_specs) + [small] * n_ties,
        out_specs=list(out_specs) + [small] * token,
        out_shape=list(out_shape) + [TOKEN] * token,
        **options,
    )
    return call(*inputs, *ties)


def chunk_copies(bufs, ref, sems, info, store, first_column=0):
    rows = ref.shape[0] // CHUNKS
    copies = []
    for position in range(CHUNKS):
        chip = info[3] ^ chip_bits(position, info[0])
        buf = bufs[position // 8].at[position % 8, :, pl.ds(first_column, ref.shape[1])]
        view = ref.at[pl.ds(pl.multiple_of(chip * rows, 16), rows), :]
        pair = (view, buf) if store else (buf, view)
        copies.append(pltpu.make_async_copy(*pair, sems.at[position]))
    return copies


def start(copies):
    for copy in copies:
        copy.start()
    return copies


def wait(copies):
    for copy in copies:
        copy.wait()


def fetch(pairs, sems):
    return start([pltpu.make_async_copy(a, b, sems.at[i]) for i, (a, b) in enumerate(pairs)])


def normalize(values):
    centred = values - jnp.mean(values, -1, keepdims=True)
    inverse = lax.rsqrt(jnp.mean(centred * centred, -1, keepdims=True) + EPSILON)
    return centred * inverse, inverse


def norm_back(scaled, normed, inverse):
    return inverse * (
        scaled
        - jnp.mean(scaled, -1, keepdims=True)
        - normed * jnp.mean(scaled * normed, -1, keepdims=True)
    )


def swap_halves(values):
    lanes = lax.broadcasted_iota(jnp.int32, values.shape, 1)
    return jnp.where(
        lanes % HEAD_DIM < HEAD_DIM // 2,
        pltpu.roll(values, 128 - HEAD_DIM // 2, 1),
        pltpu.roll(values, HEAD_DIM // 2, 1),
    )


def turn(values, cosine, sine):
    return jnp.concatenate(
        [
            values[:, at : at + 128] * cosine + swap_halves(values[:, at : at + 128]) * sine
            for at in range(0, values.shape[1], 128)
        ],
        1,
    )


def prepare_kernel(info, w_ref, gain_ref, mine_ref, theirs_ref):
    count = w_ref.shape[0]
    half = mine_ref.shape[1] // 3
    square = (count, count)
    diagonal = lax.broadcasted_iota(jnp.int32, square, 0) == lax.broadcasted_iota(jnp.int32, square, 1)
    gain = gain_ref[...].astype(BF).astype(F32)
    gain = jnp.sum(jnp.where(diagonal, gain, 0.0), 1, keepdims=True)
    for i in range(3):
        for core, ref in ((info[0], mine_ref), (1 - info[0], theirs_ref)):
            part = w_ref[:, pl.ds(pl.multiple_of((2 * i + core) * half, 128), half)]
            ref[:, i * half : (i + 1) * half] = (part.astype(BF).astype(F32) * gain).astype(BF)


def finish_kernel(info, keep_ref, recv_ref, w_ref, gain_ref, out_ref, gain_out):
    count = w_ref.shape[0]
    half = keep_ref.shape[1] // 3
    square = (count, count)
    diagonal = lax.broadcasted_iota(jnp.int32, square, 0) == lax.broadcasted_iota(jnp.int32, square, 1)
    gain = gain_ref[...].astype(BF).astype(F32)
    gain = jnp.sum(jnp.where(diagonal, gain, 0.0), 1, keepdims=True)
    total = jnp.zeros((count, 1), F32)
    for i in range(3):
        for core, ref in ((info[0], keep_ref), (1 - info[0], recv_ref)):
            columns = pl.ds(pl.multiple_of((2 * i + core) * half, 128), half)
            part = ref[:, i * half : (i + 1) * half]
            weights = w_ref[:, columns].astype(BF).astype(F32)
            total += jnp.sum(part * weights, 1, keepdims=True)
            out_ref[:, columns] = part * gain
    gain_out[...] = jnp.sum(jnp.where(diagonal, total, 0.0), 0, keepdims=True)


def finish_up_kernel(info, keep_ref, recv_ref, w_ref, gain_ref, out_ref, wo_ref, gain_out):
    count, columns = w_ref.shape
    hidden, half = columns // 2, wo_ref.shape[1] // 2
    piece = hidden // CHUNKS
    square = (count, count)
    diagonal = lax.broadcasted_iota(jnp.int32, square, 0) == lax.broadcasted_iota(jnp.int32, square, 1)
    gain = gain_ref[...].astype(BF).astype(F32)
    gain = jnp.sum(jnp.where(diagonal, gain, 0.0), 1, keepdims=True)
    keep, recv = keep_ref[...], recv_ref[...]
    first = info[0] == 0
    zero, one = jnp.where(first, keep, recv), jnp.where(first, recv, keep)
    wo_ref[:, :half] = zero[:, hidden:]
    wo_ref[:, half:] = one[:, hidden:]
    parts = []
    for i in range(CHUNKS):
        parts += [zero[:, i * piece : (i + 1) * piece], one[:, i * piece : (i + 1) * piece]]
    sums = jnp.concatenate(parts, 1)
    weights = w_ref[...].astype(BF).astype(F32)
    total = jnp.sum(sums * weights, 1, keepdims=True)
    gain_out[...] = jnp.sum(jnp.where(diagonal, total, 0.0), 0, keepdims=True)
    out_ref[...] = sums * gain


def norm_kernel(info, x_own, x_oth, clean_own, clean_oth, a1_ref):
    core = info[0]
    rows = x_own.shape[0]
    for i, ref in enumerate((x_own, x_oth, clean_own, clean_oth)):
        slot = 2 * (i // 2) + (core if i % 2 == 0 else 1 - core)
        for at in range(0, rows, TILE):
            normed, _ = normalize(ref[at : at + TILE, :].astype(F32))
            a1_ref[slot, at : at + TILE, :] = normed.astype(BF)


def qkv_kernel(info, a1_ref, cos_ref, sin_ref, w0, w1, qkv_ref, w_ref, sems):
    half = a1_ref.shape[1] // 2
    step = pl.program_id(0)

    @pl.when(step == 0)
    def _():
        wait(start(chunk_copies((w0, w1), w_ref, sems, info, False)))

    low = a1_ref[...]
    cosine, sine = cos_ref[...], sin_ref[...]
    keys = dot(low, w_ref[:, half : 2 * half])
    qkv_ref[:, 2 * half :] = dot(low, w_ref[:, 2 * half : 3 * half]).astype(BF)
    qkv_ref[:, half : 2 * half] = turn(keys, cosine, sine).astype(BF)

    @pl.when(step < 2)
    def _():
        queries = dot(low, w_ref[:, :half])
        qkv_ref[:, :half] = turn(queries, cosine, sine).astype(BF)


def block_masks(info):
    noisy, block_len = info[1], info[2]
    keys = lax.broadcasted_iota(jnp.int32, (BLOCK, 2 * BLOCK), 0)
    queries = lax.broadcasted_iota(jnp.int32, (BLOCK, 2 * BLOCK), 1) % BLOCK
    starts = queries & (-block_len)
    clean_ok = keys < starts + jnp.where(noisy == 1, 0, block_len)
    local_ok = jnp.logical_and((keys & (-block_len)) == starts, noisy == 1)
    return clean_ok, local_ok


def by_head(values):
    wide = values.astype(F32)
    first = lax.broadcasted_iota(jnp.int32, wide.shape, 1) < HEAD_DIM
    return jnp.concatenate([jnp.where(first, wide, 0.0), jnp.where(first, 0.0, wide)], 0).astype(BF)


def head_quadrants(mixed):
    return jnp.concatenate([mixed[:HEAD_DIM, :BLOCK], mixed[HEAD_DIM : 2 * HEAD_DIM, BLOCK:]], 0)


def block_scores(queries, clean_keys, own_keys, at, masks):
    size = at + BLOCK
    scores = dot_nt(clean_keys[:size, :], queries)
    own = dot_nt(own_keys[at:size, :], queries)
    parts = [scores[:at]] if at else []
    parts.append(jnp.where(masks[0], scores[at:], MASKED))
    parts.append(jnp.where(masks[1], own, MASKED))
    return parts


def attend_kernel(info, q_ref, k_ref, v_ref, kc_ref, vc_ref, ot_ref, lse_ref):
    masks = block_masks(info)
    length = q_ref.shape[0]
    ones = jnp.ones((16, length), BF)
    own_vt = jnp.concatenate([transposed(v_ref[...]), ones], 0)
    clean_vt = jnp.concatenate([transposed(vc_ref[...]), ones], 0)

    def scores(at):
        queries = by_head(q_ref[at : at + BLOCK, :] * BF(HEAD_DIM**-0.5))
        return block_scores(queries, kc_ref, k_ref, at, masks)

    ready = scores(0)
    for at in range(0, length, BLOCK):
        parts = ready
        if at + BLOCK < length:
            ready = scores(at + BLOCK)
        size = at + BLOCK
        largest = functools.reduce(jnp.maximum, [jnp.max(part, 0, keepdims=True) for part in parts])
        weights = [jnp.exp(part - largest).astype(BF) for part in parts]
        mixed = dot(own_vt[:, at:size], weights[-1]) + dot(clean_vt[:, at:size], weights[-2])
        if at:
            mixed += dot(clean_vt[:, :at], weights[0])
        total = mixed[128:129]
        ot_ref[:, at:size] = head_quadrants(mixed / total).astype(BF)
        block = at // BLOCK
        lse_ref[block : block + 1, :] = largest + jnp.log(total)


def out_weight_kernel(info, w0, w1, out_ref):
    rows = w0.shape[1]
    for position in range(CHUNKS):
        chip = info[3] ^ chip_bits(position, info[0])
        source = (w0, w1)[position // 8]
        out_ref[pl.ds(pl.multiple_of(chip * rows, 16), rows), :] = source[position % 8]


def out_kernel(info, x_own, x_oth, ot_own, ot_oth, wo_own, wo_oth, r1_ref, a2_ref, ot_all, sum_ref):
    core = info[0]
    rows, width = x_own.shape
    half = width // 2
    mine = pl.ds(pl.multiple_of(core * half, 128), half)
    theirs = pl.ds(pl.multiple_of((1 - core) * half, 128), half)
    for i, x_ref in enumerate((x_own, x_oth)):
        at_rows = pl.ds(pl.multiple_of((core if i == 0 else 1 - core) * rows, 128), rows)
        ot_all[mine, :] = ot_own[:, at_rows]
        ot_all[theirs, :] = ot_oth[:, at_rows]
        merged = transposed(ot_all[...])
        sum_ref[:, mine] = dot(merged, wo_own[...])
        sum_ref[:, theirs] = dot(merged, wo_oth[...])
        for at in range(0, rows, TILE):
            r1 = x_ref[at : at + TILE, :].astype(F32) + sum_ref[at : at + TILE, :]
            if i == 0:
                r1_ref[at : at + TILE, :] = r1
            a2_ref[i * rows + at : i * rows + at + TILE, :] = normalize(r1)[0].astype(BF)


def gelu_parts(u):
    c = math.sqrt(2.0 / math.pi)
    square = u * u
    half = 0.5 + 0.5 * jnp.tanh(u * (c + (0.044715 * c) * square))
    active = u * half
    slope = half + active * (1.0 - half) * (2.0 * c + (6.0 * 0.044715 * c) * square)
    return active, slope


def up_kernel(
    info, a2_in, dy_own, dy_oth, w0, w1, g_out, slope_out, d0, d1,
    a2_ref, dy_ref, w_ref, g_ref, slope_ref, dw_ref, sems, w_sems, g_sems,
):
    rows = dy_own.shape[0]
    hidden = w_ref.shape[1]
    a2_copy = fetch([(a2_in, a2_ref)], sems)
    w_in = start(chunk_copies((w0, w1), w_ref, w_sems, info, False))
    dy_in = fetch(
        [(dy_own, dy_ref.at[pl.ds(0, rows)]), (dy_oth, dy_ref.at[pl.ds(rows, rows)])], sems.at[pl.ds(2, 2)]
    )
    wait(a2_copy + w_in)
    ready = dot(a2_ref[...], w_ref[:, :TILE])
    out = []
    for col in range(0, hidden, TILE):
        u = ready
        if col + TILE < hidden:
            ready = dot(a2_ref[...], w_ref[:, col + TILE : col + 2 * TILE])
        span = slice(col, col + TILE)
        active, slope = gelu_parts(u)
        g_ref[:, span] = active.astype(BF)
        slope_ref[:, span] = slope.astype(BF)
        at = pl.ds(col, TILE)
        pairs = [(g_ref.at[:, at], g_out.at[:, at]), (slope_ref.at[:, at], slope_out.at[:, at])]
        out += fetch(pairs, g_sems.at[pl.ds(2 * (col // TILE), 2)])
        if col == 0:
            wait(dy_in)
        dw_ref[span, :] = dot_tn(g_ref[:, span], dy_ref[...]).astype(BF)
    wait(out + start(chunk_copies((d0, d1), dw_ref, w_sems, info, True)))


def down_kernel(
    info, a2_in, slope_in, dy_own, dy_oth, u0, u1, w0, w1, e_ref, send_ref, d0, d1,
    a2_ref, dy_ref, slope_ref, up_ref, w_ref, du_ref, dw_ref, sems, w_sems, u_sems,
):
    rows = dy_own.shape[0]
    hidden = w_ref.shape[0]
    low, high = pl.ds(0, rows), pl.ds(rows, rows)
    dy_in = fetch([(dy_own, dy_ref.at[low]), (dy_oth, dy_ref.at[high])], sems)
    w_in = start(chunk_copies((w0, w1), w_ref, w_sems, info, False))
    slope_copy = fetch([(slope_in, slope_ref)], sems.at[pl.ds(2, 1)])
    a2_copy = fetch([(a2_in, a2_ref)], sems.at[pl.ds(3, 1)])
    u_in = start(chunk_copies((u0, u1), up_ref, u_sems, info, False))
    wait(dy_in + w_in)
    ready = dot_nt(dy_ref[...], w_ref[:TILE, :])
    for col in range(0, hidden, TILE):
        grad = ready
        if col + TILE < hidden:
            ready = dot_nt(dy_ref[...], w_ref[col + TILE : col + 2 * TILE, :])
        if col == 0:
            wait(slope_copy + a2_copy)
        span = slice(col, col + TILE)
        du_ref[:, span] = (grad * slope_ref[:, span].astype(F32)).astype(BF)
        dw_ref[:, span] = dot_tn(a2_ref[...], du_ref[:, span]).astype(BF)
    out = start(chunk_copies((d0, d1), dw_ref, w_sems, info, True))
    wait(u_in)
    send_ref[...] = dot_nt(du_ref[rows:, :], up_ref[...]).astype(BF)
    e_ref[...] = dot_nt(du_ref[:rows, :], up_ref[...])
    wait(out)


def mix_kernel(info, g_in, w0, w1, y_ref, send_ref, g_ref, w_ref, sems, w_sems):
    rows = y_ref.shape[0]
    w_in = start(chunk_copies((w0, w1), w_ref, w_sems, info, False))
    wait(fetch([(g_in, g_ref)], sems) + w_in)
    send_ref[...] = dot(g_ref[rows:, :], w_ref[...]).astype(BF)
    y_ref[...] = dot(g_ref[:rows, :], w_ref[...])


def join_kernel(column, *refs):
    out = refs[-1]
    at = 0
    for ref in refs[:-1]:
        out[at : at + ref.shape[0]] = ref[:, :, column : column + out.shape[2]]
        at += ref.shape[0]


def touch_kernel(_):
    pass


def halve_kernel(keep_ref, recv_ref, keep_out, send_out):
    count = keep_out.shape[0]
    for part in range(2):
        span = slice(part * count, (part + 1) * count)
        total = keep_ref[span].astype(F32) + recv_ref[span].astype(F32)
        (keep_out, send_out)[part][...] = total.astype(BF)


def spread_kernel(*refs):
    count = (len(refs) - 3) // 3
    totals, sends = refs[2 * count : 3 * count], refs[3 * count :]
    at = 0
    for i in range(count):
        keep_ref, recv_ref = refs[2 * i], refs[2 * i + 1]
        rows, columns = totals[i].shape
        for part in range(4):
            total = keep_ref[part].astype(F32) + recv_ref[part].astype(F32)
            if part == 0:
                totals[i][...] = total
                continue
            for j in range(columns // WIDE):
                low = at + j * rows
                sends[part - 1][low : low + rows, :] = total[:, j * WIDE : (j + 1) * WIDE].astype(BF)
        at += rows * columns // WIDE


def result_kernel(count, info, *refs):
    totals, arrived, outs = refs[:count], refs[count : count + 3], list(refs[count + 3 :])
    core = info[0]
    at = 0
    for i in range(count):
        rows, columns = totals[i].shape
        parts = []
        for j in range(columns // WIDE):
            low = at + j * rows
            part = totals[i][:, j * WIDE : (j + 1) * WIDE]
            for ref in arrived:
                part = part + ref[low : low + rows, :].astype(F32)
            parts.append(part)
        at += rows * columns // WIDE
        keep = outs.pop(0)
        if keep.shape[0] == rows:
            for j, part in enumerate(parts):
                keep[:, j * WIDE : (j + 1) * WIDE] = part
            continue
        send = outs.pop(0)
        half = rows // 2
        for j, part in enumerate(parts):
            span = slice(j * WIDE, (j + 1) * WIDE)
            keep[:, span] = jnp.where(core == 0, part[:half], part[half:])
            send[:, span] = jnp.where(core == 0, part[half:], part[:half])


def clean_kernel(own_ref, recv_ref, out_ref):
    out_ref[...] = (own_ref[...].astype(F32) + recv_ref[...].astype(F32)).astype(BF)


def mlp_back_kernel(r1_ref, e_ref, recv_ref, dy_ref, dr1_ref, dr_ref):
    normed, inverse = normalize(r1_ref[...])
    scaled = e_ref[...] + recv_ref[...].astype(F32)
    dr1 = dy_ref[...].astype(F32) + norm_back(scaled, normed, inverse)
    dr1_ref[...] = dr1
    dr_ref[...] = dr1.astype(BF)


def out_back_kernel(
    info, dr_own, dr_oth, wo_own, wo_oth, ot_own, ot_oth, _0, _1, do_ref, d0, d1, dr_all, ot_all, dwo_ref, sems
):
    core = info[0]
    rows, width = dr_own.shape
    half = width // 2
    mine = pl.ds(pl.multiple_of(core * half, 128), half)
    theirs = pl.ds(pl.multiple_of((1 - core) * half, 128), half)
    dr_all[pl.ds(pl.multiple_of(core * rows, 128), rows), :] = dr_own[...]
    dr_all[pl.ds(pl.multiple_of((1 - core) * rows, 128), rows), :] = dr_oth[...]
    ot_all[mine, :] = ot_own[...]
    ot_all[theirs, :] = ot_oth[...]
    dwo_ref[...] = dot(ot_all[...], dr_all[:, mine]).astype(BF)
    copies = start(chunk_copies((d0, d1), dwo_ref, sems, info, True, d0.shape[2] - half))
    grad = dot_nt(dr_all[:, mine], wo_own[mine, :])
    grad += dot_nt(dr_all[:, theirs], wo_oth[mine, :])
    do_ref[...] = grad.astype(BF)
    wait(copies)


def attend_back_kernel(
    info, q_ref, k_ref, v_ref, kc_ref, vc_ref, do_ref, ot_ref, lse_ref, cos_ref, sin_ref,
    dq_ref, dk_ref, dv_ref, dkc_ref, dvc_ref, dk_sum, dv_sum,
):
    masks = block_masks(info)
    length = q_ref.shape[0]
    dk_sum[...] = jnp.zeros_like(dk_sum)
    dv_sum[...] = jnp.zeros_like(dv_sum)
    scale = BF(HEAD_DIM**-0.5)
    own_kt = transposed(k_ref[...] * scale)
    clean_kt = transposed(kc_ref[...] * scale)

    def first_part(at):
        size = at + BLOCK
        queries = by_head(q_ref[at:size, :] * scale)
        grads = by_head(do_ref[at:size, :])
        parts = block_scores(queries, kc_ref, k_ref, at, masks)
        clean_dp = dot_nt(vc_ref[:size, :], grads)
        slopes = [clean_dp[:at]] if at else []
        slopes += [clean_dp[at:], dot_nt(v_ref[at:size, :], grads)]
        return queries, grads, parts, slopes

    ready = first_part(0)
    for at in range(0, length, BLOCK):
        queries, grads, parts, slopes = ready
        size = at + BLOCK
        if size < length:
            ready = first_part(size)
        block = at // BLOCK
        lse = lse_ref[block : block + 1, :]
        products = do_ref[at:size, :].astype(F32).T * ot_ref[:, at:size].astype(F32)
        shared = jnp.concatenate(
            [
                jnp.sum(products[:HEAD_DIM], 0, keepdims=True),
                jnp.sum(products[HEAD_DIM:], 0, keepdims=True),
            ],
            1,
        )
        weights = [jnp.exp(part - lse) for part in parts]
        changes = [(w * (s - shared)).astype(BF) for w, s in zip(weights, slopes)]
        weights = [w.astype(BF) for w in weights]
        dq = dot(own_kt[:, at:size], changes[-1]) + dot(clean_kt[:, at:size], changes[-2])
        dk = dot(changes[-1], queries)
        dv_ref[at:size, :] = dot(weights[-1], grads).astype(BF)
        dk_sum[at:size, :] += dot(changes[-2], queries)
        dv_sum[at:size, :] += dot(weights[-2], grads)
        if at:
            dq += dot(clean_kt[:, :at], changes[0])
            dk_sum[:at, :] += dot(changes[0], queries)
            dv_sum[:at, :] += dot(weights[0], grads)
        cosine, sine = cos_ref[at:size, :], -sin_ref[at:size, :]
        dq_ref[at:size, :] = turn(head_quadrants(dq).T, cosine, sine).astype(BF)
        dk_ref[at:size, :] = turn(dk, cosine, sine).astype(BF)
    dkc_ref[...] = turn(dk_sum[...], cos_ref[...], -sin_ref[...]).astype(BF)
    dvc_ref[...] = dv_sum[...].astype(BF)


def qkv_weight_kernel(
    info, dq_ref, dk_ref, dv_ref, dkc_ref, dvc_ref, a1_ref, d0, d1, dw_ref, sems
):
    length, half = dq_ref.shape
    own, clean = a1_ref.at[pl.ds(0, length)], a1_ref.at[pl.ds(length, length)]
    dw_ref[:, :half] = dot_tn(own[...], dq_ref[...]).astype(BF)
    for i, (a, b) in enumerate(((dk_ref, dkc_ref), (dv_ref, dvc_ref))):
        total = dot_tn(own[...], a[...]) + dot_tn(clean[...], b[...])
        dw_ref[:, (i + 1) * half : (i + 2) * half] = total.astype(BF)
    wait(start(chunk_copies((d0, d1), dw_ref, sems, info, True)))


def clean_back_kernel(info, dkc_ref, dvc_ref, w0, w1, keep_ref, send_ref, w_ref, sems):
    core = info[0]
    half = dkc_ref.shape[1]
    rows = keep_ref.shape[0]
    wait(start(chunk_copies((w0, w1), w_ref, sems, info, False)))
    w_k, w_v = [w_ref.at[:, pl.ds(i * half, half)] for i in (1, 2)]
    for at, ref in (((1 - core) * rows, send_ref), (core * rows, keep_ref)):
        span = pl.ds(pl.multiple_of(at, 128), rows)
        clean = dot_nt(dkc_ref[span, :], w_k[...]) + dot_nt(dvc_ref[span, :], w_v[...])
        ref[...] = clean.astype(BF)


def qkv_back_kernel(
    info, dq_ref, dk_ref, dv_ref, w0, w1, own_ref, send_ref, w_ref, sems
):
    core = info[0]
    half = dq_ref.shape[1]
    rows = own_ref.shape[0]
    wait(start(chunk_copies((w0, w1), w_ref, sems, info, False)))
    w_q, w_k, w_v = [w_ref.at[:, pl.ds(i * half, half)] for i in range(3)]
    for at, ref in (((1 - core) * rows, send_ref), (core * rows, own_ref)):
        span = pl.ds(pl.multiple_of(at, 128), rows)
        own = dot_nt(dq_ref[span, :], w_q[...]) + dot_nt(dk_ref[span, :], w_k[...])
        own += dot_nt(dv_ref[span, :], w_v[...])
        ref[...] = own.astype(ref.dtype)


def input_back_kernel(info, x_ref, own_ref, recv_ref, clean_ref, arrived_ref, dr1_ref, out_ref):
    for at in range(0, x_ref.shape[0], TILE):
        rows = slice(at, at + TILE)
        normed, inverse = normalize(x_ref[rows, :].astype(F32))
        scaled = own_ref[rows, :] + recv_ref[rows, :].astype(F32)
        clean = clean_ref[rows, :].astype(F32) + arrived_ref[rows, :].astype(F32)
        scaled += jnp.where(info[1] == 0, clean, 0.0)
        out_ref[rows, :] = (dr1_ref[rows, :] + norm_back(scaled, normed, inverse)).astype(BF)


def core_swap(value):
    size = lax.axis_size("stream")
    return lax.ppermute(value, "stream", [(i, i ^ 1) for i in range(size)])


def z_swap(value, bits):
    size = lax.axis_size("batch")
    return lax.ppermute(value, "batch", [(i, i ^ (bits << 1)) for i in range(size)])


def cross_swap(value, y_core):
    batches, streams = lax.axis_size("batch"), lax.axis_size("stream")
    pairs = []
    for b in range(batches):
        for s in range(streams):
            peer = (b ^ 1, s) if s % 2 == y_core else (b, s ^ 2)
            pairs.append((b * streams + s, peer[0] * streams + peer[1]))
    return lax.ppermute(value, ALL, pairs)


def chip_groups():
    batches, streams = lax.axis_size("batch"), lax.axis_size("stream")
    return [
        [b * streams + 2 * x + c for b in range(batches) for x in range(streams // 2)]
        for c in range(2)
    ]


def join(parts, ties=(), column=0, width=None):
    shape = (sum(part.shape[0] for part in parts), parts[0].shape[1], width or parts[0].shape[2])
    return tied_call(
        functools.partial(join_kernel, column),
        parts,
        ties,
        True,
        in_specs=[VMEM] * len(parts),
        out_specs=[VMEM],
        out_shape=[sds(shape, BF)],
        compiler_params=params(10),
    )


def arrival(value):
    if not is_fast():
        return []
    return tied_call(
        touch_kernel,
        [value],
        (),
        True,
        in_specs=[pl.BlockSpec(memory_space=pl.ANY)],
        out_specs=[],
        out_shape=[],
        compiler_params=params(4),
    )


def is_fast():
    return 2 * lax.axis_size("batch") == CHUNKS


class Gather:
    def __init__(self, chunk, first, *ties):
        self.chunk, self.first, self.tokens = chunk, first, []
        if is_fast():
            held = chunk[None]
            if ties:
                held, token = join([held], ties)
                self.tokens = [token]
            self.parts = [held] + [z_swap(held, bits) for bits in (1, 2, 3)]

    def middle(self, *ties):
        if is_fast():
            self.held, token = join(self.parts, ties)
            self.received = cross_swap(self.held, 0)
            self.tokens = [token]
        return self.tokens

    def last(self, *ties, column=0, width=None):
        if is_fast():
            held, token = join([self.held, self.received], ties, column, width)
            self.tokens = [token]
            return [held, cross_swap(held, 1)]
        width = width or self.chunk.shape[1]
        return slow_gather(self.chunk[:, column : column + width], self.first)


def slow_gather(chunk, first):
    full = lax.all_gather(chunk, ALL, axis=0, tiled=True, axis_index_groups=chip_groups())
    full = full.reshape(CHUNKS, -1, full.shape[1])
    orders = [jnp.stack([full[chip_bits(p, c)] for p in range(CHUNKS)]) for c in range(2)]
    full = jnp.where(first, *orders)
    return [full[:8], full[8:]]


def halve(keep, received, ties):
    count, rows, columns = keep.shape
    return tied_call(
        halve_kernel,
        [keep, received],
        ties,
        True,
        in_specs=[VMEM] * 2,
        out_specs=[VMEM] * 2,
        out_shape=[sds((count // 2, rows, columns), BF)] * 2,
        compiler_params=params(12),
    )


class ScatterSum:
    def __init__(self, keep, send, whole=False):
        self.keep, self.send, self.whole = keep, send, whole
        if is_fast():
            self.received = cross_swap(send, 1)

    def second(self, *ties):
        if not is_fast():
            return []
        self.keep, send, token = halve(self.keep, self.received, ties)
        self.received = cross_swap(send, 0)
        return [token]


def third(sums, ties):
    if not is_fast():
        return [], [], []
    shapes = [part.keep.shape[1:] for part in sums]
    rows = sum(rows * columns for rows, columns in shapes) // WIDE
    *out, token = tied_call(
        spread_kernel,
        [part for one in sums for part in (one.keep, one.received)],
        ties,
        True,
        in_specs=[VMEM] * (2 * len(sums)),
        out_specs=[VMEM] * (len(sums) + 3),
        out_shape=[sds(shape, F32) for shape in shapes] + [sds((rows, WIDE), BF)] * 3,
        compiler_params=params(16),
    )
    arrived = [z_swap(part, i + 1) for i, part in enumerate(out[len(sums) :])]
    return out[: len(sums)], arrived, [token]


def result(sums, totals, arrived, info, first, ties):
    if not is_fast():
        out = []
        for one in sums:
            total = slow_sum(one.keep, one.send, first)
            if one.whole:
                out.append(total)
            else:
                count = total.shape[0] // 2
                out.append(jnp.where(first, total[:count], total[count:]))
                out.append(jnp.where(first, total[count:], total[:count]))
        return out, []
    shapes = []
    for one, total in zip(sums, totals):
        rows, columns = total.shape
        shapes += [(rows, columns)] if one.whole else [(rows // 2, columns)] * 2
    *out, token = tied_call(
        functools.partial(result_kernel, len(sums)),
        [info, *totals, *arrived],
        ties,
        True,
        in_specs=[SMEM] + [VMEM] * (len(sums) + 3),
        out_specs=[VMEM] * len(shapes),
        out_shape=[sds(shape, F32) for shape in shapes],
        compiler_params=params(8),
    )
    return out, [token]


def slow_sum(keep, send, first):
    both = jnp.concatenate([keep, send], 0)
    orders = [[chip_bits(p, c) for p in range(CHUNKS)] for c in range(2)]
    sorted_ = [jnp.stack([both[orders[c].index(k)] for k in range(CHUNKS)]) for c in range(2)]
    full = jnp.where(first, *sorted_).astype(F32)
    full = full.reshape(-1, full.shape[2])
    return lax.psum_scatter(
        full, ALL, scatter_dimension=0, tiled=True, axis_index_groups=chip_groups()
    )


def local(tokens, cotangent, block_size, gain_attn, w_qkv, w_out, gain_mlp, w_up, w_down):
    rows, width = tokens.shape[1:]
    half = width // 2
    length = 2 * rows
    batches = lax.axis_size("batch")
    chips = 2 * batches
    hidden = w_up.shape[1] // 2
    stream, batch = lax.axis_index("stream"), lax.axis_index("batch")
    core, noisy = stream % 2, stream // 2
    me = batch * 2 + noisy if chips == CHUNKS else jnp.zeros_like(batch)
    info = jnp.stack([core, noisy, block_size[0], me]).astype(jnp.int32)
    first = core == 0
    n_rows = w_qkv.shape[0]

    def in_order(own, other, axis):
        return jnp.where(
            first, jnp.concatenate([own, other], axis), jnp.concatenate([other, own], axis)
        )

    def mine_theirs(zero, one):
        return jnp.where(first, zero, one), jnp.where(first, one, zero)

    gain_row = gain_attn[None]
    mine, theirs = tied_call(
        prepare_kernel,
        [info, w_qkv, gain_row],
        in_specs=[SMEM, VMEM, VMEM],
        out_specs=[VMEM] * 2,
        out_shape=[sds((n_rows, 3 * half), BF)] * 2,
        compiler_params=params(4),
    )
    chunk_one = in_order(mine, core_swap(theirs), 0)
    gain_two = gain_mlp.astype(BF).astype(F32)[:, None]
    up_rows = w_up.astype(BF).astype(F32)
    scaled = (up_rows * gain_two).astype(BF).reshape(n_rows, chips, 2, -1)
    out_low = w_out.astype(BF)
    mine, theirs = mine_theirs(
        *[
            jnp.concatenate(
                [scaled[:, :, c].reshape(n_rows, -1), out_low[:, c * half : (c + 1) * half]], 1
            )
            for c in range(2)
        ]
    )
    chunk_two = in_order(mine, core_swap(theirs), 0)

    x_own = tokens[0]
    dy_own = cotangent[0]
    streams = lax.axis_size("stream")
    to_noisy = [(i, i + streams // 2) for i in range(streams // 2)]
    to_clean = [(b, a) for a, b in to_noisy]
    arrived = lax.ppermute(x_own, "stream", to_noisy)
    clean_own = jnp.where(noisy == 1, arrived, x_own)
    x_oth = core_swap(x_own)
    clean_oth = core_swap(clean_own)
    dy_oth = core_swap(dy_own)

    places = jnp.arange(length, dtype=jnp.int32)
    lanes = jnp.arange(128, dtype=jnp.int32)
    half_dim = HEAD_DIM // 2
    frequency = jnp.exp(-math.log(10000.0) * (lanes % half_dim).astype(F32) / half_dim)
    angles = places.astype(F32)[:, None] * frequency[None, :]
    cosine = jnp.cos(angles)
    sine = jnp.where((lanes % HEAD_DIM < half_dim)[None], -jnp.sin(angles), jnp.sin(angles))

    sem = pltpu.SemaphoreType.DMA
    tokens = types.SimpleNamespace()
    tokens.tables = [cosine[:8], sine[:8], chunk_two[:8, :128].astype(F32)] if is_fast() else []

    one = Gather(chunk_one, first)
    tokens.one_middle = one.middle(*tokens.tables)
    bufs_one = one.last()
    tokens.one_last = one.tokens
    two = Gather(chunk_two, first, *[*tokens.one_last])
    tokens.two_start = two.tokens
    a1, *tokens.norm = tied_call(
        norm_kernel,
        [info, x_own, x_oth, clean_own, clean_oth],
        [*tokens.two_start],
        True,
        in_specs=[SMEM] + [VMEM] * 4,
        out_specs=[VMEM],
        out_shape=[sds((4, rows, width), BF)],
        compiler_params=params(20),
    )
    a1 = a1.reshape(2 * length, width)

    tokens.two_middle = two.middle(*tokens.norm)

    qkv, *tokens.qkv = tied_call(
        qkv_kernel,
        [info, a1, cosine, sine, *bufs_one],
        [*tokens.two_middle] or tokens.norm,
        True,
        grid=(4,),
        in_specs=[
            SMEM,
            pl.BlockSpec((rows, width), lambda i: (i, 0)),
            pl.BlockSpec((rows, 128), lambda i: (i % 2, 0)),
            pl.BlockSpec((rows, 128), lambda i: (i % 2, 0)),
        ]
        + [HBM] * 2,
        out_specs=[pl.BlockSpec((rows, 3 * half), lambda i: (i, 0))],
        out_shape=[pltpu.HBM((2 * length, 3 * half), BF)],
        scratch_shapes=[pltpu.VMEM((width, 3 * half), BF), sem((CHUNKS,))],
        compiler_params=params(24),
    )
    qkv = pltpu.with_memory_space_constraint(qkv, pltpu.HBM)
    bufs_out = two.last(*tokens.qkv, column=hidden, width=half)
    tokens.out_last = two.tokens
    bufs_two = two.last(*tokens.qkv, width=hidden)
    tokens.two_last = two.tokens
    three = Gather(w_down.astype(BF), first, *[*tokens.two_last])
    tokens.three_start = three.tokens

    pairs = half // 128

    def pair_spec(part, clean):
        return pl.BlockSpec((length, 128), lambda p: (clean, part * pairs + p))

    qkv_specs = [pair_spec(0, 0), pair_spec(1, 0), pair_spec(2, 0), pair_spec(1, 1), pair_spec(2, 1)]
    lse_spec = pl.BlockSpec((length // BLOCK, 2 * BLOCK), lambda p: (p, 0))
    ot_own, lse, *tokens.attend = tied_call(
        attend_kernel,
        [info, qkv, qkv, qkv, qkv, qkv],
        [*tokens.out_last, *tokens.two_last, *tokens.three_start],
        True,
        grid=(pairs,),
        in_specs=[SMEM] + qkv_specs,
        out_specs=[pl.BlockSpec((128, length), lambda p: (p, 0)), lse_spec],
        out_shape=[sds((half, length), BF), sds((pairs * length // BLOCK, 2 * BLOCK), F32)],
        compiler_params=params(28),
    )
    ot_oth = core_swap(ot_own)
    tokens.three_middle = three.middle(*tokens.attend)

    (wo_own,) = tied_call(
        out_weight_kernel,
        [info, *bufs_out],
        [*tokens.three_middle],
        in_specs=[SMEM] + [VMEM] * 2,
        out_specs=[VMEM],
        out_shape=[sds((width, half), BF)],
        compiler_params=params(8),
    )
    wo_oth = core_swap(wo_own)

    r1, a2, *tokens.out = tied_call(
        out_kernel,
        [info, x_own, x_oth, ot_own, ot_oth, wo_own, wo_oth],
        [],
        True,
        in_specs=[SMEM] + [VMEM] * 6,
        out_specs=[VMEM] * 2,
        out_shape=[sds((rows, width), F32), sds((length, width), BF)],
        scratch_shapes=[pltpu.VMEM((width, rows), BF), pltpu.VMEM((rows, width), F32)],
        compiler_params=params(20),
    )

    bufs_three = three.last(*tokens.out)
    tokens.three_last = three.tokens
    down_bufs = [sds((8, 2 * width // CHUNKS, width), BF)] * 2
    up_bufs = [sds((8, width // CHUNKS, hidden + half), BF)] * 2
    one_bufs = [sds((8, width // CHUNKS, 3 * half), BF)] * 2
    g, slope, *down_parts, up_done = tied_call(
        up_kernel,
        [info, a2, dy_own, dy_oth, *bufs_two],
        [*tokens.three_last],
        True,
        in_specs=[SMEM] + [HBM] * 5,
        out_specs=[HBM] * 4,
        out_shape=[sds((length, hidden), BF), sds((length, hidden), BF)] + down_bufs,
        scratch_shapes=[
            pltpu.VMEM((length, width), BF),
            pltpu.VMEM((length, width), BF),
            pltpu.VMEM((width, hidden), BF),
            pltpu.VMEM((length, hidden), BF),
            pltpu.VMEM((length, hidden), BF),
            pltpu.VMEM((hidden, width), BF),
            sem((4,)),
            sem((CHUNKS,)),
            sem((2 * hidden // TILE,)),
        ],
        compiler_params=params(44),
    )
    sum_down = ScatterSum(*down_parts, whole=True)
    tokens.up = [up_done]

    e_own, e_send, *up_parts, down_done = tied_call(
        down_kernel,
        [info, a2, slope, dy_own, dy_oth, *bufs_two, *bufs_three],
        [],
        True,
        in_specs=[SMEM] + [HBM] * 8,
        out_specs=[VMEM] * 2 + [HBM] * 2,
        out_shape=[sds((rows, width), F32), sds((rows, width), BF)] + up_bufs,
        scratch_shapes=[
            pltpu.VMEM((length, width), BF),
            pltpu.VMEM((length, width), BF),
            pltpu.VMEM((length, hidden), BF),
            pltpu.VMEM((width, hidden), BF),
            pltpu.VMEM((hidden, width), BF),
            pltpu.VMEM((length, hidden), BF),
            pltpu.VMEM((width, hidden), BF),
            sem((5,)),
            sem((CHUNKS,)),
            sem((CHUNKS,)),
        ],
        compiler_params=params(30),
    )
    e_recv = core_swap(e_send)
    tokens.down = [down_done]
    tokens.down_second = sum_down.second(*tokens.down)

    row_block = pl.BlockSpec((BLOCK, width), lambda i: (i, 0))
    dr1, dr_own = tied_call(
        mlp_back_kernel,
        [r1, e_own, e_recv, dy_own],
        [*tokens.down_second],
        grid=(rows // BLOCK,),
        in_specs=[row_block] * 4,
        out_specs=[row_block] * 2,
        out_shape=[sds((rows, width), F32), sds((rows, width), BF)],
        compiler_params=params(8),
    )
    dr_oth = core_swap(dr_own)

    do, *up_parts, out_back_done = tied_call(
        out_back_kernel,
        [info, dr_own, dr_oth, wo_own, wo_oth, ot_own, ot_oth, *up_parts],
        [],
        True,
        in_specs=[SMEM] + [VMEM] * 6 + [HBM] * 2,
        out_specs=[VMEM] + [HBM] * 2,
        out_shape=[sds((length, half), BF)] + up_bufs,
        input_output_aliases={7: 1, 8: 2},
        scratch_shapes=[
            pltpu.VMEM((length, width), BF),
            pltpu.VMEM((width, length), BF),
            pltpu.VMEM((width, half), BF),
            sem((CHUNKS,)),
        ],
        compiler_params=params(20),
    )
    sum_up = ScatterSum(*up_parts)
    tokens.out_back = [out_back_done]
    tokens.down_arrival = arrival(sum_down.received) if is_fast() else []
    down_totals, down_arrived, tokens.down_third = third([sum_down], [*tokens.out_back])

    column = pl.BlockSpec((length, 128), lambda p: (0, p))
    whole = pl.BlockSpec((length, 128), lambda p: (0, 0))
    *grads, attend_back_done = tied_call(
        attend_back_kernel,
        [info, qkv, qkv, qkv, qkv, qkv, do, ot_own, lse, cosine, sine],
        [*tokens.down_third],
        True,
        grid=(pairs,),
        in_specs=[SMEM]
        + qkv_specs
        + [column, pl.BlockSpec((128, length), lambda p: (p, 0)), lse_spec, whole, whole],
        out_specs=[column] * 5,
        out_shape=[sds((length, half), BF)] * 5,
        scratch_shapes=[pltpu.VMEM((length, 128), F32)] * 2,
        compiler_params=params(36),
    )
    tokens.attend_back = [attend_back_done]
    (grad_down,), tokens.down_result = result(
        [sum_down], down_totals, down_arrived, info, first, [*tokens.attend_back]
    )
    tokens.up_second = sum_up.second(*tokens.down_result)
    *one_parts, weight_done = tied_call(
        qkv_weight_kernel,
        [info, *grads, a1],
        [*tokens.up_second],
        True,
        in_specs=[SMEM] + [VMEM] * 6,
        out_specs=[HBM] * 2,
        out_shape=one_bufs,
        scratch_shapes=[pltpu.VMEM((width, 3 * half), BF), sem((CHUNKS,))],
        compiler_params=params(24),
    )
    sum_one = ScatterSum(*one_parts)
    tokens.weight = [weight_done]
    clean_part, clean_send, clean_back_done = tied_call(
        clean_back_kernel,
        [info, *grads[3:], *bufs_one],
        [*tokens.weight],
        True,
        in_specs=[SMEM] + [VMEM] * 2 + [HBM] * 2,
        out_specs=[VMEM] * 2,
        out_shape=[sds((rows, width), BF)] * 2,
        scratch_shapes=[pltpu.VMEM((width, 3 * half), BF), sem((CHUNKS,))],
        compiler_params=params(24),
    )
    tokens.clean_back = [clean_back_done]

    def mix():
        return tied_call(
            mix_kernel,
            [info, g, *bufs_three],
            [*tokens.clean_back],
            True,
            in_specs=[SMEM] + [HBM] * 3,
            out_specs=[VMEM] * 2,
            out_shape=[sds((rows, width), F32), sds((rows, width), BF)],
            scratch_shapes=[
                pltpu.VMEM((length, hidden), BF),
                pltpu.VMEM((hidden, width), BF),
                sem((1,)),
                sem((CHUNKS,)),
            ],
            compiler_params=params(16),
        )

    y_own, y_send, *tokens.mix = mix()
    up_totals, up_arrived, tokens.up_third = third([sum_up], [*tokens.mix])
    clean_swapped = core_swap(clean_send)
    tokens.one_second = sum_one.second(*tokens.up_third)

    (clean_total,) = tied_call(
        clean_kernel,
        [clean_part, clean_swapped],
        [*tokens.one_second],
        in_specs=[VMEM] * 2,
        out_specs=[VMEM],
        out_shape=[sds((rows, width), BF)],
        compiler_params=params(8),
    )
    clean_arrived = lax.ppermute(clean_total, "stream", to_clean)

    own_part, own_send, back_done = tied_call(
        qkv_back_kernel,
        [info, *grads[:3], *bufs_one],
        [*tokens.one_second],
        True,
        in_specs=[SMEM] + [VMEM] * 3 + [HBM] * 2,
        out_specs=[VMEM] * 2,
        out_shape=[sds((rows, width), F32), sds((rows, width), BF)],
        scratch_shapes=[pltpu.VMEM((width, 3 * half), BF), sem((CHUNKS,))],
        compiler_params=params(24),
    )
    own_arrived = core_swap(own_send)
    tokens.qkv_back = [back_done]
    tokens.clean_arrival = arrival(clean_arrived)
    one_totals, one_arrived, tokens.one_third = third([sum_one], [*tokens.qkv_back])
    up_sums, tokens.up_result = result(
        [sum_up], up_totals, up_arrived, info, first, [*tokens.one_third]
    )
    output = (r1 + y_own + core_swap(y_send).astype(F32)).astype(BF)

    input_grad, *tokens.input = tied_call(
        input_back_kernel,
        [info, x_own, own_part, own_arrived, clean_total, clean_arrived, dr1],
        [*tokens.up_result],
        True,
        in_specs=[SMEM] + [VMEM] * 6,
        out_specs=[VMEM],
        out_shape=[sds((rows, width), BF)],
        compiler_params=params(12),
    )
    one_sums, tokens.one_result = result(
        [sum_one], one_totals, one_arrived, info, first, [*tokens.input]
    )
    grad_qkv, grad_gain = tied_call(
        finish_kernel,
        [info, one_sums[0], core_swap(one_sums[1]), w_qkv, gain_row],
        in_specs=[SMEM] + [VMEM] * 4,
        out_specs=[VMEM] * 2,
        out_shape=[sds((n_rows, 3 * width), F32), sds((1, n_rows), F32)],
        compiler_params=params(4),
    )

    up_swapped = core_swap(up_sums[1])
    if is_fast():
        grad_w_up, grad_out, gain_up = tied_call(
            finish_up_kernel,
            [info, up_sums[0], up_swapped, w_up, gain_mlp[None]],
            [],
            in_specs=[SMEM] + [VMEM] * 4,
            out_specs=[VMEM] * 3,
            out_shape=[
                sds((n_rows, 2 * hidden), F32),
                sds((n_rows, width), F32),
                sds((1, n_rows), F32),
            ],
            compiler_params=params(8),
        )
        grad_gain_up = gain_up[0]
    else:
        ordered = mine_theirs(up_sums[0], up_swapped)
        grad_out = jnp.concatenate([v[:, hidden:] for v in ordered], 1)
        sums_up = jnp.stack([v[:, :hidden].reshape(n_rows, chips, -1) for v in ordered], 2)
        sums_up = sums_up.reshape(n_rows, 2 * hidden)
        grad_w_up = sums_up * gain_two
        grad_gain_up = jnp.sum(sums_up * up_rows, 1)
    return (
        output[None],
        input_grad[None],
        grad_gain[0],
        grad_qkv,
        grad_out,
        grad_gain_up,
        grad_w_up,
        grad_down,
    )


def solution(mesh):
    rows = P("batch", "stream", None)
    flat, split = P(ALL), P(ALL, None)
    return jax.shard_map(
        local,
        mesh=mesh,
        in_specs=(rows, rows, P("batch"), flat, split, split, flat, split, split),
        out_specs=(rows, rows, flat, split, split, flat, split, split),
        check_vma=False,
    )
```

```python
import functools
import math
import types

import jax
import jax.numpy as jnp
from jax import lax
from jax.experimental import pallas as pl
from jax.experimental.pallas import tpu as pltpu
from jax.sharding import PartitionSpec as P

HEAD_DIM = 64
EPSILON = 1e-05
MASKED = -1e30
BF = jnp.bfloat16
F32 = jnp.float32
ALL = ("batch", "stream")
COSTS = dict(
    touch=0.1,
    halve=0.5,
    spread=0.5,
    prepare=0.5,
    norm=1.5,
    qkv=30.0,
    attend=30.0,
    out_weight=0.5,
    out=0.5,
    up=30.0,
    down=30.0,
    mlp_back=0.1,
    out_back=0.3,
    attend_back=12,
    qkv_weight=30.0,
    clean_back=30,
    mix=30,
    clean=0.5,
    qkv_back=30,
    input_back=30,
    finish=0.5,
    finish_up=30.0,
    join=0.4,
    result=0.05,
)
CHUNKS = 16
WIDE = 384
BLOCK = 128
TILE = 256
VMEM = pl.BlockSpec(memory_space=pltpu.VMEM)
SMEM = pl.BlockSpec(memory_space=pltpu.SMEM)
HBM = pl.BlockSpec(memory_space=pl.ANY)


def chip_bits(position, core):
    last = ((position >> 2) & 1) * (2 - core) ^ ((position >> 3) & 1) * (1 + core)
    return (position & 3) << 2 ^ last


def dot(a, b):
    return jnp.dot(a, b, preferred_element_type=F32)


def dot_nt(a, b):
    return lax.dot_general(a, b, (((1,), (1,)), ((), ())), preferred_element_type=F32)


def dot_tn(a, b):
    return lax.dot_general(a, b, (((0,), (0,)), ((), ())), preferred_element_type=F32)


def transposed(a):
    return a.astype(F32).T.astype(a.dtype)


def params(mib):
    return pltpu.CompilerParams(vmem_limit_bytes=mib << 20)


def cost(us):
    return pl.CostEstimate(flops=int(us * 1e9), bytes_accessed=1, transcendentals=0)


def sds(shape, dtype):
    return jax.ShapeDtypeStruct(shape, dtype)


TOKEN = sds((8, 128), F32)


def tied_call(
    kernel, inputs, ties=(), token=False, in_specs=None, out_specs=None, out_shape=None, **options
):
    n_in, n_ties = len(inputs), len(ties)
    name = getattr(kernel, "func", kernel).__name__
    options["cost_estimate"] = cost(COSTS[name[: -len("_kernel")]])
    n_out = len(out_shape)

    def body(*refs):
        rest = refs[n_in + n_ties :]
        if token:
            rest[n_out][...] = jnp.zeros(TOKEN.shape, F32)
            rest = rest[:n_out] + rest[n_out + 1 :]
        kernel(*refs[:n_in], *rest)

    if "grid" in options:
        small = pl.BlockSpec(TOKEN.shape, lambda *_: (0, 0))
    else:
        small = VMEM
    inputs = [
        pltpu.with_memory_space_constraint(value, pltpu.HBM) if spec is HBM else value
        for value, spec in zip(inputs, in_specs)
    ]
    out_shape = [
        pltpu.HBM(shape.shape, shape.dtype) if spec is HBM else shape
        for shape, spec in zip(out_shape, out_specs)
    ]
    call = pl.pallas_call(
        body,
        in_specs=list(in_specs) + [small] * n_ties,
        out_specs=list(out_specs) + [small] * token,
        out_shape=list(out_shape) + [TOKEN] * token,
        **options,
    )
    return call(*inputs, *ties)


def chunk_copies(bufs, ref, sems, info, store, first_column=0):
    rows = ref.shape[0] // CHUNKS
    copies = []
    for position in range(CHUNKS):
        chip = info[3] ^ chip_bits(position, info[0])
        buf = bufs[position // 8].at[position % 8, :, pl.ds(first_column, ref.shape[1])]
        view = ref.at[pl.ds(pl.multiple_of(chip * rows, 16), rows), :]
        pair = (view, buf) if store else (buf, view)
        copies.append(pltpu.make_async_copy(*pair, sems.at[position]))
    return copies


def start(copies):
    for copy in copies:
        copy.start()
    return copies


def wait(copies):
    for copy in copies:
        copy.wait()


def fetch(pairs, sems):
    return start([pltpu.make_async_copy(a, b, sems.at[i]) for i, (a, b) in enumerate(pairs)])


def normalize(values):
    centred = values - jnp.mean(values, -1, keepdims=True)
    inverse = lax.rsqrt(jnp.mean(centred * centred, -1, keepdims=True) + EPSILON)
    return centred * inverse, inverse


def norm_back(scaled, normed, inverse):
    return inverse * (
        scaled
        - jnp.mean(scaled, -1, keepdims=True)
        - normed * jnp.mean(scaled * normed, -1, keepdims=True)
    )


def swap_halves(values):
    lanes = lax.broadcasted_iota(jnp.int32, values.shape, 1)
    return jnp.where(
        lanes % HEAD_DIM < HEAD_DIM // 2,
        pltpu.roll(values, 128 - HEAD_DIM // 2, 1),
        pltpu.roll(values, HEAD_DIM // 2, 1),
    )


def turn(values, cosine, sine):
    return jnp.concatenate(
        [
            values[:, at : at + 128] * cosine + swap_halves(values[:, at : at + 128]) * sine
            for at in range(0, values.shape[1], 128)
        ],
        1,
    )


def prepare_kernel(info, w_ref, gain_ref, mine_ref, theirs_ref):
    count = w_ref.shape[0]
    half = mine_ref.shape[1] // 3
    square = (count, count)
    diagonal = lax.broadcasted_iota(jnp.int32, square, 0) == lax.broadcasted_iota(jnp.int32, square, 1)
    gain = gain_ref[...].astype(BF).astype(F32)
    gain = jnp.sum(jnp.where(diagonal, gain, 0.0), 1, keepdims=True)
    for i in range(3):
        for core, ref in ((info[0], mine_ref), (1 - info[0], theirs_ref)):
            part = w_ref[:, pl.ds(pl.multiple_of((2 * i + core) * half, 128), half)]
            ref[:, i * half : (i + 1) * half] = (part.astype(BF).astype(F32) * gain).astype(BF)


def finish_kernel(info, keep_ref, recv_ref, w_ref, gain_ref, out_ref, gain_out):
    count = w_ref.shape[0]
    half = keep_ref.shape[1] // 3
    square = (count, count)
    diagonal = lax.broadcasted_iota(jnp.int32, square, 0) == lax.broadcasted_iota(jnp.int32, square, 1)
    gain = gain_ref[...].astype(BF).astype(F32)
    gain = jnp.sum(jnp.where(diagonal, gain, 0.0), 1, keepdims=True)
    total = jnp.zeros((count, 1), F32)
    for i in range(3):
        for core, ref in ((info[0], keep_ref), (1 - info[0], recv_ref)):
            columns = pl.ds(pl.multiple_of((2 * i + core) * half, 128), half)
            part = ref[:, i * half : (i + 1) * half]
            weights = w_ref[:, columns].astype(BF).astype(F32)
            total += jnp.sum(part * weights, 1, keepdims=True)
            out_ref[:, columns] = part * gain
    gain_out[...] = jnp.sum(jnp.where(diagonal, total, 0.0), 0, keepdims=True)


def finish_up_kernel(info, keep_ref, recv_ref, w_ref, gain_ref, out_ref, wo_ref, gain_out):
    count, columns = w_ref.shape
    hidden, half = columns // 2, wo_ref.shape[1] // 2
    piece = hidden // CHUNKS
    square = (count, count)
    diagonal = lax.broadcasted_iota(jnp.int32, square, 0) == lax.broadcasted_iota(jnp.int32, square, 1)
    gain = gain_ref[...].astype(BF).astype(F32)
    gain = jnp.sum(jnp.where(diagonal, gain, 0.0), 1, keepdims=True)
    keep, recv = keep_ref[...], recv_ref[...]
    first = info[0] == 0
    zero, one = jnp.where(first, keep, recv), jnp.where(first, recv, keep)
    wo_ref[:, :half] = zero[:, hidden:]
    wo_ref[:, half:] = one[:, hidden:]
    parts = []
    for i in range(CHUNKS):
        parts += [zero[:, i * piece : (i + 1) * piece], one[:, i * piece : (i + 1) * piece]]
    sums = jnp.concatenate(parts, 1)
    weights = w_ref[...].astype(BF).astype(F32)
    total = jnp.sum(sums * weights, 1, keepdims=True)
    gain_out[...] = jnp.sum(jnp.where(diagonal, total, 0.0), 0, keepdims=True)
    out_ref[...] = sums * gain


def norm_kernel(info, x_own, x_oth, clean_own, clean_oth, a1_ref):
    core = info[0]
    rows = x_own.shape[0]
    for i, ref in enumerate((x_own, x_oth, clean_own, clean_oth)):
        slot = 2 * (i // 2) + (core if i % 2 == 0 else 1 - core)
        for at in range(0, rows, TILE):
            normed, _ = normalize(ref[at : at + TILE, :].astype(F32))
            a1_ref[slot, at : at + TILE, :] = normed.astype(BF)


def qkv_kernel(info, a1_ref, cos_ref, sin_ref, w0, w1, qkv_ref, w_ref, sems):
    half = a1_ref.shape[1] // 2
    step = pl.program_id(0)

    @pl.when(step == 0)
    def _():
        wait(start(chunk_copies((w0, w1), w_ref, sems, info, False)))

    low = a1_ref[...]
    cosine, sine = cos_ref[...], sin_ref[...]
    keys = dot(low, w_ref[:, half : 2 * half])
    qkv_ref[:, 2 * half :] = dot(low, w_ref[:, 2 * half : 3 * half]).astype(BF)
    qkv_ref[:, half : 2 * half] = turn(keys, cosine, sine).astype(BF)

    @pl.when(step < 2)
    def _():
        queries = dot(low, w_ref[:, :half])
        qkv_ref[:, :half] = turn(queries, cosine, sine).astype(BF)


def block_masks(info):
    noisy, block_len = info[1], info[2]
    keys = lax.broadcasted_iota(jnp.int32, (BLOCK, 2 * BLOCK), 0)
    queries = lax.broadcasted_iota(jnp.int32, (BLOCK, 2 * BLOCK), 1) % BLOCK
    starts = queries & (-block_len)
    clean_ok = keys < starts + jnp.where(noisy == 1, 0, block_len)
    local_ok = jnp.logical_and((keys & (-block_len)) == starts, noisy == 1)
    return clean_ok, local_ok


def by_head(values):
    wide = values.astype(F32)
    first = lax.broadcasted_iota(jnp.int32, wide.shape, 1) < HEAD_DIM
    return jnp.concatenate([jnp.where(first, wide, 0.0), jnp.where(first, 0.0, wide)], 0).astype(BF)


def head_quadrants(mixed):
    return jnp.concatenate([mixed[:HEAD_DIM, :BLOCK], mixed[HEAD_DIM : 2 * HEAD_DIM, BLOCK:]], 0)


def block_scores(queries, clean_keys, own_keys, at, masks):
    size = at + BLOCK
    scores = dot_nt(clean_keys[:size, :], queries)
    own = dot_nt(own_keys[at:size, :], queries)
    parts = [scores[:at]] if at else []
    parts.append(jnp.where(masks[0], scores[at:], MASKED))
    parts.append(jnp.where(masks[1], own, MASKED))
    return parts


def attend_kernel(info, q_ref, k_ref, v_ref, kc_ref, vc_ref, ot_ref, lse_ref):
    masks = block_masks(info)
    length = q_ref.shape[0]
    ones = jnp.ones((16, length), BF)
    own_vt = jnp.concatenate([transposed(v_ref[...]), ones], 0)
    clean_vt = jnp.concatenate([transposed(vc_ref[...]), ones], 0)

    def scores(at):
        queries = by_head(q_ref[at : at + BLOCK, :] * BF(HEAD_DIM**-0.5))
        return block_scores(queries, kc_ref, k_ref, at, masks)

    ready = scores(0)
    for at in range(0, length, BLOCK):
        parts = ready
        if at + BLOCK < length:
            ready = scores(at + BLOCK)
        size = at + BLOCK
        largest = functools.reduce(jnp.maximum, [jnp.max(part, 0, keepdims=True) for part in parts])
        weights = [jnp.exp(part - largest).astype(BF) for part in parts]
        mixed = dot(own_vt[:, at:size], weights[-1]) + dot(clean_vt[:, at:size], weights[-2])
        if at:
            mixed += dot(clean_vt[:, :at], weights[0])
        total = mixed[128:129]
        ot_ref[:, at:size] = head_quadrants(mixed / total).astype(BF)
        block = at // BLOCK
        lse_ref[block : block + 1, :] = largest + jnp.log(total)


def out_weight_kernel(info, w0, w1, out_ref):
    rows = w0.shape[1]
    for position in range(CHUNKS):
        chip = info[3] ^ chip_bits(position, info[0])
        source = (w0, w1)[position // 8]
        out_ref[pl.ds(pl.multiple_of(chip * rows, 16), rows), :] = source[position % 8]


def out_kernel(info, x_own, x_oth, ot_own, ot_oth, wo_own, wo_oth, r1_ref, a2_ref, ot_all, sum_ref):
    core = info[0]
    rows, width = x_own.shape
    half = width // 2
    mine = pl.ds(pl.multiple_of(core * half, 128), half)
    theirs = pl.ds(pl.multiple_of((1 - core) * half, 128), half)
    for i, x_ref in enumerate((x_own, x_oth)):
        at_rows = pl.ds(pl.multiple_of((core if i == 0 else 1 - core) * rows, 128), rows)
        ot_all[mine, :] = ot_own[:, at_rows]
        ot_all[theirs, :] = ot_oth[:, at_rows]
        merged = transposed(ot_all[...])
        sum_ref[:, mine] = dot(merged, wo_own[...])
        sum_ref[:, theirs] = dot(merged, wo_oth[...])
        for at in range(0, rows, TILE):
            r1 = x_ref[at : at + TILE, :].astype(F32) + sum_ref[at : at + TILE, :]
            if i == 0:
                r1_ref[at : at + TILE, :] = r1
            a2_ref[i * rows + at : i * rows + at + TILE, :] = normalize(r1)[0].astype(BF)


def gelu_parts(u):
    c = math.sqrt(2.0 / math.pi)
    square = u * u
    half = 0.5 + 0.5 * jnp.tanh(u * (c + (0.044715 * c) * square))
    active = u * half
    slope = half + active * (1.0 - half) * (2.0 * c + (6.0 * 0.044715 * c) * square)
    return active, slope


def up_kernel(
    info, a2_in, dy_own, dy_oth, w0, w1, g_out, slope_out, d0, d1,
    a2_ref, dy_ref, w_ref, g_ref, slope_ref, dw_ref, sems, w_sems, g_sems,
):
    rows = dy_own.shape[0]
    hidden = w_ref.shape[1]
    a2_copy = fetch([(a2_in, a2_ref)], sems)
    w_in = start(chunk_copies((w0, w1), w_ref, w_sems, info, False))
    dy_in = fetch(
        [(dy_own, dy_ref.at[pl.ds(0, rows)]), (dy_oth, dy_ref.at[pl.ds(rows, rows)])], sems.at[pl.ds(2, 2)]
    )
    wait(a2_copy + w_in)
    ready = dot(a2_ref[...], w_ref[:, :TILE])
    out = []
    for col in range(0, hidden, TILE):
        u = ready
        if col + TILE < hidden:
            ready = dot(a2_ref[...], w_ref[:, col + TILE : col + 2 * TILE])
        span = slice(col, col + TILE)
        active, slope = gelu_parts(u)
        g_ref[:, span] = active.astype(BF)
        slope_ref[:, span] = slope.astype(BF)
        at = pl.ds(col, TILE)
        pairs = [(g_ref.at[:, at], g_out.at[:, at]), (slope_ref.at[:, at], slope_out.at[:, at])]
        out += fetch(pairs, g_sems.at[pl.ds(2 * (col // TILE), 2)])
        if col == 0:
            wait(dy_in)
        dw_ref[span, :] = dot_tn(g_ref[:, span], dy_ref[...]).astype(BF)
    wait(out + start(chunk_copies((d0, d1), dw_ref, w_sems, info, True)))


def down_kernel(
    info, a2_in, slope_in, dy_own, dy_oth, u0, u1, w0, w1, e_ref, send_ref, d0, d1,
    a2_ref, dy_ref, slope_ref, up_ref, w_ref, du_ref, dw_ref, sems, w_sems, u_sems,
):
    rows = dy_own.shape[0]
    hidden = w_ref.shape[0]
    low, high = pl.ds(0, rows), pl.ds(rows, rows)
    dy_in = fetch([(dy_own, dy_ref.at[low]), (dy_oth, dy_ref.at[high])], sems)
    w_in = start(chunk_copies((w0, w1), w_ref, w_sems, info, False))
    slope_copy = fetch([(slope_in, slope_ref)], sems.at[pl.ds(2, 1)])
    a2_copy = fetch([(a2_in, a2_ref)], sems.at[pl.ds(3, 1)])
    u_in = start(chunk_copies((u0, u1), up_ref, u_sems, info, False))
    wait(dy_in + w_in)
    ready = dot_nt(dy_ref[...], w_ref[:TILE, :])
    for col in range(0, hidden, TILE):
        grad = ready
        if col + TILE < hidden:
            ready = dot_nt(dy_ref[...], w_ref[col + TILE : col + 2 * TILE, :])
        if col == 0:
            wait(slope_copy + a2_copy)
        span = slice(col, col + TILE)
        du_ref[:, span] = (grad * slope_ref[:, span].astype(F32)).astype(BF)
        dw_ref[:, span] = dot_tn(a2_ref[...], du_ref[:, span]).astype(BF)
    out = start(chunk_copies((d0, d1), dw_ref, w_sems, info, True))
    wait(u_in)
    send_ref[...] = dot_nt(du_ref[rows:, :], up_ref[...]).astype(BF)
    e_ref[...] = dot_nt(du_ref[:rows, :], up_ref[...])
    wait(out)


def mix_kernel(info, g_in, w0, w1, y_ref, send_ref, g_ref, w_ref, sems, w_sems):
    rows = y_ref.shape[0]
    w_in = start(chunk_copies((w0, w1), w_ref, w_sems, info, False))
    wait(fetch([(g_in, g_ref)], sems) + w_in)
    send_ref[...] = dot(g_ref[rows:, :], w_ref[...]).astype(BF)
    y_ref[...] = dot(g_ref[:rows, :], w_ref[...])


def join_kernel(column, *refs):
    out = refs[-1]
    at = 0
    for ref in refs[:-1]:
        out[at : at + ref.shape[0]] = ref[:, :, column : column + out.shape[2]]
        at += ref.shape[0]


def touch_kernel(_):
    pass


def halve_kernel(keep_ref, recv_ref, keep_out, send_out):
    count = keep_out.shape[0]
    for part in range(2):
        span = slice(part * count, (part + 1) * count)
        total = keep_ref[span].astype(F32) + recv_ref[span].astype(F32)
        (keep_out, send_out)[part][...] = total.astype(BF)


def spread_kernel(*refs):
    count = (len(refs) - 3) // 3
    totals, sends = refs[2 * count : 3 * count], refs[3 * count :]
    at = 0
    for i in range(count):
        keep_ref, recv_ref = refs[2 * i], refs[2 * i + 1]
        rows, columns = totals[i].shape
        for part in range(4):
            total = keep_ref[part].astype(F32) + recv_ref[part].astype(F32)
            if part == 0:
                totals[i][...] = total
                continue
            for j in range(columns // WIDE):
                low = at + j * rows
                sends[part - 1][low : low + rows, :] = total[:, j * WIDE : (j + 1) * WIDE].astype(BF)
        at += rows * columns // WIDE


def result_kernel(count, info, *refs):
    totals, arrived, outs = refs[:count], refs[count : count + 3], list(refs[count + 3 :])
    core = info[0]
    at = 0
    for i in range(count):
        rows, columns = totals[i].shape
        parts = []
        for j in range(columns // WIDE):
            low = at + j * rows
            part = totals[i][:, j * WIDE : (j + 1) * WIDE]
            for ref in arrived:
                part = part + ref[low : low + rows, :].astype(F32)
            parts.append(part)
        at += rows * columns // WIDE
        keep = outs.pop(0)
        if keep.shape[0] == rows:
            for j, part in enumerate(parts):
                keep[:, j * WIDE : (j + 1) * WIDE] = part
            continue
        send = outs.pop(0)
        half = rows // 2
        for j, part in enumerate(parts):
            span = slice(j * WIDE, (j + 1) * WIDE)
            keep[:, span] = jnp.where(core == 0, part[:half], part[half:])
            send[:, span] = jnp.where(core == 0, part[half:], part[:half])


def clean_kernel(own_ref, recv_ref, out_ref):
    out_ref[...] = (own_ref[...].astype(F32) + recv_ref[...].astype(F32)).astype(BF)


def mlp_back_kernel(r1_ref, e_ref, recv_ref, dy_ref, dr1_ref, dr_ref):
    normed, inverse = normalize(r1_ref[...])
    scaled = e_ref[...] + recv_ref[...].astype(F32)
    dr1 = dy_ref[...].astype(F32) + norm_back(scaled, normed, inverse)
    dr1_ref[...] = dr1
    dr_ref[...] = dr1.astype(BF)


def out_back_kernel(
    info, dr_own, dr_oth, wo_own, wo_oth, ot_own, ot_oth, _0, _1, do_ref, d0, d1, dr_all, ot_all, dwo_ref, sems
):
    core = info[0]
    rows, width = dr_own.shape
    half = width // 2
    mine = pl.ds(pl.multiple_of(core * half, 128), half)
    theirs = pl.ds(pl.multiple_of((1 - core) * half, 128), half)
    dr_all[pl.ds(pl.multiple_of(core * rows, 128), rows), :] = dr_own[...]
    dr_all[pl.ds(pl.multiple_of((1 - core) * rows, 128), rows), :] = dr_oth[...]
    ot_all[mine, :] = ot_own[...]
    ot_all[theirs, :] = ot_oth[...]
    dwo_ref[...] = dot(ot_all[...], dr_all[:, mine]).astype(BF)
    copies = start(chunk_copies((d0, d1), dwo_ref, sems, info, True, d0.shape[2] - half))
    grad = dot_nt(dr_all[:, mine], wo_own[mine, :])
    grad += dot_nt(dr_all[:, theirs], wo_oth[mine, :])
    do_ref[...] = grad.astype(BF)
    wait(copies)


def attend_back_kernel(
    info, q_ref, k_ref, v_ref, kc_ref, vc_ref, do_ref, ot_ref, lse_ref, cos_ref, sin_ref,
    dq_ref, dk_ref, dv_ref, dkc_ref, dvc_ref, dk_sum, dv_sum,
):
    masks = block_masks(info)
    length = q_ref.shape[0]
    dk_sum[...] = jnp.zeros_like(dk_sum)
    dv_sum[...] = jnp.zeros_like(dv_sum)
    scale = BF(HEAD_DIM**-0.5)
    own_kt = transposed(k_ref[...] * scale)
    clean_kt = transposed(kc_ref[...] * scale)

    def first_part(at):
        size = at + BLOCK
        queries = by_head(q_ref[at:size, :] * scale)
        grads = by_head(do_ref[at:size, :])
        parts = block_scores(queries, kc_ref, k_ref, at, masks)
        clean_dp = dot_nt(vc_ref[:size, :], grads)
        slopes = [clean_dp[:at]] if at else []
        slopes += [clean_dp[at:], dot_nt(v_ref[at:size, :], grads)]
        return queries, grads, parts, slopes

    ready = first_part(0)
    for at in range(0, length, BLOCK):
        queries, grads, parts, slopes = ready
        size = at + BLOCK
        if size < length:
            ready = first_part(size)
        block = at // BLOCK
        lse = lse_ref[block : block + 1, :]
        products = do_ref[at:size, :].astype(F32).T * ot_ref[:, at:size].astype(F32)
        shared = jnp.concatenate(
            [
                jnp.sum(products[:HEAD_DIM], 0, keepdims=True),
                jnp.sum(products[HEAD_DIM:], 0, keepdims=True),
            ],
            1,
        )
        weights = [jnp.exp(part - lse) for part in parts]
        changes = [(w * (s - shared)).astype(BF) for w, s in zip(weights, slopes)]
        weights = [w.astype(BF) for w in weights]
        dq = dot(own_kt[:, at:size], changes[-1]) + dot(clean_kt[:, at:size], changes[-2])
        dk = dot(changes[-1], queries)
        dv_ref[at:size, :] = dot(weights[-1], grads).astype(BF)
        dk_sum[at:size, :] += dot(changes[-2], queries)
        dv_sum[at:size, :] += dot(weights[-2], grads)
        if at:
            dq += dot(clean_kt[:, :at], changes[0])
            dk_sum[:at, :] += dot(changes[0], queries)
            dv_sum[:at, :] += dot(weights[0], grads)
        cosine, sine = cos_ref[at:size, :], -sin_ref[at:size, :]
        dq_ref[at:size, :] = turn(head_quadrants(dq).T, cosine, sine).astype(BF)
        dk_ref[at:size, :] = turn(dk, cosine, sine).astype(BF)
    dkc_ref[...] = turn(dk_sum[...], cos_ref[...], -sin_ref[...]).astype(BF)
    dvc_ref[...] = dv_sum[...].astype(BF)


def qkv_weight_kernel(
    info, dq_ref, dk_ref, dv_ref, dkc_ref, dvc_ref, a1_ref, d0, d1, dw_ref, sems
):
    length, half = dq_ref.shape
    own, clean = a1_ref.at[pl.ds(0, length)], a1_ref.at[pl.ds(length, length)]
    dw_ref[:, :half] = dot_tn(own[...], dq_ref[...]).astype(BF)
    for i, (a, b) in enumerate(((dk_ref, dkc_ref), (dv_ref, dvc_ref))):
        total = dot_tn(own[...], a[...]) + dot_tn(clean[...], b[...])
        dw_ref[:, (i + 1) * half : (i + 2) * half] = total.astype(BF)
    wait(start(chunk_copies((d0, d1), dw_ref, sems, info, True)))


def clean_back_kernel(info, dkc_ref, dvc_ref, w0, w1, keep_ref, send_ref, w_ref, sems):
    core = info[0]
    half = dkc_ref.shape[1]
    rows = keep_ref.shape[0]
    wait(start(chunk_copies((w0, w1), w_ref, sems, info, False)))
    w_k, w_v = [w_ref.at[:, pl.ds(i * half, half)] for i in (1, 2)]
    for at, ref in (((1 - core) * rows, send_ref), (core * rows, keep_ref)):
        span = pl.ds(pl.multiple_of(at, 128), rows)
        clean = dot_nt(dkc_ref[span, :], w_k[...]) + dot_nt(dvc_ref[span, :], w_v[...])
        ref[...] = clean.astype(BF)


def qkv_back_kernel(
    info, dq_ref, dk_ref, dv_ref, w0, w1, own_ref, send_ref, w_ref, sems
):
    core = info[0]
    half = dq_ref.shape[1]
    rows = own_ref.shape[0]
    wait(start(chunk_copies((w0, w1), w_ref, sems, info, False)))
    w_q, w_k, w_v = [w_ref.at[:, pl.ds(i * half, half)] for i in range(3)]
    for at, ref in (((1 - core) * rows, send_ref), (core * rows, own_ref)):
        span = pl.ds(pl.multiple_of(at, 128), rows)
        own = dot_nt(dq_ref[span, :], w_q[...]) + dot_nt(dk_ref[span, :], w_k[...])
        own += dot_nt(dv_ref[span, :], w_v[...])
        ref[...] = own.astype(ref.dtype)


def input_back_kernel(info, x_ref, own_ref, recv_ref, clean_ref, arrived_ref, dr1_ref, out_ref):
    for at in range(0, x_ref.shape[0], TILE):
        rows = slice(at, at + TILE)
        normed, inverse = normalize(x_ref[rows, :].astype(F32))
        scaled = own_ref[rows, :] + recv_ref[rows, :].astype(F32)
        clean = clean_ref[rows, :].astype(F32) + arrived_ref[rows, :].astype(F32)
        scaled += jnp.where(info[1] == 0, clean, 0.0)
        out_ref[rows, :] = (dr1_ref[rows, :] + norm_back(scaled, normed, inverse)).astype(BF)


def core_swap(value):
    size = lax.axis_size("stream")
    return lax.ppermute(value, "stream", [(i, i ^ 1) for i in range(size)])


def z_swap(value, bits):
    size = lax.axis_size("batch")
    return lax.ppermute(value, "batch", [(i, i ^ (bits << 1)) for i in range(size)])


def cross_swap(value, y_core):
    batches, streams = lax.axis_size("batch"), lax.axis_size("stream")
    pairs = []
    for b in range(batches):
        for s in range(streams):
            peer = (b ^ 1, s) if s % 2 == y_core else (b, s ^ 2)
            pairs.append((b * streams + s, peer[0] * streams + peer[1]))
    return lax.ppermute(value, ALL, pairs)


def chip_groups():
    batches, streams = lax.axis_size("batch"), lax.axis_size("stream")
    return [
        [b * streams + 2 * x + c for b in range(batches) for x in range(streams // 2)]
        for c in range(2)
    ]


def join(parts, ties=(), column=0, width=None):
    shape = (sum(part.shape[0] for part in parts), parts[0].shape[1], width or parts[0].shape[2])
    return tied_call(
        functools.partial(join_kernel, column),
        parts,
        ties,
        True,
        in_specs=[VMEM] * len(parts),
        out_specs=[VMEM],
        out_shape=[sds(shape, BF)],
        compiler_params=params(10),
    )


def arrival(value):
    if not is_fast():
        return []
    return tied_call(
        touch_kernel,
        [value],
        (),
        True,
        in_specs=[pl.BlockSpec(memory_space=pl.ANY)],
        out_specs=[],
        out_shape=[],
        compiler_params=params(4),
    )


def is_fast():
    return 2 * lax.axis_size("batch") == CHUNKS


class Gather:
    def __init__(self, chunk, first, *ties):
        self.chunk, self.first, self.tokens = chunk, first, []
        if is_fast():
            held = chunk[None]
            if ties:
                held, token = join([held], ties)
                self.tokens = [token]
            self.parts = [held] + [z_swap(held, bits) for bits in (1, 2, 3)]

    def middle(self, *ties):
        if is_fast():
            self.held, token = join(self.parts, ties)
            self.received = cross_swap(self.held, 0)
            self.tokens = [token]
        return self.tokens

    def last(self, *ties, column=0, width=None):
        if is_fast():
            held, token = join([self.held, self.received], ties, column, width)
            self.tokens = [token]
            return [held, cross_swap(held, 1)]
        width = width or self.chunk.shape[1]
        return slow_gather(self.chunk[:, column : column + width], self.first)


def slow_gather(chunk, first):
    full = lax.all_gather(chunk, ALL, axis=0, tiled=True, axis_index_groups=chip_groups())
    full = full.reshape(CHUNKS, -1, full.shape[1])
    orders = [jnp.stack([full[chip_bits(p, c)] for p in range(CHUNKS)]) for c in range(2)]
    full = jnp.where(first, *orders)
    return [full[:8], full[8:]]


def halve(keep, received, ties):
    count, rows, columns = keep.shape
    return tied_call(
        halve_kernel,
        [keep, received],
        ties,
        True,
        in_specs=[VMEM] * 2,
        out_specs=[VMEM] * 2,
        out_shape=[sds((count // 2, rows, columns), BF)] * 2,
        compiler_params=params(12),
    )


class ScatterSum:
    def __init__(self, keep, send, whole=False):
        self.keep, self.send, self.whole = keep, send, whole
        if is_fast():
            self.received = cross_swap(send, 1)

    def second(self, *ties):
        if not is_fast():
            return []
        self.keep, send, token = halve(self.keep, self.received, ties)
        self.received = cross_swap(send, 0)
        return [token]


def third(sums, ties):
    if not is_fast():
        return [], [], []
    shapes = [part.keep.shape[1:] for part in sums]
    rows = sum(rows * columns for rows, columns in shapes) // WIDE
    *out, token = tied_call(
        spread_kernel,
        [part for one in sums for part in (one.keep, one.received)],
        ties,
        True,
        in_specs=[VMEM] * (2 * len(sums)),
        out_specs=[VMEM] * (len(sums) + 3),
        out_shape=[sds(shape, F32) for shape in shapes] + [sds((rows, WIDE), BF)] * 3,
        compiler_params=params(16),
    )
    arrived = [z_swap(part, i + 1) for i, part in enumerate(out[len(sums) :])]
    return out[: len(sums)], arrived, [token]


def result(sums, totals, arrived, info, first, ties):
    if not is_fast():
        out = []
        for one in sums:
            total = slow_sum(one.keep, one.send, first)
            if one.whole:
                out.append(total)
            else:
                count = total.shape[0] // 2
                out.append(jnp.where(first, total[:count], total[count:]))
                out.append(jnp.where(first, total[count:], total[:count]))
        return out, []
    shapes = []
    for one, total in zip(sums, totals):
        rows, columns = total.shape
        shapes += [(rows, columns)] if one.whole else [(rows // 2, columns)] * 2
    *out, token = tied_call(
        functools.partial(result_kernel, len(sums)),
        [info, *totals, *arrived],
        ties,
        True,
        in_specs=[SMEM] + [VMEM] * (len(sums) + 3),
        out_specs=[VMEM] * len(shapes),
        out_shape=[sds(shape, F32) for shape in shapes],
        compiler_params=params(8),
    )
    return out, [token]


def slow_sum(keep, send, first):
    both = jnp.concatenate([keep, send], 0)
    orders = [[chip_bits(p, c) for p in range(CHUNKS)] for c in range(2)]
    sorted_ = [jnp.stack([both[orders[c].index(k)] for k in range(CHUNKS)]) for c in range(2)]
    full = jnp.where(first, *sorted_).astype(F32)
    full = full.reshape(-1, full.shape[2])
    return lax.psum_scatter(
        full, ALL, scatter_dimension=0, tiled=True, axis_index_groups=chip_groups()
    )


def local(tokens, cotangent, block_size, gain_attn, w_qkv, w_out, gain_mlp, w_up, w_down):
    rows, width = tokens.shape[1:]
    half = width // 2
    length = 2 * rows
    batches = lax.axis_size("batch")
    chips = 2 * batches
    hidden = w_up.shape[1] // 2
    stream, batch = lax.axis_index("stream"), lax.axis_index("batch")
    core, noisy = stream % 2, stream // 2
    me = batch * 2 + noisy if chips == CHUNKS else jnp.zeros_like(batch)
    info = jnp.stack([core, noisy, block_size[0], me]).astype(jnp.int32)
    first = core == 0
    n_rows = w_qkv.shape[0]

    def in_order(own, other, axis):
        return jnp.where(
            first, jnp.concatenate([own, other], axis), jnp.concatenate([other, own], axis)
        )

    def mine_theirs(zero, one):
        return jnp.where(first, zero, one), jnp.where(first, one, zero)

    gain_row = gain_attn[None]
    mine, theirs = tied_call(
        prepare_kernel,
        [info, w_qkv, gain_row],
        in_specs=[SMEM, VMEM, VMEM],
        out_specs=[VMEM] * 2,
        out_shape=[sds((n_rows, 3 * half), BF)] * 2,
        compiler_params=params(4),
    )
    chunk_one = in_order(mine, core_swap(theirs), 0)
    gain_two = gain_mlp.astype(BF).astype(F32)[:, None]
    up_rows = w_up.astype(BF).astype(F32)
    scaled = (up_rows * gain_two).astype(BF).reshape(n_rows, chips, 2, -1)
    out_low = w_out.astype(BF)
    mine, theirs = mine_theirs(
        *[
            jnp.concatenate(
                [scaled[:, :, c].reshape(n_rows, -1), out_low[:, c * half : (c + 1) * half]], 1
            )
            for c in range(2)
        ]
    )
    chunk_two = in_order(mine, core_swap(theirs), 0)

    x_own = tokens[0]
    dy_own = cotangent[0]
    streams = lax.axis_size("stream")
    to_noisy = [(i, i + streams // 2) for i in range(streams // 2)]
    to_clean = [(b, a) for a, b in to_noisy]
    arrived = lax.ppermute(x_own, "stream", to_noisy)
    clean_own = jnp.where(noisy == 1, arrived, x_own)
    x_oth = core_swap(x_own)
    clean_oth = core_swap(clean_own)
    dy_oth = core_swap(dy_own)

    places = jnp.arange(length, dtype=jnp.int32)
    lanes = jnp.arange(128, dtype=jnp.int32)
    half_dim = HEAD_DIM // 2
    frequency = jnp.exp(-math.log(10000.0) * (lanes % half_dim).astype(F32) / half_dim)
    angles = places.astype(F32)[:, None] * frequency[None, :]
    cosine = jnp.cos(angles)
    sine = jnp.where((lanes % HEAD_DIM < half_dim)[None], -jnp.sin(angles), jnp.sin(angles))

    sem = pltpu.SemaphoreType.DMA
    tokens = types.SimpleNamespace()
    tokens.tables = [cosine[:8], sine[:8]] if is_fast() else []
    tokens.two_chunk = [chunk_two[:8, :128].astype(F32)] if is_fast() else []

    one = Gather(chunk_one, first)
    tokens.one_middle = one.middle(*tokens.two_chunk)
    bufs_one = one.last(*tokens.tables)
    tokens.one_last = one.tokens
    two = Gather(chunk_two, first, *[*tokens.one_last])
    tokens.two_start = two.tokens
    a1, *tokens.norm = tied_call(
        norm_kernel,
        [info, x_own, x_oth, clean_own, clean_oth],
        [*tokens.two_start],
        True,
        in_specs=[SMEM] + [VMEM] * 4,
        out_specs=[VMEM],
        out_shape=[sds((4, rows, width), BF)],
        compiler_params=params(20),
    )
    a1 = a1.reshape(2 * length, width)

    tokens.two_middle = two.middle(*tokens.norm)

    qkv, *tokens.qkv = tied_call(
        qkv_kernel,
        [info, a1, cosine, sine, *bufs_one],
        [*tokens.norm] or tokens.norm,
        True,
        grid=(4,),
        in_specs=[
            SMEM,
            pl.BlockSpec((rows, width), lambda i: (i, 0)),
            pl.BlockSpec((rows, 128), lambda i: (i % 2, 0)),
            pl.BlockSpec((rows, 128), lambda i: (i % 2, 0)),
        ]
        + [HBM] * 2,
        out_specs=[pl.BlockSpec((rows, 3 * half), lambda i: (i, 0))],
        out_shape=[pltpu.HBM((2 * length, 3 * half), BF)],
        scratch_shapes=[pltpu.VMEM((width, 3 * half), BF), sem((CHUNKS,))],
        compiler_params=params(24),
    )
    qkv = pltpu.with_memory_space_constraint(qkv, pltpu.HBM)
    bufs_out = two.last(*tokens.qkv, column=hidden, width=half)
    tokens.out_last = two.tokens
    bufs_two = two.last(*tokens.qkv, width=hidden)
    tokens.two_last = two.tokens
    three = Gather(w_down.astype(BF), first, *[*tokens.two_last])
    tokens.three_start = three.tokens

    pairs = half // 128

    def pair_spec(part, clean):
        return pl.BlockSpec((length, 128), lambda p: (clean, part * pairs + p))

    qkv_specs = [pair_spec(0, 0), pair_spec(1, 0), pair_spec(2, 0), pair_spec(1, 1), pair_spec(2, 1)]
    lse_spec = pl.BlockSpec((length // BLOCK, 2 * BLOCK), lambda p: (p, 0))
    ot_own, lse, *tokens.attend = tied_call(
        attend_kernel,
        [info, qkv, qkv, qkv, qkv, qkv],
        [*tokens.out_last, *tokens.two_last, *tokens.three_start],
        True,
        grid=(pairs,),
        in_specs=[SMEM] + qkv_specs,
        out_specs=[pl.BlockSpec((128, length), lambda p: (p, 0)), lse_spec],
        out_shape=[sds((half, length), BF), sds((pairs * length // BLOCK, 2 * BLOCK), F32)],
        compiler_params=params(28),
    )
    ot_oth = core_swap(ot_own)
    tokens.three_middle = three.middle(*tokens.attend)

    (wo_own,) = tied_call(
        out_weight_kernel,
        [info, *bufs_out],
        [*tokens.three_middle],
        in_specs=[SMEM] + [VMEM] * 2,
        out_specs=[VMEM],
        out_shape=[sds((width, half), BF)],
        compiler_params=params(8),
    )
    wo_oth = core_swap(wo_own)

    r1, a2, *tokens.out = tied_call(
        out_kernel,
        [info, x_own, x_oth, ot_own, ot_oth, wo_own, wo_oth],
        [*tokens.three_middle],
        True,
        in_specs=[SMEM] + [VMEM] * 6,
        out_specs=[VMEM] * 2,
        out_shape=[sds((rows, width), F32), sds((length, width), BF)],
        scratch_shapes=[pltpu.VMEM((width, rows), BF), pltpu.VMEM((rows, width), F32)],
        compiler_params=params(20),
    )

    bufs_three = three.last(*tokens.out)
    tokens.three_last = three.tokens
    down_bufs = [sds((8, 2 * width // CHUNKS, width), BF)] * 2
    up_bufs = [sds((8, width // CHUNKS, hidden + half), BF)] * 2
    one_bufs = [sds((8, width // CHUNKS, 3 * half), BF)] * 2
    g, slope, *down_parts, up_done = tied_call(
        up_kernel,
        [info, a2, dy_own, dy_oth, *bufs_two],
        [*tokens.three_last],
        True,
        in_specs=[SMEM] + [HBM] * 5,
        out_specs=[HBM] * 4,
        out_shape=[sds((length, hidden), BF), sds((length, hidden), BF)] + down_bufs,
        scratch_shapes=[
            pltpu.VMEM((length, width), BF),
            pltpu.VMEM((length, width), BF),
            pltpu.VMEM((width, hidden), BF),
            pltpu.VMEM((length, hidden), BF),
            pltpu.VMEM((length, hidden), BF),
            pltpu.VMEM((hidden, width), BF),
            sem((4,)),
            sem((CHUNKS,)),
            sem((2 * hidden // TILE,)),
        ],
        compiler_params=params(44),
    )
    sum_down = ScatterSum(*down_parts, whole=True)
    tokens.up = [up_done]

    e_own, e_send, *up_parts, down_done = tied_call(
        down_kernel,
        [info, a2, slope, dy_own, dy_oth, *bufs_two, *bufs_three],
        [],
        True,
        in_specs=[SMEM] + [HBM] * 8,
        out_specs=[VMEM] * 2 + [HBM] * 2,
        out_shape=[sds((rows, width), F32), sds((rows, width), BF)] + up_bufs,
        scratch_shapes=[
            pltpu.VMEM((length, width), BF),
            pltpu.VMEM((length, width), BF),
            pltpu.VMEM((length, hidden), BF),
            pltpu.VMEM((width, hidden), BF),
            pltpu.VMEM((hidden, width), BF),
            pltpu.VMEM((length, hidden), BF),
            pltpu.VMEM((width, hidden), BF),
            sem((5,)),
            sem((CHUNKS,)),
            sem((CHUNKS,)),
        ],
        compiler_params=params(30),
    )
    e_recv = core_swap(e_send)
    tokens.down = [down_done]
    tokens.down_second = sum_down.second(*tokens.down)

    row_block = pl.BlockSpec((BLOCK, width), lambda i: (i, 0))
    dr1, dr_own = tied_call(
        mlp_back_kernel,
        [r1, e_own, e_recv, dy_own],
        [*tokens.down_second],
        grid=(rows // BLOCK,),
        in_specs=[row_block] * 4,
        out_specs=[row_block] * 2,
        out_shape=[sds((rows, width), F32), sds((rows, width), BF)],
        compiler_params=params(8),
    )
    dr_oth = core_swap(dr_own)

    do, *up_parts, out_back_done = tied_call(
        out_back_kernel,
        [info, dr_own, dr_oth, wo_own, wo_oth, ot_own, ot_oth, *up_parts],
        [],
        True,
        in_specs=[SMEM] + [VMEM] * 6 + [HBM] * 2,
        out_specs=[VMEM] + [HBM] * 2,
        out_shape=[sds((length, half), BF)] + up_bufs,
        input_output_aliases={7: 1, 8: 2},
        scratch_shapes=[
            pltpu.VMEM((length, width), BF),
            pltpu.VMEM((width, length), BF),
            pltpu.VMEM((width, half), BF),
            sem((CHUNKS,)),
        ],
        compiler_params=params(20),
    )
    sum_up = ScatterSum(*up_parts)
    tokens.out_back = [out_back_done]
    tokens.down_arrival = arrival(sum_down.received) if is_fast() else []
    down_totals, down_arrived, tokens.down_third = third([sum_down], [*tokens.out_back])

    column = pl.BlockSpec((length, 128), lambda p: (0, p))
    whole = pl.BlockSpec((length, 128), lambda p: (0, 0))
    *grads, attend_back_done = tied_call(
        attend_back_kernel,
        [info, qkv, qkv, qkv, qkv, qkv, do, ot_own, lse, cosine, sine],
        [*tokens.down_third],
        True,
        grid=(pairs,),
        in_specs=[SMEM]
        + qkv_specs
        + [column, pl.BlockSpec((128, length), lambda p: (p, 0)), lse_spec, whole, whole],
        out_specs=[column] * 5,
        out_shape=[sds((length, half), BF)] * 5,
        scratch_shapes=[pltpu.VMEM((length, 128), F32)] * 2,
        compiler_params=params(36),
    )
    tokens.attend_back = [attend_back_done]
    (grad_down,), tokens.down_result = result(
        [sum_down], down_totals, down_arrived, info, first, [*tokens.attend_back]
    )
    tokens.up_second = sum_up.second(*tokens.down_result)
    *one_parts, weight_done = tied_call(
        qkv_weight_kernel,
        [info, *grads, a1],
        [*tokens.up_second],
        True,
        in_specs=[SMEM] + [VMEM] * 6,
        out_specs=[HBM] * 2,
        out_shape=one_bufs,
        scratch_shapes=[pltpu.VMEM((width, 3 * half), BF), sem((CHUNKS,))],
        compiler_params=params(24),
    )
    sum_one = ScatterSum(*one_parts)
    tokens.weight = [weight_done]
    clean_part, clean_send, clean_back_done = tied_call(
        clean_back_kernel,
        [info, *grads[3:], *bufs_one],
        [*tokens.weight],
        True,
        in_specs=[SMEM] + [VMEM] * 2 + [HBM] * 2,
        out_specs=[VMEM] * 2,
        out_shape=[sds((rows, width), BF)] * 2,
        scratch_shapes=[pltpu.VMEM((width, 3 * half), BF), sem((CHUNKS,))],
        compiler_params=params(24),
    )
    tokens.clean_back = [clean_back_done]

    own_part, own_send, back_done = tied_call(
        qkv_back_kernel,
        [info, *grads[:3], *bufs_one],
        [*tokens.clean_back],
        True,
        in_specs=[SMEM] + [VMEM] * 3 + [HBM] * 2,
        out_specs=[VMEM] * 2,
        out_shape=[sds((rows, width), F32), sds((rows, width), BF)],
        scratch_shapes=[pltpu.VMEM((width, 3 * half), BF), sem((CHUNKS,))],
        compiler_params=params(24),
    )
    own_arrived = core_swap(own_send)
    tokens.qkv_back = [back_done]
    up_totals, up_arrived, tokens.up_third = third([sum_up], [*tokens.qkv_back])
    clean_swapped = core_swap(clean_send)
    tokens.one_second = sum_one.second(*tokens.up_third)

    (clean_total,) = tied_call(
        clean_kernel,
        [clean_part, clean_swapped],
        [*tokens.one_second],
        in_specs=[VMEM] * 2,
        out_specs=[VMEM],
        out_shape=[sds((rows, width), BF)],
        compiler_params=params(8),
    )
    clean_arrived = lax.ppermute(clean_total, "stream", to_clean)

    def mix():
        return tied_call(
            mix_kernel,
            [info, g, *bufs_three],
            [*tokens.one_second],
            True,
            in_specs=[SMEM] + [HBM] * 3,
            out_specs=[VMEM] * 2,
            out_shape=[sds((rows, width), F32), sds((rows, width), BF)],
            scratch_shapes=[
                pltpu.VMEM((length, hidden), BF),
                pltpu.VMEM((hidden, width), BF),
                sem((1,)),
                sem((CHUNKS,)),
            ],
            compiler_params=params(16),
        )

    y_own, y_send, *tokens.mix = mix()
    tokens.clean_arrival = arrival(clean_arrived)
    up_sums, tokens.up_result = result(
        [sum_up], up_totals, up_arrived, info, first, [*tokens.mix]
    )
    one_totals, one_arrived, tokens.one_third = third([sum_one], [*tokens.up_result])
    output = (r1 + y_own + core_swap(y_send).astype(F32)).astype(BF)

    input_grad, *tokens.input = tied_call(
        input_back_kernel,
        [info, x_own, own_part, own_arrived, clean_total, clean_arrived, dr1],
        [*tokens.one_third],
        True,
        in_specs=[SMEM] + [VMEM] * 6,
        out_specs=[VMEM],
        out_shape=[sds((rows, width), BF)],
        compiler_params=params(12),
    )
    one_sums, tokens.one_result = result(
        [sum_one], one_totals, one_arrived, info, first, [*tokens.input]
    )
    grad_qkv, grad_gain = tied_call(
        finish_kernel,
        [info, one_sums[0], core_swap(one_sums[1]), w_qkv, gain_row],
        in_specs=[SMEM] + [VMEM] * 4,
        out_specs=[VMEM] * 2,
        out_shape=[sds((n_rows, 3 * width), F32), sds((1, n_rows), F32)],
        compiler_params=params(4),
    )

    up_swapped = core_swap(up_sums[1])
    if is_fast():
        grad_w_up, grad_out, gain_up = tied_call(
            finish_up_kernel,
            [info, up_sums[0], up_swapped, w_up, gain_mlp[None]],
            [*tokens.one_result],
            in_specs=[SMEM] + [VMEM] * 4,
            out_specs=[VMEM] * 3,
            out_shape=[
                sds((n_rows, 2 * hidden), F32),
                sds((n_rows, width), F32),
                sds((1, n_rows), F32),
            ],
            compiler_params=params(8),
        )
        grad_gain_up = gain_up[0]
    else:
        ordered = mine_theirs(up_sums[0], up_swapped)
        grad_out = jnp.concatenate([v[:, hidden:] for v in ordered], 1)
        sums_up = jnp.stack([v[:, :hidden].reshape(n_rows, chips, -1) for v in ordered], 2)
        sums_up = sums_up.reshape(n_rows, 2 * hidden)
        grad_w_up = sums_up * gain_two
        grad_gain_up = jnp.sum(sums_up * up_rows, 1)
    return (
        output[None],
        input_grad[None],
        grad_gain[0],
        grad_qkv,
        grad_out,
        grad_gain_up,
        grad_w_up,
        grad_down,
    )


def solution(mesh):
    rows = P("batch", "stream", None)
    flat, split = P(ALL), P(ALL, None)
    return jax.shard_map(
        local,
        mesh=mesh,
        in_specs=(rows, rows, P("batch"), flat, split, split, flat, split, split),
        out_specs=(rows, rows, flat, split, split, flat, split, split),
        check_vma=False,
    )
```

```python
import functools
import math
import types

import jax
import jax.numpy as jnp
from jax import lax
from jax.experimental import pallas as pl
from jax.experimental.pallas import tpu as pltpu
from jax.sharding import PartitionSpec as P

HEAD_DIM = 64
EPSILON = 1e-05
MASKED = -1e30
BF = jnp.bfloat16
F32 = jnp.float32
ALL = ("batch", "stream")
COSTS = dict(
    touch=0.1,
    halve=12,
    spread=0.5,
    prepare=0.5,
    norm=1.5,
    qkv=30.0,
    attend=30.0,
    out_weight=0.5,
    out=0.5,
    up=0.1,
    down=0.5,
    mlp_back=0.1,
    out_back=0.3,
    attend_back=12,
    qkv_weight=30.0,
    clean_back=30,
    mix=30,
    clean=0.5,
    qkv_back=30,
    input_back=30,
    finish=0.5,
    finish_up=30.0,
    join=0.4,
    result=0.05,
)
CHUNKS = 16
WIDE = 384
BLOCK = 128
TILE = 256
VMEM = pl.BlockSpec(memory_space=pltpu.VMEM)
SMEM = pl.BlockSpec(memory_space=pltpu.SMEM)
HBM = pl.BlockSpec(memory_space=pl.ANY)


def chip_bits(position, core):
    last = ((position >> 2) & 1) * (2 - core) ^ ((position >> 3) & 1) * (1 + core)
    return (position & 3) << 2 ^ last


def dot(a, b):
    return jnp.dot(a, b, preferred_element_type=F32)


def dot_nt(a, b):
    return lax.dot_general(a, b, (((1,), (1,)), ((), ())), preferred_element_type=F32)


def dot_tn(a, b):
    return lax.dot_general(a, b, (((0,), (0,)), ((), ())), preferred_element_type=F32)


def transposed(a):
    return a.astype(F32).T.astype(a.dtype)


def params(mib):
    return pltpu.CompilerParams(vmem_limit_bytes=mib << 20)


def cost(us):
    return pl.CostEstimate(flops=int(us * 1e9), bytes_accessed=1, transcendentals=0)


def sds(shape, dtype):
    return jax.ShapeDtypeStruct(shape, dtype)


TOKEN = sds((8, 128), F32)


def tied_call(
    kernel, inputs, ties=(), token=False, in_specs=None, out_specs=None, out_shape=None, **options
):
    n_in, n_ties = len(inputs), len(ties)
    name = getattr(kernel, "func", kernel).__name__
    options["cost_estimate"] = cost(COSTS[name[: -len("_kernel")]])
    n_out = len(out_shape)

    def body(*refs):
        rest = refs[n_in + n_ties :]
        if token:
            rest[n_out][...] = jnp.zeros(TOKEN.shape, F32)
            rest = rest[:n_out] + rest[n_out + 1 :]
        kernel(*refs[:n_in], *rest)

    if "grid" in options:
        small = pl.BlockSpec(TOKEN.shape, lambda *_: (0, 0))
    else:
        small = VMEM
    inputs = [
        pltpu.with_memory_space_constraint(value, pltpu.HBM) if spec is HBM else value
        for value, spec in zip(inputs, in_specs)
    ]
    out_shape = [
        pltpu.HBM(shape.shape, shape.dtype) if spec is HBM else shape
        for shape, spec in zip(out_shape, out_specs)
    ]
    call = pl.pallas_call(
        body,
        in_specs=list(in_specs) + [small] * n_ties,
        out_specs=list(out_specs) + [small] * token,
        out_shape=list(out_shape) + [TOKEN] * token,
        **options,
    )
    return call(*inputs, *ties)


def chunk_copies(bufs, ref, sems, info, store, first_column=0):
    rows = ref.shape[0] // CHUNKS
    copies = []
    for position in range(CHUNKS):
        chip = info[3] ^ chip_bits(position, info[0])
        buf = bufs[position // 8].at[position % 8, :, pl.ds(first_column, ref.shape[1])]
        view = ref.at[pl.ds(pl.multiple_of(chip * rows, 16), rows), :]
        pair = (view, buf) if store else (buf, view)
        copies.append(pltpu.make_async_copy(*pair, sems.at[position]))
    return copies


def start(copies):
    for copy in copies:
        copy.start()
    return copies


def wait(copies):
    for copy in copies:
        copy.wait()


def fetch(pairs, sems):
    return start([pltpu.make_async_copy(a, b, sems.at[i]) for i, (a, b) in enumerate(pairs)])


def normalize(values):
    centred = values - jnp.mean(values, -1, keepdims=True)
    inverse = lax.rsqrt(jnp.mean(centred * centred, -1, keepdims=True) + EPSILON)
    return centred * inverse, inverse


def norm_back(scaled, normed, inverse):
    return inverse * (
        scaled
        - jnp.mean(scaled, -1, keepdims=True)
        - normed * jnp.mean(scaled * normed, -1, keepdims=True)
    )


def swap_halves(values):
    lanes = lax.broadcasted_iota(jnp.int32, values.shape, 1)
    return jnp.where(
        lanes % HEAD_DIM < HEAD_DIM // 2,
        pltpu.roll(values, 128 - HEAD_DIM // 2, 1),
        pltpu.roll(values, HEAD_DIM // 2, 1),
    )


def turn(values, cosine, sine):
    return jnp.concatenate(
        [
            values[:, at : at + 128] * cosine + swap_halves(values[:, at : at + 128]) * sine
            for at in range(0, values.shape[1], 128)
        ],
        1,
    )


def prepare_kernel(info, w_ref, gain_ref, mine_ref, theirs_ref):
    count = w_ref.shape[0]
    half = mine_ref.shape[1] // 3
    square = (count, count)
    diagonal = lax.broadcasted_iota(jnp.int32, square, 0) == lax.broadcasted_iota(jnp.int32, square, 1)
    gain = gain_ref[...].astype(BF).astype(F32)
    gain = jnp.sum(jnp.where(diagonal, gain, 0.0), 1, keepdims=True)
    for i in range(3):
        for core, ref in ((info[0], mine_ref), (1 - info[0], theirs_ref)):
            part = w_ref[:, pl.ds(pl.multiple_of((2 * i + core) * half, 128), half)]
            ref[:, i * half : (i + 1) * half] = (part.astype(BF).astype(F32) * gain).astype(BF)


def finish_kernel(info, keep_ref, recv_ref, w_ref, gain_ref, out_ref, gain_out):
    count = w_ref.shape[0]
    half = keep_ref.shape[1] // 3
    square = (count, count)
    diagonal = lax.broadcasted_iota(jnp.int32, square, 0) == lax.broadcasted_iota(jnp.int32, square, 1)
    gain = gain_ref[...].astype(BF).astype(F32)
    gain = jnp.sum(jnp.where(diagonal, gain, 0.0), 1, keepdims=True)
    total = jnp.zeros((count, 1), F32)
    for i in range(3):
        for core, ref in ((info[0], keep_ref), (1 - info[0], recv_ref)):
            columns = pl.ds(pl.multiple_of((2 * i + core) * half, 128), half)
            part = ref[:, i * half : (i + 1) * half]
            weights = w_ref[:, columns].astype(BF).astype(F32)
            total += jnp.sum(part * weights, 1, keepdims=True)
            out_ref[:, columns] = part * gain
    gain_out[...] = jnp.sum(jnp.where(diagonal, total, 0.0), 0, keepdims=True)


def finish_up_kernel(info, keep_ref, recv_ref, w_ref, gain_ref, out_ref, wo_ref, gain_out):
    count, columns = w_ref.shape
    hidden, half = columns // 2, wo_ref.shape[1] // 2
    piece = hidden // CHUNKS
    square = (count, count)
    diagonal = lax.broadcasted_iota(jnp.int32, square, 0) == lax.broadcasted_iota(jnp.int32, square, 1)
    gain = gain_ref[...].astype(BF).astype(F32)
    gain = jnp.sum(jnp.where(diagonal, gain, 0.0), 1, keepdims=True)
    keep, recv = keep_ref[...], recv_ref[...]
    first = info[0] == 0
    zero, one = jnp.where(first, keep, recv), jnp.where(first, recv, keep)
    wo_ref[:, :half] = zero[:, hidden:]
    wo_ref[:, half:] = one[:, hidden:]
    parts = []
    for i in range(CHUNKS):
        parts += [zero[:, i * piece : (i + 1) * piece], one[:, i * piece : (i + 1) * piece]]
    sums = jnp.concatenate(parts, 1)
    weights = w_ref[...].astype(BF).astype(F32)
    total = jnp.sum(sums * weights, 1, keepdims=True)
    gain_out[...] = jnp.sum(jnp.where(diagonal, total, 0.0), 0, keepdims=True)
    out_ref[...] = sums * gain


def norm_kernel(info, x_own, x_oth, clean_own, clean_oth, a1_ref):
    core = info[0]
    rows = x_own.shape[0]
    for i, ref in enumerate((x_own, x_oth, clean_own, clean_oth)):
        slot = 2 * (i // 2) + (core if i % 2 == 0 else 1 - core)
        for at in range(0, rows, TILE):
            normed, _ = normalize(ref[at : at + TILE, :].astype(F32))
            a1_ref[slot, at : at + TILE, :] = normed.astype(BF)


def qkv_kernel(info, a1_ref, cos_ref, sin_ref, w0, w1, qkv_ref, w_ref, sems):
    half = a1_ref.shape[1] // 2
    step = pl.program_id(0)

    @pl.when(step == 0)
    def _():
        wait(start(chunk_copies((w0, w1), w_ref, sems, info, False)))

    low = a1_ref[...]
    cosine, sine = cos_ref[...], sin_ref[...]
    keys = dot(low, w_ref[:, half : 2 * half])
    qkv_ref[:, 2 * half :] = dot(low, w_ref[:, 2 * half : 3 * half]).astype(BF)
    qkv_ref[:, half : 2 * half] = turn(keys, cosine, sine).astype(BF)

    @pl.when(step < 2)
    def _():
        queries = dot(low, w_ref[:, :half])
        qkv_ref[:, :half] = turn(queries, cosine, sine).astype(BF)


def block_masks(info):
    noisy, block_len = info[1], info[2]
    keys = lax.broadcasted_iota(jnp.int32, (BLOCK, 2 * BLOCK), 0)
    queries = lax.broadcasted_iota(jnp.int32, (BLOCK, 2 * BLOCK), 1) % BLOCK
    starts = queries & (-block_len)
    clean_ok = keys < starts + jnp.where(noisy == 1, 0, block_len)
    local_ok = jnp.logical_and((keys & (-block_len)) == starts, noisy == 1)
    return clean_ok, local_ok


def by_head(values):
    wide = values.astype(F32)
    first = lax.broadcasted_iota(jnp.int32, wide.shape, 1) < HEAD_DIM
    return jnp.concatenate([jnp.where(first, wide, 0.0), jnp.where(first, 0.0, wide)], 0).astype(BF)


def head_quadrants(mixed):
    return jnp.concatenate([mixed[:HEAD_DIM, :BLOCK], mixed[HEAD_DIM : 2 * HEAD_DIM, BLOCK:]], 0)


def block_scores(queries, clean_keys, own_keys, at, masks):
    size = at + BLOCK
    scores = dot_nt(clean_keys[:size, :], queries)
    own = dot_nt(own_keys[at:size, :], queries)
    parts = [scores[:at]] if at else []
    parts.append(jnp.where(masks[0], scores[at:], MASKED))
    parts.append(jnp.where(masks[1], own, MASKED))
    return parts


def attend_kernel(info, q_ref, k_ref, v_ref, kc_ref, vc_ref, ot_ref, lse_ref):
    masks = block_masks(info)
    length = q_ref.shape[0]
    ones = jnp.ones((16, length), BF)
    own_vt = jnp.concatenate([transposed(v_ref[...]), ones], 0)
    clean_vt = jnp.concatenate([transposed(vc_ref[...]), ones], 0)

    def scores(at):
        queries = by_head(q_ref[at : at + BLOCK, :] * BF(HEAD_DIM**-0.5))
        return block_scores(queries, kc_ref, k_ref, at, masks)

    ready = scores(0)
    for at in range(0, length, BLOCK):
        parts = ready
        if at + BLOCK < length:
            ready = scores(at + BLOCK)
        size = at + BLOCK
        largest = functools.reduce(jnp.maximum, [jnp.max(part, 0, keepdims=True) for part in parts])
        weights = [jnp.exp(part - largest).astype(BF) for part in parts]
        mixed = dot(own_vt[:, at:size], weights[-1]) + dot(clean_vt[:, at:size], weights[-2])
        if at:
            mixed += dot(clean_vt[:, :at], weights[0])
        total = mixed[128:129]
        ot_ref[:, at:size] = head_quadrants(mixed / total).astype(BF)
        block = at // BLOCK
        lse_ref[block : block + 1, :] = largest + jnp.log(total)


def out_weight_kernel(info, w0, w1, out_ref):
    rows = w0.shape[1]
    for position in range(CHUNKS):
        chip = info[3] ^ chip_bits(position, info[0])
        source = (w0, w1)[position // 8]
        out_ref[pl.ds(pl.multiple_of(chip * rows, 16), rows), :] = source[position % 8]


def out_kernel(info, x_own, x_oth, ot_own, ot_oth, wo_own, wo_oth, r1_ref, a2_ref, ot_all, sum_ref):
    core = info[0]
    rows, width = x_own.shape
    half = width // 2
    mine = pl.ds(pl.multiple_of(core * half, 128), half)
    theirs = pl.ds(pl.multiple_of((1 - core) * half, 128), half)
    for i, x_ref in enumerate((x_own, x_oth)):
        at_rows = pl.ds(pl.multiple_of((core if i == 0 else 1 - core) * rows, 128), rows)
        ot_all[mine, :] = ot_own[:, at_rows]
        ot_all[theirs, :] = ot_oth[:, at_rows]
        merged = transposed(ot_all[...])
        sum_ref[:, mine] = dot(merged, wo_own[...])
        sum_ref[:, theirs] = dot(merged, wo_oth[...])
        for at in range(0, rows, TILE):
            r1 = x_ref[at : at + TILE, :].astype(F32) + sum_ref[at : at + TILE, :]
            if i == 0:
                r1_ref[at : at + TILE, :] = r1
            a2_ref[i * rows + at : i * rows + at + TILE, :] = normalize(r1)[0].astype(BF)


def gelu_parts(u):
    c = math.sqrt(2.0 / math.pi)
    square = u * u
    half = 0.5 + 0.5 * jnp.tanh(u * (c + (0.044715 * c) * square))
    active = u * half
    slope = half + active * (1.0 - half) * (2.0 * c + (6.0 * 0.044715 * c) * square)
    return active, slope


def up_kernel(
    info, a2_in, dy_own, dy_oth, w0, w1, g_out, slope_out, d0, d1,
    a2_ref, dy_ref, w_ref, g_ref, slope_ref, dw_ref, sems, w_sems, g_sems,
):
    rows = dy_own.shape[0]
    hidden = w_ref.shape[1]
    a2_copy = fetch([(a2_in, a2_ref)], sems)
    w_in = start(chunk_copies((w0, w1), w_ref, w_sems, info, False))
    dy_in = fetch(
        [(dy_own, dy_ref.at[pl.ds(0, rows)]), (dy_oth, dy_ref.at[pl.ds(rows, rows)])], sems.at[pl.ds(2, 2)]
    )
    wait(a2_copy + w_in)
    ready = dot(a2_ref[...], w_ref[:, :TILE])
    out = []
    for col in range(0, hidden, TILE):
        u = ready
        if col + TILE < hidden:
            ready = dot(a2_ref[...], w_ref[:, col + TILE : col + 2 * TILE])
        span = slice(col, col + TILE)
        active, slope = gelu_parts(u)
        g_ref[:, span] = active.astype(BF)
        slope_ref[:, span] = slope.astype(BF)
        at = pl.ds(col, TILE)
        pairs = [(g_ref.at[:, at], g_out.at[:, at]), (slope_ref.at[:, at], slope_out.at[:, at])]
        out += fetch(pairs, g_sems.at[pl.ds(2 * (col // TILE), 2)])
        if col == 0:
            wait(dy_in)
        dw_ref[span, :] = dot_tn(g_ref[:, span], dy_ref[...]).astype(BF)
    wait(out + start(chunk_copies((d0, d1), dw_ref, w_sems, info, True)))


def down_kernel(
    info, a2_in, slope_in, dy_own, dy_oth, u0, u1, w0, w1, e_ref, send_ref, d0, d1,
    a2_ref, dy_ref, slope_ref, up_ref, w_ref, du_ref, dw_ref, sems, w_sems, u_sems,
):
    rows = dy_own.shape[0]
    hidden = w_ref.shape[0]
    low, high = pl.ds(0, rows), pl.ds(rows, rows)
    dy_in = fetch([(dy_own, dy_ref.at[low]), (dy_oth, dy_ref.at[high])], sems)
    w_in = start(chunk_copies((w0, w1), w_ref, w_sems, info, False))
    slope_copy = fetch([(slope_in, slope_ref)], sems.at[pl.ds(2, 1)])
    a2_copy = fetch([(a2_in, a2_ref)], sems.at[pl.ds(3, 1)])
    u_in = start(chunk_copies((u0, u1), up_ref, u_sems, info, False))
    wait(dy_in + w_in)
    ready = dot_nt(dy_ref[...], w_ref[:TILE, :])
    for col in range(0, hidden, TILE):
        grad = ready
        if col + TILE < hidden:
            ready = dot_nt(dy_ref[...], w_ref[col + TILE : col + 2 * TILE, :])
        if col == 0:
            wait(slope_copy + a2_copy)
        span = slice(col, col + TILE)
        du_ref[:, span] = (grad * slope_ref[:, span].astype(F32)).astype(BF)
        dw_ref[:, span] = dot_tn(a2_ref[...], du_ref[:, span]).astype(BF)
    out = start(chunk_copies((d0, d1), dw_ref, w_sems, info, True))
    wait(u_in)
    send_ref[...] = dot_nt(du_ref[rows:, :], up_ref[...]).astype(BF)
    e_ref[...] = dot_nt(du_ref[:rows, :], up_ref[...])
    wait(out)


def mix_kernel(info, g_in, w0, w1, y_ref, send_ref, g_ref, w_ref, sems, w_sems):
    rows = y_ref.shape[0]
    w_in = start(chunk_copies((w0, w1), w_ref, w_sems, info, False))
    wait(fetch([(g_in, g_ref)], sems) + w_in)
    send_ref[...] = dot(g_ref[rows:, :], w_ref[...]).astype(BF)
    y_ref[...] = dot(g_ref[:rows, :], w_ref[...])


def join_kernel(column, *refs):
    out = refs[-1]
    at = 0
    for ref in refs[:-1]:
        out[at : at + ref.shape[0]] = ref[:, :, column : column + out.shape[2]]
        at += ref.shape[0]


def touch_kernel(_):
    pass


def halve_kernel(keep_ref, recv_ref, keep_out, send_out):
    count = keep_out.shape[0]
    for part in range(2):
        span = slice(part * count, (part + 1) * count)
        total = keep_ref[span].astype(F32) + recv_ref[span].astype(F32)
        (keep_out, send_out)[part][...] = total.astype(BF)


def spread_kernel(*refs):
    count = (len(refs) - 3) // 3
    totals, sends = refs[2 * count : 3 * count], refs[3 * count :]
    at = 0
    for i in range(count):
        keep_ref, recv_ref = refs[2 * i], refs[2 * i + 1]
        rows, columns = totals[i].shape
        for part in range(4):
            total = keep_ref[part].astype(F32) + recv_ref[part].astype(F32)
            if part == 0:
                totals[i][...] = total
                continue
            for j in range(columns // WIDE):
                low = at + j * rows
                sends[part - 1][low : low + rows, :] = total[:, j * WIDE : (j + 1) * WIDE].astype(BF)
        at += rows * columns // WIDE


def result_kernel(count, info, *refs):
    totals, arrived, outs = refs[:count], refs[count : count + 3], list(refs[count + 3 :])
    core = info[0]
    at = 0
    for i in range(count):
        rows, columns = totals[i].shape
        parts = []
        for j in range(columns // WIDE):
            low = at + j * rows
            part = totals[i][:, j * WIDE : (j + 1) * WIDE]
            for ref in arrived:
                part = part + ref[low : low + rows, :].astype(F32)
            parts.append(part)
        at += rows * columns // WIDE
        keep = outs.pop(0)
        if keep.shape[0] == rows:
            for j, part in enumerate(parts):
                keep[:, j * WIDE : (j + 1) * WIDE] = part
            continue
        send = outs.pop(0)
        half = rows // 2
        for j, part in enumerate(parts):
            span = slice(j * WIDE, (j + 1) * WIDE)
            keep[:, span] = jnp.where(core == 0, part[:half], part[half:])
            send[:, span] = jnp.where(core == 0, part[half:], part[:half])


def clean_kernel(own_ref, recv_ref, out_ref):
    out_ref[...] = (own_ref[...].astype(F32) + recv_ref[...].astype(F32)).astype(BF)


def mlp_back_kernel(r1_ref, e_ref, recv_ref, dy_ref, dr1_ref, dr_ref):
    normed, inverse = normalize(r1_ref[...])
    scaled = e_ref[...] + recv_ref[...].astype(F32)
    dr1 = dy_ref[...].astype(F32) + norm_back(scaled, normed, inverse)
    dr1_ref[...] = dr1
    dr_ref[...] = dr1.astype(BF)


def out_back_kernel(
    info, dr_own, dr_oth, wo_own, wo_oth, ot_own, ot_oth, _0, _1, do_ref, d0, d1, dr_all, ot_all, dwo_ref, sems
):
    core = info[0]
    rows, width = dr_own.shape
    half = width // 2
    mine = pl.ds(pl.multiple_of(core * half, 128), half)
    theirs = pl.ds(pl.multiple_of((1 - core) * half, 128), half)
    dr_all[pl.ds(pl.multiple_of(core * rows, 128), rows), :] = dr_own[...]
    dr_all[pl.ds(pl.multiple_of((1 - core) * rows, 128), rows), :] = dr_oth[...]
    ot_all[mine, :] = ot_own[...]
    ot_all[theirs, :] = ot_oth[...]
    dwo_ref[...] = dot(ot_all[...], dr_all[:, mine]).astype(BF)
    copies = start(chunk_copies((d0, d1), dwo_ref, sems, info, True, d0.shape[2] - half))
    grad = dot_nt(dr_all[:, mine], wo_own[mine, :])
    grad += dot_nt(dr_all[:, theirs], wo_oth[mine, :])
    do_ref[...] = grad.astype(BF)
    wait(copies)


def attend_back_kernel(
    info, q_ref, k_ref, v_ref, kc_ref, vc_ref, do_ref, ot_ref, lse_ref, cos_ref, sin_ref,
    dq_ref, dk_ref, dv_ref, dkc_ref, dvc_ref, dk_sum, dv_sum,
):
    masks = block_masks(info)
    length = q_ref.shape[0]
    dk_sum[...] = jnp.zeros_like(dk_sum)
    dv_sum[...] = jnp.zeros_like(dv_sum)
    scale = BF(HEAD_DIM**-0.5)
    own_kt = transposed(k_ref[...] * scale)
    clean_kt = transposed(kc_ref[...] * scale)

    def first_part(at):
        size = at + BLOCK
        queries = by_head(q_ref[at:size, :] * scale)
        grads = by_head(do_ref[at:size, :])
        parts = block_scores(queries, kc_ref, k_ref, at, masks)
        clean_dp = dot_nt(vc_ref[:size, :], grads)
        slopes = [clean_dp[:at]] if at else []
        slopes += [clean_dp[at:], dot_nt(v_ref[at:size, :], grads)]
        return queries, grads, parts, slopes

    ready = first_part(0)
    for at in range(0, length, BLOCK):
        queries, grads, parts, slopes = ready
        size = at + BLOCK
        if size < length:
            ready = first_part(size)
        block = at // BLOCK
        lse = lse_ref[block : block + 1, :]
        products = do_ref[at:size, :].astype(F32).T * ot_ref[:, at:size].astype(F32)
        shared = jnp.concatenate(
            [
                jnp.sum(products[:HEAD_DIM], 0, keepdims=True),
                jnp.sum(products[HEAD_DIM:], 0, keepdims=True),
            ],
            1,
        )
        weights = [jnp.exp(part - lse) for part in parts]
        changes = [(w * (s - shared)).astype(BF) for w, s in zip(weights, slopes)]
        weights = [w.astype(BF) for w in weights]
        dq = dot(own_kt[:, at:size], changes[-1]) + dot(clean_kt[:, at:size], changes[-2])
        dk = dot(changes[-1], queries)
        dv_ref[at:size, :] = dot(weights[-1], grads).astype(BF)
        dk_sum[at:size, :] += dot(changes[-2], queries)
        dv_sum[at:size, :] += dot(weights[-2], grads)
        if at:
            dq += dot(clean_kt[:, :at], changes[0])
            dk_sum[:at, :] += dot(changes[0], queries)
            dv_sum[:at, :] += dot(weights[0], grads)
        cosine, sine = cos_ref[at:size, :], -sin_ref[at:size, :]
        dq_ref[at:size, :] = turn(head_quadrants(dq).T, cosine, sine).astype(BF)
        dk_ref[at:size, :] = turn(dk, cosine, sine).astype(BF)
    dkc_ref[...] = turn(dk_sum[...], cos_ref[...], -sin_ref[...]).astype(BF)
    dvc_ref[...] = dv_sum[...].astype(BF)


def qkv_weight_kernel(
    info, dq_ref, dk_ref, dv_ref, dkc_ref, dvc_ref, a1_ref, d0, d1, dw_ref, sems
):
    length, half = dq_ref.shape
    own, clean = a1_ref.at[pl.ds(0, length)], a1_ref.at[pl.ds(length, length)]
    dw_ref[:, :half] = dot_tn(own[...], dq_ref[...]).astype(BF)
    for i, (a, b) in enumerate(((dk_ref, dkc_ref), (dv_ref, dvc_ref))):
        total = dot_tn(own[...], a[...]) + dot_tn(clean[...], b[...])
        dw_ref[:, (i + 1) * half : (i + 2) * half] = total.astype(BF)
    wait(start(chunk_copies((d0, d1), dw_ref, sems, info, True)))


def clean_back_kernel(info, dkc_ref, dvc_ref, w0, w1, keep_ref, send_ref, w_ref, sems):
    core = info[0]
    half = dkc_ref.shape[1]
    rows = keep_ref.shape[0]
    wait(start(chunk_copies((w0, w1), w_ref, sems, info, False)))
    w_k, w_v = [w_ref.at[:, pl.ds(i * half, half)] for i in (1, 2)]
    for at, ref in (((1 - core) * rows, send_ref), (core * rows, keep_ref)):
        span = pl.ds(pl.multiple_of(at, 128), rows)
        clean = dot_nt(dkc_ref[span, :], w_k[...]) + dot_nt(dvc_ref[span, :], w_v[...])
        ref[...] = clean.astype(BF)


def qkv_back_kernel(
    info, dq_ref, dk_ref, dv_ref, w0, w1, own_ref, send_ref, w_ref, sems
):
    core = info[0]
    half = dq_ref.shape[1]
    rows = own_ref.shape[0]
    wait(start(chunk_copies((w0, w1), w_ref, sems, info, False)))
    w_q, w_k, w_v = [w_ref.at[:, pl.ds(i * half, half)] for i in range(3)]
    for at, ref in (((1 - core) * rows, send_ref), (core * rows, own_ref)):
        span = pl.ds(pl.multiple_of(at, 128), rows)
        own = dot_nt(dq_ref[span, :], w_q[...]) + dot_nt(dk_ref[span, :], w_k[...])
        own += dot_nt(dv_ref[span, :], w_v[...])
        ref[...] = own.astype(ref.dtype)


def input_back_kernel(info, x_ref, own_ref, recv_ref, clean_ref, arrived_ref, dr1_ref, out_ref):
    for at in range(0, x_ref.shape[0], TILE):
        rows = slice(at, at + TILE)
        normed, inverse = normalize(x_ref[rows, :].astype(F32))
        scaled = own_ref[rows, :] + recv_ref[rows, :].astype(F32)
        clean = clean_ref[rows, :].astype(F32) + arrived_ref[rows, :].astype(F32)
        scaled += jnp.where(info[1] == 0, clean, 0.0)
        out_ref[rows, :] = (dr1_ref[rows, :] + norm_back(scaled, normed, inverse)).astype(BF)


def core_swap(value):
    size = lax.axis_size("stream")
    return lax.ppermute(value, "stream", [(i, i ^ 1) for i in range(size)])


def z_swap(value, bits):
    size = lax.axis_size("batch")
    return lax.ppermute(value, "batch", [(i, i ^ (bits << 1)) for i in range(size)])


def cross_swap(value, y_core):
    batches, streams = lax.axis_size("batch"), lax.axis_size("stream")
    pairs = []
    for b in range(batches):
        for s in range(streams):
            peer = (b ^ 1, s) if s % 2 == y_core else (b, s ^ 2)
            pairs.append((b * streams + s, peer[0] * streams + peer[1]))
    return lax.ppermute(value, ALL, pairs)


def chip_groups():
    batches, streams = lax.axis_size("batch"), lax.axis_size("stream")
    return [
        [b * streams + 2 * x + c for b in range(batches) for x in range(streams // 2)]
        for c in range(2)
    ]


def join(parts, ties=(), column=0, width=None):
    shape = (sum(part.shape[0] for part in parts), parts[0].shape[1], width or parts[0].shape[2])
    return tied_call(
        functools.partial(join_kernel, column),
        parts,
        ties,
        True,
        in_specs=[VMEM] * len(parts),
        out_specs=[VMEM],
        out_shape=[sds(shape, BF)],
        compiler_params=params(10),
    )


def arrival(value):
    if not is_fast():
        return []
    return tied_call(
        touch_kernel,
        [value],
        (),
        True,
        in_specs=[pl.BlockSpec(memory_space=pl.ANY)],
        out_specs=[],
        out_shape=[],
        compiler_params=params(4),
    )


def is_fast():
    return 2 * lax.axis_size("batch") == CHUNKS


class Gather:
    def __init__(self, chunk, first, *ties):
        self.chunk, self.first, self.tokens = chunk, first, []
        if is_fast():
            held = chunk[None]
            if ties:
                held, token = join([held], ties)
                self.tokens = [token]
            self.parts = [held] + [z_swap(held, bits) for bits in (1, 2, 3)]

    def middle(self, *ties):
        if is_fast():
            self.held, token = join(self.parts, ties)
            self.received = cross_swap(self.held, 0)
            self.tokens = [token]
        return self.tokens

    def last(self, *ties, column=0, width=None):
        if is_fast():
            held, token = join([self.held, self.received], ties, column, width)
            self.tokens = [token]
            return [held, cross_swap(held, 1)]
        width = width or self.chunk.shape[1]
        return slow_gather(self.chunk[:, column : column + width], self.first)


def slow_gather(chunk, first):
    full = lax.all_gather(chunk, ALL, axis=0, tiled=True, axis_index_groups=chip_groups())
    full = full.reshape(CHUNKS, -1, full.shape[1])
    orders = [jnp.stack([full[chip_bits(p, c)] for p in range(CHUNKS)]) for c in range(2)]
    full = jnp.where(first, *orders)
    return [full[:8], full[8:]]


def halve(keep, received, ties):
    count, rows, columns = keep.shape
    return tied_call(
        halve_kernel,
        [keep, received],
        ties,
        True,
        in_specs=[VMEM] * 2,
        out_specs=[VMEM] * 2,
        out_shape=[sds((count // 2, rows, columns), BF)] * 2,
        compiler_params=params(12),
    )


class ScatterSum:
    def __init__(self, keep, send, whole=False):
        self.keep, self.send, self.whole = keep, send, whole
        if is_fast():
            self.received = cross_swap(send, 1)

    def second(self, *ties):
        if not is_fast():
            return []
        self.keep, send, token = halve(self.keep, self.received, ties)
        self.received = cross_swap(send, 0)
        return [token]


def third(sums, ties):
    if not is_fast():
        return [], [], []
    shapes = [part.keep.shape[1:] for part in sums]
    rows = sum(rows * columns for rows, columns in shapes) // WIDE
    *out, token = tied_call(
        spread_kernel,
        [part for one in sums for part in (one.keep, one.received)],
        ties,
        True,
        in_specs=[VMEM] * (2 * len(sums)),
        out_specs=[VMEM] * (len(sums) + 3),
        out_shape=[sds(shape, F32) for shape in shapes] + [sds((rows, WIDE), BF)] * 3,
        compiler_params=params(16),
    )
    arrived = [z_swap(part, i + 1) for i, part in enumerate(out[len(sums) :])]
    return out[: len(sums)], arrived, [token]


def result(sums, totals, arrived, info, first, ties):
    if not is_fast():
        out = []
        for one in sums:
            total = slow_sum(one.keep, one.send, first)
            if one.whole:
                out.append(total)
            else:
                count = total.shape[0] // 2
                out.append(jnp.where(first, total[:count], total[count:]))
                out.append(jnp.where(first, total[count:], total[:count]))
        return out, []
    shapes = []
    for one, total in zip(sums, totals):
        rows, columns = total.shape
        shapes += [(rows, columns)] if one.whole else [(rows // 2, columns)] * 2
    *out, token = tied_call(
        functools.partial(result_kernel, len(sums)),
        [info, *totals, *arrived],
        ties,
        True,
        in_specs=[SMEM] + [VMEM] * (len(sums) + 3),
        out_specs=[VMEM] * len(shapes),
        out_shape=[sds(shape, F32) for shape in shapes],
        compiler_params=params(8),
    )
    return out, [token]


def slow_sum(keep, send, first):
    both = jnp.concatenate([keep, send], 0)
    orders = [[chip_bits(p, c) for p in range(CHUNKS)] for c in range(2)]
    sorted_ = [jnp.stack([both[orders[c].index(k)] for k in range(CHUNKS)]) for c in range(2)]
    full = jnp.where(first, *sorted_).astype(F32)
    full = full.reshape(-1, full.shape[2])
    return lax.psum_scatter(
        full, ALL, scatter_dimension=0, tiled=True, axis_index_groups=chip_groups()
    )


def local(tokens, cotangent, block_size, gain_attn, w_qkv, w_out, gain_mlp, w_up, w_down):
    rows, width = tokens.shape[1:]
    half = width // 2
    length = 2 * rows
    batches = lax.axis_size("batch")
    chips = 2 * batches
    hidden = w_up.shape[1] // 2
    stream, batch = lax.axis_index("stream"), lax.axis_index("batch")
    core, noisy = stream % 2, stream // 2
    me = batch * 2 + noisy if chips == CHUNKS else jnp.zeros_like(batch)
    info = jnp.stack([core, noisy, block_size[0], me]).astype(jnp.int32)
    first = core == 0
    n_rows = w_qkv.shape[0]

    def in_order(own, other, axis):
        return jnp.where(
            first, jnp.concatenate([own, other], axis), jnp.concatenate([other, own], axis)
        )

    def mine_theirs(zero, one):
        return jnp.where(first, zero, one), jnp.where(first, one, zero)

    gain_row = gain_attn[None]
    mine, theirs = tied_call(
        prepare_kernel,
        [info, w_qkv, gain_row],
        in_specs=[SMEM, VMEM, VMEM],
        out_specs=[VMEM] * 2,
        out_shape=[sds((n_rows, 3 * half), BF)] * 2,
        compiler_params=params(4),
    )
    chunk_one = in_order(mine, core_swap(theirs), 0)
    gain_two = gain_mlp.astype(BF).astype(F32)[:, None]
    up_rows = w_up.astype(BF).astype(F32)
    scaled = (up_rows * gain_two).astype(BF).reshape(n_rows, chips, 2, -1)
    out_low = w_out.astype(BF)
    mine, theirs = mine_theirs(
        *[
            jnp.concatenate(
                [scaled[:, :, c].reshape(n_rows, -1), out_low[:, c * half : (c + 1) * half]], 1
            )
            for c in range(2)
        ]
    )
    chunk_two = in_order(mine, core_swap(theirs), 0)

    x_own = tokens[0]
    dy_own = cotangent[0]
    streams = lax.axis_size("stream")
    to_noisy = [(i, i + streams // 2) for i in range(streams // 2)]
    to_clean = [(b, a) for a, b in to_noisy]
    arrived = lax.ppermute(x_own, "stream", to_noisy)
    clean_own = jnp.where(noisy == 1, arrived, x_own)
    x_oth = core_swap(x_own)
    clean_oth = core_swap(clean_own)
    dy_oth = core_swap(dy_own)

    places = jnp.arange(length, dtype=jnp.int32)
    lanes = jnp.arange(128, dtype=jnp.int32)
    half_dim = HEAD_DIM // 2
    frequency = jnp.exp(-math.log(10000.0) * (lanes % half_dim).astype(F32) / half_dim)
    angles = places.astype(F32)[:, None] * frequency[None, :]
    cosine = jnp.cos(angles)
    sine = jnp.where((lanes % HEAD_DIM < half_dim)[None], -jnp.sin(angles), jnp.sin(angles))

    sem = pltpu.SemaphoreType.DMA
    tokens = types.SimpleNamespace()
    tokens.tables = [cosine[:8], sine[:8]] if is_fast() else []
    tokens.two_chunk = [chunk_two[:8, :128].astype(F32)] if is_fast() else []

    one = Gather(chunk_one, first)
    tokens.one_middle = one.middle(*tokens.two_chunk)
    bufs_one = one.last(*tokens.tables)
    tokens.one_last = one.tokens
    two = Gather(chunk_two, first, *[*tokens.one_last])
    tokens.two_start = two.tokens
    a1, *tokens.norm = tied_call(
        norm_kernel,
        [info, x_own, x_oth, clean_own, clean_oth],
        [*tokens.two_start],
        True,
        in_specs=[SMEM] + [VMEM] * 4,
        out_specs=[VMEM],
        out_shape=[sds((4, rows, width), BF)],
        compiler_params=params(20),
    )
    a1 = a1.reshape(2 * length, width)

    tokens.two_middle = two.middle(*tokens.norm)

    qkv, *tokens.qkv = tied_call(
        qkv_kernel,
        [info, a1, cosine, sine, *bufs_one],
        [*tokens.norm] or tokens.norm,
        True,
        grid=(4,),
        in_specs=[
            SMEM,
            pl.BlockSpec((rows, width), lambda i: (i, 0)),
            pl.BlockSpec((rows, 128), lambda i: (i % 2, 0)),
            pl.BlockSpec((rows, 128), lambda i: (i % 2, 0)),
        ]
        + [HBM] * 2,
        out_specs=[pl.BlockSpec((rows, 3 * half), lambda i: (i, 0))],
        out_shape=[pltpu.HBM((2 * length, 3 * half), BF)],
        scratch_shapes=[pltpu.VMEM((width, 3 * half), BF), sem((CHUNKS,))],
        compiler_params=params(24),
    )
    qkv = pltpu.with_memory_space_constraint(qkv, pltpu.HBM)
    bufs_out = two.last(*tokens.qkv, column=hidden, width=half)
    tokens.out_last = two.tokens
    bufs_two = two.last(*tokens.qkv, width=hidden)
    tokens.two_last = two.tokens
    three = Gather(w_down.astype(BF), first, *[*tokens.two_last])
    tokens.three_start = three.tokens

    pairs = half // 128

    def pair_spec(part, clean):
        return pl.BlockSpec((length, 128), lambda p: (clean, part * pairs + p))

    qkv_specs = [pair_spec(0, 0), pair_spec(1, 0), pair_spec(2, 0), pair_spec(1, 1), pair_spec(2, 1)]
    lse_spec = pl.BlockSpec((length // BLOCK, 2 * BLOCK), lambda p: (p, 0))
    ot_own, lse, *tokens.attend = tied_call(
        attend_kernel,
        [info, qkv, qkv, qkv, qkv, qkv],
        [*tokens.out_last, *tokens.two_last, *tokens.three_start],
        True,
        grid=(pairs,),
        in_specs=[SMEM] + qkv_specs,
        out_specs=[pl.BlockSpec((128, length), lambda p: (p, 0)), lse_spec],
        out_shape=[sds((half, length), BF), sds((pairs * length // BLOCK, 2 * BLOCK), F32)],
        compiler_params=params(28),
    )
    ot_oth = core_swap(ot_own)
    tokens.three_middle = three.middle(*tokens.attend)

    (wo_own,) = tied_call(
        out_weight_kernel,
        [info, *bufs_out],
        [*tokens.three_middle],
        in_specs=[SMEM] + [VMEM] * 2,
        out_specs=[VMEM],
        out_shape=[sds((width, half), BF)],
        compiler_params=params(8),
    )
    wo_oth = core_swap(wo_own)

    r1, a2, *tokens.out = tied_call(
        out_kernel,
        [info, x_own, x_oth, ot_own, ot_oth, wo_own, wo_oth],
        [],
        True,
        in_specs=[SMEM] + [VMEM] * 6,
        out_specs=[VMEM] * 2,
        out_shape=[sds((rows, width), F32), sds((length, width), BF)],
        scratch_shapes=[pltpu.VMEM((width, rows), BF), pltpu.VMEM((rows, width), F32)],
        compiler_params=params(20),
    )

    bufs_three = three.last(*tokens.out)
    tokens.three_last = three.tokens
    down_bufs = [sds((8, 2 * width // CHUNKS, width), BF)] * 2
    up_bufs = [sds((8, width // CHUNKS, hidden + half), BF)] * 2
    one_bufs = [sds((8, width // CHUNKS, 3 * half), BF)] * 2
    g, slope, *down_parts, up_done = tied_call(
        up_kernel,
        [info, a2, dy_own, dy_oth, *bufs_two],
        [*tokens.three_last],
        True,
        in_specs=[SMEM] + [HBM] * 5,
        out_specs=[HBM] * 4,
        out_shape=[sds((length, hidden), BF), sds((length, hidden), BF)] + down_bufs,
        scratch_shapes=[
            pltpu.VMEM((length, width), BF),
            pltpu.VMEM((length, width), BF),
            pltpu.VMEM((width, hidden), BF),
            pltpu.VMEM((length, hidden), BF),
            pltpu.VMEM((length, hidden), BF),
            pltpu.VMEM((hidden, width), BF),
            sem((4,)),
            sem((CHUNKS,)),
            sem((2 * hidden // TILE,)),
        ],
        compiler_params=params(44),
    )
    sum_down = ScatterSum(*down_parts, whole=True)
    tokens.up = [up_done]

    e_own, e_send, *up_parts, down_done = tied_call(
        down_kernel,
        [info, a2, slope, dy_own, dy_oth, *bufs_two, *bufs_three],
        [],
        True,
        in_specs=[SMEM] + [HBM] * 8,
        out_specs=[VMEM] * 2 + [HBM] * 2,
        out_shape=[sds((rows, width), F32), sds((rows, width), BF)] + up_bufs,
        scratch_shapes=[
            pltpu.VMEM((length, width), BF),
            pltpu.VMEM((length, width), BF),
            pltpu.VMEM((length, hidden), BF),
            pltpu.VMEM((width, hidden), BF),
            pltpu.VMEM((hidden, width), BF),
            pltpu.VMEM((length, hidden), BF),
            pltpu.VMEM((width, hidden), BF),
            sem((5,)),
            sem((CHUNKS,)),
            sem((CHUNKS,)),
        ],
        compiler_params=params(30),
    )
    e_recv = core_swap(e_send)
    tokens.down = [down_done]
    tokens.down_second = sum_down.second(*tokens.down)

    row_block = pl.BlockSpec((BLOCK, width), lambda i: (i, 0))
    dr1, dr_own = tied_call(
        mlp_back_kernel,
        [r1, e_own, e_recv, dy_own],
        [*tokens.down_second],
        grid=(rows // BLOCK,),
        in_specs=[row_block] * 4,
        out_specs=[row_block] * 2,
        out_shape=[sds((rows, width), F32), sds((rows, width), BF)],
        compiler_params=params(8),
    )
    dr_oth = core_swap(dr_own)

    do, *up_parts, out_back_done = tied_call(
        out_back_kernel,
        [info, dr_own, dr_oth, wo_own, wo_oth, ot_own, ot_oth, *up_parts],
        [],
        True,
        in_specs=[SMEM] + [VMEM] * 6 + [HBM] * 2,
        out_specs=[VMEM] + [HBM] * 2,
        out_shape=[sds((length, half), BF)] + up_bufs,
        input_output_aliases={7: 1, 8: 2},
        scratch_shapes=[
            pltpu.VMEM((length, width), BF),
            pltpu.VMEM((width, length), BF),
            pltpu.VMEM((width, half), BF),
            sem((CHUNKS,)),
        ],
        compiler_params=params(20),
    )
    sum_up = ScatterSum(*up_parts)
    tokens.out_back = [out_back_done]
    tokens.down_arrival = arrival(sum_down.received) if is_fast() else []
    down_totals, down_arrived, tokens.down_third = third([sum_down], [])

    column = pl.BlockSpec((length, 128), lambda p: (0, p))
    whole = pl.BlockSpec((length, 128), lambda p: (0, 0))
    *grads, attend_back_done = tied_call(
        attend_back_kernel,
        [info, qkv, qkv, qkv, qkv, qkv, do, ot_own, lse, cosine, sine],
        [*tokens.down_third],
        True,
        grid=(pairs,),
        in_specs=[SMEM]
        + qkv_specs
        + [column, pl.BlockSpec((128, length), lambda p: (p, 0)), lse_spec, whole, whole],
        out_specs=[column] * 5,
        out_shape=[sds((length, half), BF)] * 5,
        scratch_shapes=[pltpu.VMEM((length, 128), F32)] * 2,
        compiler_params=params(36),
    )
    tokens.attend_back = [attend_back_done]
    (grad_down,), tokens.down_result = result(
        [sum_down], down_totals, down_arrived, info, first, [*tokens.attend_back]
    )
    tokens.up_second = sum_up.second(*tokens.down_result)
    *one_parts, weight_done = tied_call(
        qkv_weight_kernel,
        [info, *grads, a1],
        [*tokens.up_second],
        True,
        in_specs=[SMEM] + [VMEM] * 6,
        out_specs=[HBM] * 2,
        out_shape=one_bufs,
        scratch_shapes=[pltpu.VMEM((width, 3 * half), BF), sem((CHUNKS,))],
        compiler_params=params(24),
    )
    sum_one = ScatterSum(*one_parts)
    tokens.weight = [weight_done]
    clean_part, clean_send, clean_back_done = tied_call(
        clean_back_kernel,
        [info, *grads[3:], *bufs_one],
        [*tokens.weight],
        True,
        in_specs=[SMEM] + [VMEM] * 2 + [HBM] * 2,
        out_specs=[VMEM] * 2,
        out_shape=[sds((rows, width), BF)] * 2,
        scratch_shapes=[pltpu.VMEM((width, 3 * half), BF), sem((CHUNKS,))],
        compiler_params=params(24),
    )
    tokens.clean_back = [clean_back_done]

    own_part, own_send, back_done = tied_call(
        qkv_back_kernel,
        [info, *grads[:3], *bufs_one],
        [*tokens.clean_back],
        True,
        in_specs=[SMEM] + [VMEM] * 3 + [HBM] * 2,
        out_specs=[VMEM] * 2,
        out_shape=[sds((rows, width), F32), sds((rows, width), BF)],
        scratch_shapes=[pltpu.VMEM((width, 3 * half), BF), sem((CHUNKS,))],
        compiler_params=params(24),
    )
    own_arrived = core_swap(own_send)
    tokens.qkv_back = [back_done]
    up_totals, up_arrived, tokens.up_third = third([sum_up], [*tokens.qkv_back])
    clean_swapped = core_swap(clean_send)
    tokens.one_second = sum_one.second(*tokens.up_third)

    (clean_total,) = tied_call(
        clean_kernel,
        [clean_part, clean_swapped],
        [*tokens.one_second],
        in_specs=[VMEM] * 2,
        out_specs=[VMEM],
        out_shape=[sds((rows, width), BF)],
        compiler_params=params(8),
    )
    clean_arrived = lax.ppermute(clean_total, "stream", to_clean)

    def mix():
        return tied_call(
            mix_kernel,
            [info, g, *bufs_three],
            [*tokens.one_second],
            True,
            in_specs=[SMEM] + [HBM] * 3,
            out_specs=[VMEM] * 2,
            out_shape=[sds((rows, width), F32), sds((rows, width), BF)],
            scratch_shapes=[
                pltpu.VMEM((length, hidden), BF),
                pltpu.VMEM((hidden, width), BF),
                sem((1,)),
                sem((CHUNKS,)),
            ],
            compiler_params=params(16),
        )

    tokens.clean_arrival = arrival(clean_arrived)
    up_sums, tokens.up_result = result(
        [sum_up], up_totals, up_arrived, info, first, []
    )
    one_totals, one_arrived, tokens.one_third = third([sum_one], [*tokens.up_result])
    y_own, y_send, *tokens.mix = mix()
    output = (r1 + y_own + core_swap(y_send).astype(F32)).astype(BF)

    input_grad, *tokens.input = tied_call(
        input_back_kernel,
        [info, x_own, own_part, own_arrived, clean_total, clean_arrived, dr1],
        [*tokens.one_third],
        True,
        in_specs=[SMEM] + [VMEM] * 6,
        out_specs=[VMEM],
        out_shape=[sds((rows, width), BF)],
        compiler_params=params(12),
    )
    one_sums, tokens.one_result = result(
        [sum_one], one_totals, one_arrived, info, first, [*tokens.input]
    )
    grad_qkv, grad_gain = tied_call(
        finish_kernel,
        [info, one_sums[0], core_swap(one_sums[1]), w_qkv, gain_row],
        in_specs=[SMEM] + [VMEM] * 4,
        out_specs=[VMEM] * 2,
        out_shape=[sds((n_rows, 3 * width), F32), sds((1, n_rows), F32)],
        compiler_params=params(4),
    )

    up_swapped = core_swap(up_sums[1])
    if is_fast():
        grad_w_up, grad_out, gain_up = tied_call(
            finish_up_kernel,
            [info, up_sums[0], up_swapped, w_up, gain_mlp[None]],
            [*tokens.one_result],
            in_specs=[SMEM] + [VMEM] * 4,
            out_specs=[VMEM] * 3,
            out_shape=[
                sds((n_rows, 2 * hidden), F32),
                sds((n_rows, width), F32),
                sds((1, n_rows), F32),
            ],
            compiler_params=params(8),
        )
        grad_gain_up = gain_up[0]
    else:
        ordered = mine_theirs(up_sums[0], up_swapped)
        grad_out = jnp.concatenate([v[:, hidden:] for v in ordered], 1)
        sums_up = jnp.stack([v[:, :hidden].reshape(n_rows, chips, -1) for v in ordered], 2)
        sums_up = sums_up.reshape(n_rows, 2 * hidden)
        grad_w_up = sums_up * gain_two
        grad_gain_up = jnp.sum(sums_up * up_rows, 1)
    return (
        output[None],
        input_grad[None],
        grad_gain[0],
        grad_qkv,
        grad_out,
        grad_gain_up,
        grad_w_up,
        grad_down,
    )


def solution(mesh):
    rows = P("batch", "stream", None)
    flat, split = P(ALL), P(ALL, None)
    return jax.shard_map(
        local,
        mesh=mesh,
        in_specs=(rows, rows, P("batch"), flat, split, split, flat, split, split),
        out_specs=(rows, rows, flat, split, split, flat, split, split),
        check_vma=False,
    )
```
